128 devices in a mesh: dp: 8 (over z_hi, y), ctx: 4 (over z_lo, core), tensor: 4 (over x).
Axes of the slice: x: 4, y: 4, z: 4 (z_hi: 2, z_lo: 2; z = z_hi * 2 + z_lo), core: 2. Of those that a mesh axis runs over, the one named last changes fastest.
Arguments:
- stream: bfloat16 [16, 1152, 1024], P('dp', ('ctx', 'tensor')), may hold values from -6 to 6
- segments: int32 [16, 1152], P('dp'), may hold values from 0 to 2, as said below
- w_qkv: bfloat16 [2, 1024, 3, 1024], P(None, ('dp', 'ctx'), None, 'tensor'), may hold values from -0.1875 to 0.1875
- qv_bias: bfloat16 [2, 2, 16, 64], P(None, None, 'tensor', ('dp', 'ctx')), may hold values from -3 to 3
- w_out: bfloat16 [2, 1024, 1024], P(None, 'tensor', ('dp', 'ctx')), may hold values from -2 to 2
- norm_gains: bfloat16 [2, 2, 1024], P(None, None, ('dp', 'ctx')), may hold values from 0.5 to 1.5
- shifts: bfloat16 [2, 4, 1024], P(None, None, ('dp', 'ctx')), may hold values from -2 to 2
- w_in: bfloat16 [2, 1024, 4096], P(None, ('dp', 'ctx'), 'tensor'), may hold values from -0.1875 to 0.1875
- in_bias: bfloat16 [2, 16, 256], P(None, 'tensor', ('dp', 'ctx')), may hold values from -2 to 2
- w_back: bfloat16 [2, 4096, 1024], P(None, 'tensor', ('dp', 'ctx')), may hold values from -0.09375 to 0.09375
- cotangent: bfloat16 [16, 1152, 1024], P('dp', ('ctx', 'tensor')), may hold values from -6 to 6
Outputs:
- result: float32 [16, 1152, 1024], P('dp', ('ctx', 'tensor'))
- grad_stream: float32 [16, 1152, 1024], P('dp', ('ctx', 'tensor'))
- grad_qkv: float32 [2, 1024, 3, 1024], P(None, ('dp', 'ctx'), None, 'tensor')
- grad_qvbias: float32 [2, 2, 16, 64], P(None, None, 'tensor', ('dp', 'ctx'))
- grad_wout: float32 [2, 1024, 1024], P(None, 'tensor', ('dp', 'ctx'))
- grad_gains: float32 [2, 2, 1024], P(None, None, ('dp', 'ctx'))
- grad_shifts: float32 [2, 4, 1024], P(None, None, ('dp', 'ctx'))
- grad_win: float32 [2, 1024, 4096], P(None, ('dp', 'ctx'), 'tensor')
- grad_inbias: float32 [2, 16, 256], P(None, 'tensor', ('dp', 'ctx'))
- grad_wback: float32 [2, 4096, 1024], P(None, 'tensor', ('dp', 'ctx'))
The draws below stay inside these ranges and needn't reach their ends.
Inputs may be any that keep to these rules, and one draw needn't show every extreme that they name: `segments`: each packed row holds three documents numbered 0, 1 and 2 in order, each of one token or more.
All inputs are finite; a program needn't handle non-finite values.
Results may differ from the reference program's by a relative error of at most 0.035.
Values may be sent and summed in bfloat16 or wider, within the bound.
No kernel may reach another device: no remote copies, remote signals or barrier semaphores. Data moves between devices by JAX's collectives and lax.ppermute only.
A program may use at most 192 MiB of HBM per device.

```python
import jax
import jax.numpy as jnp
from jax import lax

D = 1024
H = 16
FF = 4096
DH = 64
LAYERS = 2
LENGTH = 1152
SEQS = 16
N_CTX = 4


def draw_segments(key, part):
    key = jax.random.fold_in(key, 11)
    first_key, last_key = jax.random.split(key)
    block = LENGTH // N_CTX
    start = jax.random.randint(first_key, (SEQS, 1), 1, block)
    finish = jax.random.randint(last_key, (SEQS, 1), LENGTH - block + 1, LENGTH)
    places = jnp.arange(LENGTH, dtype=jnp.int32)[None, :]
    return (places >= start).astype(jnp.int32) + (places >= finish).astype(jnp.int32)


def block_scale(rng, shape, shards, low, high):
    def one(axis_at, shards_of):
        steps = jax.random.uniform(jax.random.fold_in(jax.random.fold_in(rng, 6), axis_at), (shards_of,), jnp.float32, low / len(shards), high / len(shards))
        return jnp.repeat(jnp.exp(steps), shape[axis_at] // shards_of).reshape((-1,) + (1,) * (len(shape) - axis_at - 1))

    factor_of = one(*shards[0])
    for cut in shards[1:]:
        factor_of = factor_of * one(*cut)
    return factor_of


def normal_values(stream_key, dims, deviation, limit, pieces=(), held_as=jnp.bfloat16):
    drawn = jax.random.normal(stream_key, dims, jnp.float32) * deviation
    if len(pieces) > 0:
        drawn = block_scale(stream_key, dims, pieces, -0.22, 0.18) * drawn
    return jnp.clip(drawn, min=-limit, max=limit).astype(held_as)


def setup_inputs(seed: int = 0) -> dict:
    key_of = jax.random.split(jax.random.key(seed), 12)
    return {
        "stream": normal_values(key_of[0], (SEQS, LENGTH, D), 1.0, 6.0, ((0, 8), (1, 16))),
        "segments": draw_segments(jax.random.fold_in(key_of[11], 71), 0),
        "w_qkv": normal_values(key_of[2], (LAYERS, D, 3, D), D ** -0.5, 0.1875, ((1, 32), (3, 4))),
        "qv_bias": normal_values(key_of[3], (LAYERS, 2, H, DH), 0.5, 3.0, ((2, 4), (3, 32))),
        "w_out": normal_values(key_of[4], (LAYERS, D, D), (D // 128) ** -0.5, 2.0, ((1, 4), (2, 32))),
        "norm_gains": jnp.clip(1.0 + 0.1 * jax.random.normal(key_of[5], (LAYERS, 2, D), jnp.float32), 0.5, 1.5).astype(jnp.bfloat16),
        "shifts": normal_values(key_of[6], (LAYERS, 4, D), 0.3, 2.0, ((2, 32),)),
        "w_in": normal_values(key_of[7], (LAYERS, D, FF), D ** -0.5, 0.1875, ((1, 32), (2, 4))),
        "in_bias": normal_values(key_of[8], (LAYERS, H, FF // H), 0.3, 2.0, ((1, 4), (2, 32))),
        "w_back": normal_values(key_of[9], (LAYERS, FF, D), FF ** -0.5, 0.09375, ((1, 4), (2, 32))),
        "cotangent": normal_values(key_of[10], (SEQS, LENGTH, D), 1.0, 6.0, ((0, 8), (1, 16))),
    }


@jax.custom_vjp
def low(v):
    return lax.optimization_barrier(v.astype(jnp.bfloat16)).astype(jnp.float32)

@jax.custom_vjp
def low_back(v):
    return v

def low_keep(v):
    return (low(v), None)

def low_pass(kept, grad):
    return (grad,)

def back_keep(v):
    return (v, None)

def back_low(kept, grad):
    return (low(grad),)
low.defvjp(low_keep, low_pass)
low_back.defvjp(back_keep, back_low)
EPSILON = 1e-12
MASKED = -1000000000.0

def product(left, right):
    return jnp.dot(left, right, precision=lax.Precision.HIGHEST, preferred_element_type=jnp.float32)

def normalize(values, gain, shift):
    mean = lax.optimization_barrier(jnp.mean(values, axis=-1, keepdims=True))
    centred = values - mean
    variance = lax.optimization_barrier(jnp.mean(centred * centred, axis=-1, keepdims=True))
    return centred * lax.rsqrt(variance + EPSILON) * gain + shift

def attend_one(items):
    query, keys, values, marks = items
    scores = jnp.einsum('qhe,khe->hqk', query, keys, precision=lax.Precision.HIGHEST) * DH ** (-0.5)
    scores = low_back(scores)
    same = marks[:, None] == marks[None, :]
    scores = jnp.where(same[None], scores, MASKED)
    top = lax.optimization_barrier(jnp.max(scores, axis=-1, keepdims=True))
    weights = jnp.exp(scores - top)
    probs = low(weights / lax.optimization_barrier(jnp.sum(weights, axis=-1, keepdims=True)))
    return jnp.einsum('hqk,khe->qhe', probs, values, precision=lax.Precision.HIGHEST)

def one_layer(state, segments, params):
    w_qkv, qv_bias, w_out, norm_gains, shifts, w_in, in_bias, w_back = params
    tokens = SEQS * LENGTH
    flat = state.reshape(tokens, D)
    packed = low_back(product(low(flat), w_qkv.reshape(D, 3 * D))).reshape(tokens, 3, D)
    pair_bias = qv_bias.reshape(2, D)
    query = low(packed[:, 0] + pair_bias[0])
    keys = low(packed[:, 1])
    values = low(packed[:, 2] + pair_bias[1])

    def split(tensor):
        return tensor.reshape(SEQS, LENGTH, H, DH)
    mixed = lax.map(jax.checkpoint(attend_one), (split(query), split(keys), split(values), segments))
    mixed = low(low_back(mixed.reshape(tokens, D)))
    attended = low_back(product(mixed, w_out)) + shifts[2]
    first = normalize(flat + attended, norm_gains[0], shifts[0])
    hidden = low_back(product(low(first), w_in)) + in_bias.reshape(FF)
    active = low(jax.nn.gelu(hidden, approximate=False))
    down = low_back(product(active, w_back)) + shifts[3]
    return normalize(first + down, norm_gains[1], shifts[1]).reshape(SEQS, LENGTH, D)

def reference(stream, segments, w_qkv, qv_bias, w_out, norm_gains, shifts, w_in, in_bias, w_back, cotangent):
    params = tuple((p.astype(jnp.float32) for p in (w_qkv, qv_bias, w_out, norm_gains, shifts, w_in, in_bias, w_back)))

    def forward(state, weights):
        for layer in range(LAYERS):
            state = one_layer(state, segments, tuple((w[layer] for w in weights)))
        return state
    result, pullback = jax.vjp(forward, stream.astype(jnp.float32), params)
    grad_stream, grads = pullback(cotangent.astype(jnp.float32))
    return (result, grad_stream, grads[0], grads[1], grads[2], grads[3], grads[4], grads[5], grads[6], grads[7])
```

```python
import jax
import jax.numpy as jnp
from jax import lax
from jax.sharding import PartitionSpec as P

EPSILON = 1e-12
MASKED = -1000000000.0
ROOT_HALF = 0.7071067811865476
ROOT_TWOPI = 2.5066282746310002
ALL = ("dp", "ctx", "tensor")
LOW = jnp.bfloat16
FULL = jnp.float32

DIMS = (("x", 1), ("y", 1), ("z", 1), ("x", 3), ("y", 3), ("z", 3))
CANON = (("z", 3), ("z", 1), ("y", 3), ("y", 1), ("x", 3), ("x", 1))
GROUPS = [[(zl * 2 + c) * 4 + x for zl in range(2) for x in range(4)] for c in range(2)]


def exchange_perm(axis, mask):
    pairs = []
    for device in range(128):
        dp, ctx, x = device // 16, (device // 4) % 4, device % 4
        at = {"x": x, "y": dp % 4, "z": (dp // 4) * 2 + ctx // 2, "core": ctx % 2}
        at[axis] ^= mask
        other = ((at["z"] // 2) * 4 + at["y"]) * 16
        other += ((at["z"] % 2) * 2 + at["core"]) * 4 + at["x"]
        pairs.append((device, other))
    return pairs


def swap(value, axis="core", mask=1):
    return lax.ppermute(value, ALL, exchange_perm(axis, mask))


def dim_at(part, phase):
    return DIMS[(part + phase) % 6]


def gather_phases(parts, first, last):
    for phase in range(first, last):
        got = [swap(value, *dim_at(q, phase)) for q, value in enumerate(parts)]
        parts = [jnp.concatenate([value, new], 0) for value, new in zip(parts, got)]
    return parts


def canonical(part, value):
    rows, cols = value.shape[1:]
    value = value.reshape((2,) * 6 + (rows, cols))
    place = [5 - [dim_at(part, phase) for phase in range(6)].index(dim) for dim in CANON]
    value = value.transpose(place[:4] + [6] + place[4:] + [7])
    return value.reshape(16 * rows, 4 * cols)


def by_phase(part, value):
    rows, cols = value.shape[0] // 16, value.shape[1] // 4
    value = value.reshape((2,) * 4 + (rows, 2, 2, cols))
    axis_of = dict(zip(CANON, (0, 1, 2, 3, 5, 6)))
    order = [axis_of[dim_at(part, phase)] for phase in range(6)]
    return value.transpose(order + [4, 7]).reshape(64, rows, cols)


def reduce_phases(parts, first, last):
    for phase in range(first, last):
        half = parts[0].shape[0] // 2
        got = [swap(value[half:], *dim_at(q, phase)) for q, value in enumerate(parts)]
        parts = [
            (value[:half].astype(FULL) + new.astype(FULL)).astype(LOW)
            for value, new in zip(parts, got)
        ]
    return parts


def relative_x(me_x, r):
    return me_x ^ (0, 1, 3, 2)[r]


def take_relative(value, me_x, axis):
    return jnp.concatenate(
        [lax.dynamic_slice_in_dim(value, relative_x(me_x, r), 1, axis) for r in range(4)], axis
    )


def take_absolute(value, me_x, axis):
    parts = []
    for x in range(4):
        off = me_x ^ x
        parts.append(lax.dynamic_slice_in_dim(value, off ^ (off >> 1), 1, axis))
    return jnp.concatenate(parts, axis)


def both(value):
    return jnp.concatenate([value, swap(value)], 0)


def own_sum(value):
    half = value.shape[0] // 2
    value = value.astype(FULL)
    return value[:half] + swap(value[half:].astype(LOW)).astype(FULL)


def normalize(values, gain, shift):
    mean = jnp.mean(values, axis=-1, keepdims=True)
    centred = values - mean
    inverse = lax.rsqrt(jnp.mean(centred * centred, axis=-1, keepdims=True) + EPSILON)
    unit = centred * inverse
    return (unit * gain + shift, unit, inverse)


def normalize_back(incoming, unit, inverse, gain):
    scaled = incoming * gain
    inner = (
        scaled
        - jnp.mean(scaled, axis=-1, keepdims=True)
        - unit * jnp.mean(scaled * unit, axis=-1, keepdims=True)
    )
    return (inverse * inner, jnp.sum(incoming * unit, axis=0), jnp.sum(incoming, axis=0))


def gelu_slope(value):
    cdf = 0.5 * (1.0 + lax.erf(value * ROOT_HALF))
    return cdf + value * jnp.exp(-0.5 * value * value) / ROOT_TWOPI


def dot(left, right, dims):
    return lax.dot_general(left, right, (dims, ((), ())), preferred_element_type=FULL)


def times(left, right):
    return dot(left, right, ((1,), (0,)))


def times_t(left, right):
    return dot(left, right, ((1,), (1,)))


def t_times(left, right):
    return dot(left, right, ((0,), (0,)))


def masked_scores(query, keys, marks, scale):
    scores = jnp.einsum("qse,kse->sqk", query, keys, preferred_element_type=FULL) * scale
    return jnp.where(marks, scores, MASKED)


def attend(qkv, marks, scale):
    scores = masked_scores(qkv[:, 0], qkv[:, 1], marks, scale)
    top = jnp.max(scores, axis=-1, keepdims=True)
    weights = jnp.exp(scores - top)
    total = jnp.sum(weights, axis=-1, keepdims=True)
    probs = (weights / total).astype(LOW)
    mixed = jnp.einsum("sqk,kse->qse", probs, qkv[:, 2], preferred_element_type=FULL)
    return mixed.astype(LOW), top + jnp.log(total)


def attend_back(qkv, marks, summary, grad_mixed, scale):
    probs = jnp.exp(masked_scores(qkv[:, 0], qkv[:, 1], marks, scale) - summary)
    low_probs = probs.astype(LOW)
    grad_probs = jnp.einsum("qse,kse->sqk", grad_mixed, qkv[:, 2], preferred_element_type=FULL)
    inner = jnp.sum(probs * grad_probs, axis=-1, keepdims=True)
    grad_scores = (probs * (grad_probs - inner)).astype(LOW)
    grad_q = jnp.einsum("sqk,kse->qse", grad_scores, qkv[:, 1], preferred_element_type=FULL)
    grad_k = jnp.einsum("sqk,qse->kse", grad_scores, qkv[:, 0], preferred_element_type=FULL)
    grad_v = jnp.einsum("sqk,qse->kse", low_probs, grad_mixed, preferred_element_type=FULL)
    return grad_q * scale, grad_k * scale, grad_v


def trade(value):
    return lax.all_to_all(
        value, ("ctx", "tensor"), 0, 0, axis_index_groups=GROUPS, tiled=True
    )


def to_heads(value, me_x):
    rows = value.shape[0] // 4
    kinds = value.shape[3]
    value = take_absolute(value, me_x, 1).reshape(2, 2, rows, 4, 2, kinds, 64)
    value = value.transpose(4, 3, 0, 2, 5, 1, 6).reshape(8, 2 * rows, kinds * 128)
    return trade(value).reshape(16 * rows, kinds, 2, 64)


def to_tokens(value, me_x):
    rows = value.shape[0] // 16
    kinds = value.shape[1]
    value = trade(value.reshape(8, 2 * rows, kinds * 128))
    value = value.reshape(2, 4, 2, rows, kinds, 2, 64).transpose(2, 5, 3, 1, 0, 4, 6)
    return take_relative(value.reshape(4 * rows, 4, 2, kinds, 64), me_x, 1)


def local(
    stream, segments, w_qkv, qv_bias, w_out, norm_gains, shifts, w_in, in_bias, w_back, cotangent
):
    layers = w_qkv.shape[0]
    dp, ctx, me_x = lax.axis_index("dp"), lax.axis_index("ctx"), lax.axis_index("tensor")
    core, z_lo = ctx & 1, ctx >> 1
    me_y, me_z = dp & 3, (dp >> 2) * 2 + z_lo
    rows = stream.shape[1]
    width = stream.shape[2]
    scale = 64 ** (-0.5)

    vectors = jnp.concatenate(
        [norm_gains.reshape(-1), shifts.reshape(-1), qv_bias.reshape(-1), in_bias.reshape(-1)]
    )
    vectors = jnp.pad(vectors, (0, 512 - vectors.shape[0]))
    spread = lax.all_to_all(jnp.broadcast_to(vectors, (128, 512)), ALL, 0, 0, tiled=True)
    spread = spread.reshape(32, 4, 512)
    gains_abs = spread[:, 0, 0:128].reshape(32, 4, 32).transpose(1, 0, 2).reshape(4, width)
    shifts_abs = spread[:, 0, 128:384].reshape(32, 8, 32).transpose(1, 0, 2).reshape(8, width)
    pair = spread[:, :, 384:416].reshape(32, 4, layers, 2, 2, 2, 2).transpose(2, 3, 1, 4, 5, 0, 6)
    pair = lax.dynamic_index_in_dim(pair.reshape(layers, 2, 4, 2, 2, 64), core, 3, False)
    pair = take_relative(pair, me_x, 2).astype(FULL)
    up = spread[:, :, 416:480].reshape(32, 4, layers, 2, 2, 8).transpose(2, 1, 3, 4, 0, 5)
    up = lax.dynamic_index_in_dim(up.reshape(layers, 4, 2, 2, 256), core, 2, False)
    up = take_relative(up, me_x, 1).astype(FULL)

    place = lax.broadcasted_iota(jnp.int32, (width, width), 1)
    block = place >> 6
    far_z = me_z ^ (((block >> 2) & 1) ^ ((block >> 3) * 3))
    far_y = me_y ^ ((block & 1) ^ (((block >> 1) & 1) * 3))
    source = (((far_z >> 1) * 4 + far_y) * 2 + (far_z & 1)) * 64 + (place & 63)
    reorder = source == lax.broadcasted_iota(jnp.int32, (width, width), 0)
    reorder_low = reorder.astype(LOW)
    reorder_full = reorder.astype(FULL)

    def absolute(value):
        return lax.dot_general(
            value, reorder_full, (((1,), (1,)), ((), ())), precision=lax.Precision.HIGHEST,
            preferred_element_type=FULL,
        )

    tokens = 2 * rows
    inputs = times(
        jnp.concatenate(
            [
                stream.reshape(tokens, width), cotangent.reshape(tokens, width),
                gains_abs, shifts_abs,
            ]
        ),
        reorder_low,
    )
    state = inputs[:tokens]
    incoming = inputs[tokens : 2 * tokens]
    gains = inputs[2 * tokens : 2 * tokens + 4].reshape(layers, 2, width)
    shift = inputs[2 * tokens + 4 :].reshape(layers, 4, width)

    columns = jnp.concatenate(
        [
            w_qkv.reshape(layers, 32, 3, 2, 128).transpose(0, 1, 3, 2, 4).reshape(
                layers, 32, 2, 384
            ),
            w_out.transpose(0, 2, 1).reshape(layers, 32, 2, 128),
            w_in.reshape(layers, 32, 2, 512),
            w_back.transpose(0, 2, 1).reshape(layers, 32, 2, 512),
        ],
        3,
    )
    keep = lax.dynamic_index_in_dim(columns, core, 2, False)
    new = swap(lax.dynamic_index_in_dim(columns, 1 - core, 2, False))
    rows_two = jnp.where(
        core == 0, jnp.concatenate([keep, new], 1), jnp.concatenate([new, keep], 1)
    )
    parts = [rows_two[None, :, :, q * 256 : (q + 1) * 256] for q in range(6)]
    parts = gather_phases(parts, 0, 4)
    weights = []
    for layer in range(layers):
        mine = [value[:, layer] for value in parts]
        if layer:
            mine, weights[-1] = lax.optimization_barrier((mine, weights[-1]))
        mine = gather_phases(mine, 4, 6)
        weights.append([canonical(q, value) for q, value in enumerate(mine)])

    marks = segments.reshape(2, 2, 2, 4, rows)
    marks = jnp.where(core == 0, marks, marks[:, :, ::-1])
    marks = marks.transpose(0, 1, 3, 2, 4).reshape(2, 16 * rows)
    marks = marks[:, :, None] == marks[:, None, :]

    saved = []
    for layer in range(layers):
        w_qk, w_vo, w_up0, w_up1, w_down0, w_down1 = weights[layer]
        w_vo = w_vo.reshape(width, 4, 256)
        w_v = w_vo[:, :, :128].reshape(width, 512)
        w_o = w_vo[:, :, 128:].reshape(width, 512)
        gathered = both(state.astype(LOW))
        qk = times(gathered, w_qk).reshape(2 * tokens, 4, 2, 2, 64).transpose(0, 1, 3, 2, 4)
        v = times(gathered, w_v).reshape(2 * tokens, 4, 2, 1, 64)
        bias = jnp.stack([pair[layer, 0], jnp.zeros_like(pair[layer, 0])], 2)
        packed = jnp.concatenate([qk + bias, v + pair[layer, 1][:, :, None]], 3).astype(LOW)
        qkv = to_heads(packed, me_x)
        mixed, summary = attend(qkv, marks, scale)
        mixed = to_tokens(mixed[:, None], me_x).reshape(2 * tokens, 512)
        attended = own_sum(times_t(mixed, w_o)) + shift[layer, 2]
        first, unit_one, inv_one = normalize(state + attended, gains[layer, 0], shift[layer, 0])
        gathered_two = both(first.astype(LOW))
        hidden = [
            times(gathered_two, w) + up[layer, :, j].reshape(1024)
            for j, w in enumerate((w_up0, w_up1))
        ]
        active = [jax.nn.gelu(value, approximate=False).astype(LOW) for value in hidden]
        down = own_sum(times_t(active[0], w_down0) + times_t(active[1], w_down1))
        state, unit_two, inv_two = normalize(
            first + down + shift[layer, 3], gains[layer, 1], shift[layer, 1]
        )
        saved.append(
            (gathered, qkv, summary, mixed, unit_one, inv_one, gathered_two, hidden, active,
             unit_two, inv_two, w_v, w_o)
        )
    result = absolute(state)

    grads = [None] * layers
    small = [None] * layers
    for layer in reversed(range(layers)):
        w_qk, _, w_up0, w_up1, w_down0, w_down1 = weights[layer]
        (gathered, qkv, summary, mixed, unit_one, inv_one, gathered_two, hidden, active,
         unit_two, inv_two, w_v, w_o) = saved[layer]
        grad_two, gain_two, shift_two = normalize_back(
            incoming, unit_two, inv_two, gains[layer, 1]
        )
        spread_two = both(grad_two.astype(LOW))
        grad_down = [t_times(spread_two, value).astype(LOW) for value in active]
        grad_hidden = [
            times(spread_two, w) * gelu_slope(value)
            for w, value in zip((w_down0, w_down1), hidden)
        ]
        grad_upbias = jnp.stack(
            [jnp.sum(value, axis=0).reshape(4, 256) for value in grad_hidden], 1
        )
        low_hidden = [value.astype(LOW) for value in grad_hidden]
        grad_up = [t_times(gathered_two, value).astype(LOW) for value in low_hidden]
        grad_first = grad_two + own_sum(
            times_t(low_hidden[0], w_up0) + times_t(low_hidden[1], w_up1)
        )
        grad_one, gain_one, shift_one = normalize_back(
            grad_first, unit_one, inv_one, gains[layer, 0]
        )
        spread_one = both(grad_one.astype(LOW))
        grad_o = t_times(spread_one, mixed).astype(LOW)
        grad_mixed = times(spread_one, w_o).astype(LOW).reshape(2 * tokens, 4, 2, 1, 64)
        grad_mixed = to_heads(grad_mixed, me_x)[:, 0]
        grad_q, grad_k, grad_v = attend_back(qkv, marks, summary, grad_mixed, scale)
        grad_pair = jnp.stack([jnp.sum(grad_q, axis=(0, 1)), jnp.sum(grad_v, axis=(0, 1))])
        low_packed = to_tokens(jnp.stack([grad_q, grad_k, grad_v], 1).astype(LOW), me_x)
        low_qk = low_packed[:, :, :, :2].transpose(0, 1, 3, 2, 4).reshape(2 * tokens, 1024)
        low_v = low_packed[:, :, :, 2].reshape(2 * tokens, 512)
        grad_qk = t_times(gathered, low_qk).astype(LOW)
        grad_v = t_times(gathered, low_v).astype(LOW)
        incoming = grad_one + own_sum(times_t(low_qk, w_qk) + times_t(low_v, w_v))
        grad_vo = jnp.concatenate(
            [grad_v.reshape(width, 4, 128), grad_o.reshape(width, 4, 128)], 2
        ).reshape(width, 1024)
        grads[layer] = reduce_phases(
            [by_phase(q, value) for q, value in enumerate([grad_qk, grad_vo] + grad_up + grad_down)],
            0,
            2,
        )
        small[layer] = (
            jnp.stack([gain_one, gain_two]),
            jnp.stack(
                [shift_one, shift_two, jnp.sum(grad_one, axis=0), jnp.sum(grad_two, axis=0)]
            ),
            grad_pair,
            grad_upbias,
        )
    grad_stream = absolute(incoming)

    parts = [jnp.stack([grads[layer][q] for layer in range(layers)], 1) for q in range(6)]
    parts = reduce_phases(parts, 2, 6)
    total = jnp.concatenate([value[0] for value in parts], 2).reshape(layers, 2, 32, 1536)
    keep = lax.dynamic_index_in_dim(total, core, 1, False)
    new = swap(lax.dynamic_index_in_dim(total, 1 - core, 1, False))
    total = jnp.stack(
        [jnp.where(core == 0, keep, new), jnp.where(core == 0, new, keep)], 2
    ).astype(FULL)
    out_qkv = total[..., :384].reshape(layers, 32, 2, 3, 128).transpose(0, 1, 3, 2, 4)
    out_qkv = out_qkv.reshape(layers, 32, 3, 256)
    out_o = total[..., 384:512].reshape(layers, 32, 256).transpose(0, 2, 1)
    out_up = total[..., 512:1024].reshape(layers, 32, 1024)
    out_down = total[..., 1024:].reshape(layers, 32, 1024).transpose(0, 2, 1)

    vec = absolute(
        jnp.concatenate([small[layer][0] for layer in range(layers)]
                        + [small[layer][1] for layer in range(layers)])
    )
    vec = vec.reshape(12, 32, 32).transpose(1, 0, 2).reshape(32, 1, 384)
    vec = jnp.broadcast_to(vec, (32, 4, 384))
    pair = jnp.stack([small[layer][2] for layer in range(layers)])
    head = me_x * 4 + core * 2 + z_lo
    pair = jnp.where((jnp.arange(16) == head)[:, None], pair[:, :, None], 0.0)
    pair = pair.reshape(layers, 2, 4, 4, 32, 2).transpose(4, 2, 0, 1, 3, 5).reshape(32, 4, 32)
    up = take_absolute(jnp.stack([small[layer][3] for layer in range(layers)]), me_x, 1)
    up = jnp.where((jnp.arange(2) == core)[:, None, None], up[:, :, None], 0.0)
    up = up.reshape(layers, 4, 4, 32, 8).transpose(3, 1, 0, 2, 4).reshape(32, 4, 64)
    vec = jnp.concatenate([vec, pair, up, jnp.zeros((32, 4, 32), FULL)], 2).reshape(128, 512)
    vec = jnp.sum(lax.all_to_all(vec, ALL, 0, 0, tiled=True), axis=0)

    return (
        result.reshape(stream.shape),
        grad_stream.reshape(stream.shape),
        out_qkv,
        vec[384:416].reshape(qv_bias.shape),
        out_o,
        vec[:128].reshape(norm_gains.shape),
        vec[128:384].reshape(shifts.shape),
        out_up,
        vec[416:480].reshape(in_bias.shape),
        out_down,
    )


def solution(mesh):
    return jax.shard_map(
        local,
        mesh=mesh,
        in_specs=(
            P("dp", ("ctx", "tensor"), None),
            P("dp", None),
            P(None, ("dp", "ctx"), None, "tensor"),
            P(None, None, "tensor", ("dp", "ctx")),
            P(None, "tensor", ("dp", "ctx")),
            P(None, None, ("dp", "ctx")),
            P(None, None, ("dp", "ctx")),
            P(None, ("dp", "ctx"), "tensor"),
            P(None, "tensor", ("dp", "ctx")),
            P(None, "tensor", ("dp", "ctx")),
            P("dp", ("ctx", "tensor"), None),
        ),
        out_specs=(
            P("dp", ("ctx", "tensor"), None),
            P("dp", ("ctx", "tensor"), None),
            P(None, ("dp", "ctx"), None, "tensor"),
            P(None, None, "tensor", ("dp", "ctx")),
            P(None, "tensor", ("dp", "ctx")),
            P(None, None, ("dp", "ctx")),
            P(None, None, ("dp", "ctx")),
            P(None, ("dp", "ctx"), "tensor"),
            P(None, "tensor", ("dp", "ctx")),
            P(None, "tensor", ("dp", "ctx")),
        ),
        check_vma=False,
    )
```

```python
import jax
import jax.numpy as jnp
from jax import lax
from jax.experimental import pallas as pl
from jax.experimental.pallas import tpu as pltpu
from jax.sharding import PartitionSpec as P

EPSILON = 1e-12
MASKED = -1000000000.0
ROOT_HALF = 0.7071067811865476
ROOT_TWOPI = 2.5066282746310002
ALL = ("dp", "ctx", "tensor")
LOW = jnp.bfloat16
FULL = jnp.float32

DIMS = (("x", 1), ("y", 1), ("z", 1), ("x", 3), ("y", 3), ("z", 3))
CANON = (("z", 3), ("z", 1), ("y", 3), ("y", 1), ("x", 3), ("x", 1))
GROUPS = [[(zl * 2 + c) * 4 + x for zl in range(2) for x in range(4)] for c in range(2)]


def exchange_perm(axis, mask):
    pairs = []
    for device in range(128):
        dp, ctx, x = device // 16, (device // 4) % 4, device % 4
        at = {"x": x, "y": dp % 4, "z": (dp // 4) * 2 + ctx // 2, "core": ctx % 2}
        at[axis] ^= mask
        other = ((at["z"] // 2) * 4 + at["y"]) * 16
        other += ((at["z"] % 2) * 2 + at["core"]) * 4 + at["x"]
        pairs.append((device, other))
    return pairs


def swap(value, axis="core", mask=1):
    return lax.ppermute(value, ALL, exchange_perm(axis, mask))


def dim_at(part, phase):
    return DIMS[(part + phase) % 6]


def gather_phases(parts, first, last):
    for phase in range(first, last):
        got = [swap(value, *dim_at(q, phase)) for q, value in enumerate(parts)]
        parts = [jnp.concatenate([value, new], 0) for value, new in zip(parts, got)]
    return parts


def reduce_phases(parts, first, last):
    for phase in range(first, last):
        half = parts[0].shape[0] // 2
        got = [swap(value[half:], *dim_at(q, phase)) for q, value in enumerate(parts)]
        parts = [
            (value[:half].astype(FULL) + new.astype(FULL)).astype(LOW)
            for value, new in zip(parts, got)
        ]
    return parts


def relative_x(me_x, r):
    return me_x ^ (0, 1, 3, 2)[r]


def take_relative(value, me_x, axis):
    return jnp.concatenate(
        [lax.dynamic_slice_in_dim(value, relative_x(me_x, r), 1, axis) for r in range(4)], axis
    )


def take_absolute(value, me_x, axis):
    parts = []
    for x in range(4):
        off = me_x ^ x
        parts.append(lax.dynamic_slice_in_dim(value, off ^ (off >> 1), 1, axis))
    return jnp.concatenate(parts, axis)


def both(value):
    return jnp.concatenate([value, swap(value)], 0)


def own_sum(value):
    half = value.shape[0] // 2
    value = value.astype(FULL)
    return value[:half] + swap(value[half:].astype(LOW)).astype(FULL)


def normalize(values, gain, shift):
    mean = jnp.mean(values, axis=-1, keepdims=True)
    centred = values - mean
    inverse = lax.rsqrt(jnp.mean(centred * centred, axis=-1, keepdims=True) + EPSILON)
    unit = centred * inverse
    return (unit * gain + shift, unit, inverse)


def normalize_back(incoming, unit, inverse, gain):
    scaled = incoming * gain
    inner = (
        scaled
        - jnp.mean(scaled, axis=-1, keepdims=True)
        - unit * jnp.mean(scaled * unit, axis=-1, keepdims=True)
    )
    return (inverse * inner, jnp.sum(incoming * unit, axis=0), jnp.sum(incoming, axis=0))


def dot(left, right, dims):
    return lax.dot_general(left, right, (dims, ((), ())), preferred_element_type=FULL)


def times(left, right):
    return dot(left, right, ((1,), (0,)))


def times_t(left, right):
    return dot(left, right, ((1,), (1,)))


def t_times(left, right):
    return dot(left, right, ((0,), (0,)))


VMEM_BYTES = 56 * 1024 * 1024


def part_axes(part, gathered):
    return [dim_at(part, 5 - a if gathered else a) for a in range(6)]


def part_spec(part, gathered):
    axes = part_axes(part, gathered)

    def index(r, *_):
        at = {("x", 3): r // 2, ("x", 1): r % 2}
        return tuple(at.get(dim, 0) for dim in axes) + (0, 0)

    return pl.BlockSpec(tuple(1 if dim[0] == "x" else 2 for dim in axes) + (64, 256), index)


def part_places(part, gathered):
    axes = part_axes(part, gathered)
    places = []
    for i in range(16):
        bits = {("z", 3): i >> 3, ("z", 1): (i >> 2) & 1, ("y", 3): (i >> 1) & 1, ("y", 1): i & 1}
        places.append(tuple(bits.get(dim, 0) for dim in axes))
    return places


def load_part(ref, part):
    return jnp.concatenate([ref[place] for place in part_places(part, True)], 0)


def store_part(ref, part, value):
    for i, place in enumerate(part_places(part, False)):
        ref[place] = value[i * 64 : (i + 1) * 64]


def part_view(value):
    return value.reshape((2,) * 6 + value.shape[-2:])


PART_OUT = jax.ShapeDtypeStruct((2,) * 6 + (64, 256), LOW)


def call(body, grid, in_specs, out_specs, out_shape, scratch, args, flops, scalars=()):
    size = sum(value.size * value.dtype.itemsize for value in args)
    size += sum(value.size * value.dtype.itemsize for value in out_shape)
    return pl.pallas_call(
        body,
        grid_spec=pltpu.PrefetchScalarGridSpec(
            num_scalar_prefetch=len(scalars),
            grid=grid,
            in_specs=in_specs,
            out_specs=out_specs,
            scratch_shapes=scratch,
        ),
        out_shape=out_shape,
        compiler_params=pltpu.CompilerParams(vmem_limit_bytes=VMEM_BYTES),
        cost_estimate=pl.CostEstimate(flops=flops, bytes_accessed=size, transcendentals=0),
    )(*scalars, *args)


def whole(shape):
    return pl.BlockSpec(shape, lambda *_: (0,) * len(shape))


def pick(value):
    return pl.BlockSpec(
        (1,) + value.shape[1:], lambda r, *_: (r,) + (0,) * (len(value.shape) - 1)
    )


def cross(left, right):
    lane = lax.broadcasted_iota(jnp.int32, left.shape, 1) < 64
    turned_left, turned_right = pltpu.roll(left, 64, 1), pltpu.roll(right, 64, 1)
    return jnp.where(lane, left, turned_right), jnp.where(lane, turned_left, right)


def split_rows(value):
    n = value.shape[0] // 4
    return (
        jnp.concatenate([value[:n], value[2 * n : 3 * n]], 0),
        jnp.concatenate([value[n : 2 * n], value[3 * n :]], 0),
    )


def join_rows(left, right):
    n = left.shape[0] // 2
    return jnp.concatenate([left[:n], right[:n], left[n:], right[n:]], 0)


def accumulate(ref, r, value):
    @pl.when(r == 0)
    def _():
        ref[...] = value

    @pl.when(r > 0)
    def _():
        ref[...] += value


def project_body(order, x, w_qk, w_vo, bias_q, bias_v, out):
    qk = times(x[...], load_part(w_qk, 0))
    v = times(x[...], load_part(w_vo, 1)[:, :128]) + bias_v[0]
    kinds = (qk[:, :128] + bias_q[0], qk[:, 128:], v)
    for i, value in enumerate(kinds):
        for j, head in enumerate(cross(*split_rows(value))):
            out[j, 0, :, i * 128 : (i + 1) * 128] = head.astype(LOW)


def heads_spec(rows, lanes):
    return pl.BlockSpec((2, 1, rows, lanes), lambda r, order: (0, order[r], 0, 0))


def project(order, x, w_qk, w_vo, bias_q, bias_v):
    m = x.shape[0]
    (out,) = call(
        project_body, (4,),
        [whole(x.shape), part_spec(0, True), part_spec(1, True), pick(bias_q), pick(bias_v)],
        [heads_spec(m // 2, 384)],
        [jax.ShapeDtypeStruct((2, 4, m // 2, 384), LOW)], [],
        (x, part_view(w_qk), part_view(w_vo), bias_q, bias_v), 2 * m * 1024 * 1536, (order,),
    )
    return out


def tokens_of(ref, lanes):
    left, right = cross(ref[0, 0, :, lanes].astype(FULL), ref[1, 0, :, lanes].astype(FULL))
    return join_rows(left, right).astype(LOW)


def mix_body(order, heads, w_vo, mixed_out, out):
    r = pl.program_id(0)
    mixed = tokens_of(heads, slice(0, 128))
    mixed_out[0] = mixed
    accumulate(out, r, times_t(mixed, load_part(w_vo, 1)[:, 128:]))


def mix(order, heads, w_vo):
    m = heads.shape[2] * 2
    return call(
        mix_body, (4,),
        [heads_spec(m // 2, 128), part_spec(1, True)],
        [pl.BlockSpec((1, m, 128), lambda r, *_: (r, 0, 0)), whole((m, 1024))],
        [jax.ShapeDtypeStruct((4, m, 128), LOW), jax.ShapeDtypeStruct((m, 1024), FULL)], [],
        (heads, part_view(w_vo)), 2 * m * 1024 * 512, (order,),
    )


def mix_back_body(order, x, w_vo, out):
    value = times(x[...], load_part(w_vo, 1)[:, 128:])
    for j, head in enumerate(cross(*split_rows(value))):
        out[j, 0] = head.astype(LOW)


def mix_back(order, x, w_vo):
    m = x.shape[0]
    (out,) = call(
        mix_back_body, (4,),
        [whole(x.shape), part_spec(1, True)],
        [heads_spec(m // 2, 128)],
        [jax.ShapeDtypeStruct((2, 4, m // 2, 128), LOW)], [],
        (x, part_view(w_vo)), 2 * m * 1024 * 512, (order,),
    )
    return out


def project_back_body(order, heads, x, spread, mixed, w_qk, w_vo, grad_qk, grad_vo, out):
    r = pl.program_id(0)
    q, k, v = [tokens_of(heads, slice(i * 128, (i + 1) * 128)) for i in range(3)]
    qk = jnp.concatenate([q, k], 1)
    store_part(grad_qk, 0, t_times(x[...], qk).astype(LOW))
    grad_v = t_times(x[...], v).astype(LOW)
    grad_o = t_times(spread[...], mixed[0]).astype(LOW)
    store_part(grad_vo, 1, jnp.concatenate([grad_v, grad_o], 1))
    terms = times_t(qk, load_part(w_qk, 0)) + times_t(v, load_part(w_vo, 1)[:, :128])
    accumulate(out, r, terms)


def project_back(order, heads, x, spread, mixed, w_qk, w_vo):
    m = x.shape[0]
    return call(
        project_back_body, (4,),
        [
            heads_spec(m // 2, 384), whole(x.shape), whole(x.shape), pick(mixed),
            part_spec(0, True), part_spec(1, True),
        ],
        [part_spec(0, False), part_spec(1, False), whole((m, 1024))],
        [PART_OUT, PART_OUT, jax.ShapeDtypeStruct((m, 1024), FULL)], [],
        (heads, x, spread, mixed, part_view(w_qk), part_view(w_vo)),
        2 * m * 1024 * 3584, (order,),
    )


def feed_body(x, bias, u0, u1, d0, d1, hidden_out, active_out, out):
    total = None
    for j, (up, down) in enumerate(((u0, d0), (u1, d1))):
        hidden = times(x[...], load_part(up, 2 + j)) + bias[0, j : j + 1]
        hidden_out[0, j] = hidden
        active = (hidden * (0.5 * (1.0 + lax.erf(hidden * ROOT_HALF)))).astype(LOW)
        active_out[0, j] = active
        term = times_t(active, load_part(down, 4 + j))
        total = term if total is None else total + term
    accumulate(out, pl.program_id(0), total)


def feed(x, bias, weights):
    m = x.shape[0]
    block = pl.BlockSpec((1, 2, m, 256), lambda r: (r, 0, 0, 0))
    return call(
        feed_body, (4,),
        [whole(x.shape), pick(bias)] + [part_spec(q, True) for q in range(2, 6)],
        [block, block, whole((m, 1024))],
        [
            jax.ShapeDtypeStruct((4, 2, m, 256), FULL), jax.ShapeDtypeStruct((4, 2, m, 256), LOW),
            jax.ShapeDtypeStruct((m, 1024), FULL),
        ], [],
        (x, bias) + tuple(part_view(w) for w in weights), 4 * m * 1024 * 2048,
    )


def feed_back_body(
    spread, x, hidden, active, u0, u1, d0, d1, g_u0, g_u1, g_d0, g_d1, grad_bias, out
):
    total = None
    for j, (up, down, g_up, g_down) in enumerate(((u0, d0, g_u0, g_d0), (u1, d1, g_u1, g_d1))):
        value = hidden[0, j]
        slope = 0.5 * (1.0 + lax.erf(value * ROOT_HALF))
        slope += value * jnp.exp(-0.5 * value * value) * (1.0 / ROOT_TWOPI)
        grad = times(spread[...], load_part(down, 4 + j)) * slope
        grad_bias[0, j : j + 1] = jnp.sum(grad, axis=0, keepdims=True)
        low = grad.astype(LOW)
        store_part(g_down, 4 + j, t_times(spread[...], active[0, j]).astype(LOW))
        store_part(g_up, 2 + j, t_times(x[...], low).astype(LOW))
        term = times_t(low, load_part(up, 2 + j))
        total = term if total is None else total + term
    accumulate(out, pl.program_id(0), total)


def feed_back(spread, x, hidden, active, weights):
    m = x.shape[0]
    return call(
        feed_back_body, (4,),
        [whole(x.shape), whole(x.shape), pick(hidden), pick(active)]
        + [part_spec(q, True) for q in range(2, 6)],
        [part_spec(q, False) for q in range(2, 6)]
        + [pl.BlockSpec((1, 2, 256), lambda r: (r, 0, 0)), whole((m, 1024))],
        [PART_OUT] * 4
        + [jax.ShapeDtypeStruct((4, 2, 256), FULL), jax.ShapeDtypeStruct((m, 1024), FULL)], [],
        (spread, x, hidden, active) + tuple(part_view(w) for w in weights), 8 * m * 1024 * 2048,
    )


def one_row(value, s):
    lane = lax.broadcasted_iota(jnp.int32, value.shape, 1) // 64 == s
    return jnp.where(lane, value, jnp.zeros_like(value))


def scores_of(keys, query, mark_keys, mark_query, s):
    scores = times_t(keys, one_row(query, s) * LOW(0.125))
    same = mark_keys[:, s : s + 1] == mark_query[s : s + 1, :]
    return jnp.where(same, scores, MASKED)


def attend_body(query, keys, values, mark_keys, mark_query, out, summary):
    turned = values[...].astype(FULL).T.astype(LOW)
    results = []
    for s in range(2):
        scores = scores_of(keys[...], query[...], mark_keys, mark_query, s)
        top = jnp.max(scores, axis=0, keepdims=True)
        weights = jnp.exp(scores - top)
        total = jnp.sum(weights, axis=0, keepdims=True)
        probs = (weights * (1.0 / total)).astype(LOW)
        results.append(times(turned[s * 64 : (s + 1) * 64], probs))
        summary[s : s + 1] = top + jnp.log(total)
    out[...] = jnp.concatenate(results, 0).T.astype(LOW)


def attend(qkv, mark_keys, mark_query):
    n = qkv.shape[0]
    q = 384

    return call(
        attend_body, (n // q,),
        [
            pl.BlockSpec((q, 128), lambda i: (i, 0)), pl.BlockSpec((n, 128), lambda i: (0, 1)),
            pl.BlockSpec((n, 128), lambda i: (0, 2)), whole((n, 2)),
            pl.BlockSpec((2, q), lambda i: (0, i)),
        ],
        [pl.BlockSpec((q, 128), lambda i: (i, 0)), pl.BlockSpec((2, q), lambda i: (0, i))],
        [jax.ShapeDtypeStruct((n, 128), LOW), jax.ShapeDtypeStruct((2, n), FULL)], [],
        (qkv, qkv, qkv, mark_keys, mark_query), 8 * n * n * 128,
    )


def attend_back_body(
    query, keys, values, grad_mixed, mark_keys, mark_query, summary, out, sums, sum_k, sum_v, sum_q
):
    i = pl.program_id(0)
    n, q = keys.shape[0], query.shape[0]
    turned = keys[...].astype(FULL).T.astype(LOW)
    lane = lax.broadcasted_iota(jnp.int32, (n, 128), 1) < 64
    grads_q, grads_k, grads_v = [], [], []
    for s in range(2):
        scores = scores_of(keys[...], query[...], mark_keys, mark_query, s)
        probs = jnp.exp(scores - summary[s : s + 1])
        grad_probs = times_t(values[...], one_row(grad_mixed[...], s))
        inner = jnp.sum(probs * grad_probs, axis=0, keepdims=True)
        low_probs = probs.astype(LOW)
        grad_scores = (probs * (grad_probs - inner)).astype(LOW)
        grads_v.append(times(low_probs, grad_mixed[...]))
        grads_k.append(times(grad_scores, query[...]))
        grads_q.append(times(turned[s * 64 : (s + 1) * 64], grad_scores))
    accumulate(sum_k, i, jnp.where(lane, grads_k[0], grads_k[1]) * 0.125)
    accumulate(sum_v, i, jnp.where(lane, grads_v[0], grads_v[1]))
    grad_q = jnp.concatenate(grads_q, 0).T * 0.125
    accumulate(sum_q, i, jnp.sum(grad_q, axis=0, keepdims=True))
    out[pl.ds(pl.multiple_of(i * q, q), q), :128] = grad_q.astype(LOW)

    @pl.when(i == pl.num_programs(0) - 1)
    def _():
        out[:, 128:256] = sum_k[...].astype(LOW)
        out[:, 256:] = sum_v[...].astype(LOW)
        sums[0:1] = sum_q[...]
        sums[1:2] = jnp.sum(sum_v[...], axis=0, keepdims=True)


def attend_back(qkv, grad_mixed, mark_keys, mark_query, summary):
    n = qkv.shape[0]
    q = 384
    return call(
        attend_back_body, (n // q,),
        [
            pl.BlockSpec((q, 128), lambda i: (i, 0)), pl.BlockSpec((n, 128), lambda i: (0, 1)),
            pl.BlockSpec((n, 128), lambda i: (0, 2)), pl.BlockSpec((q, 128), lambda i: (i, 0)),
            whole((n, 2)), pl.BlockSpec((2, q), lambda i: (0, i)),
            pl.BlockSpec((2, q), lambda i: (0, i)),
        ],
        [whole((n, 384)), whole((2, 128))],
        [jax.ShapeDtypeStruct((n, 384), LOW), jax.ShapeDtypeStruct((2, 128), FULL)],
        [pltpu.VMEM((n, 128), FULL), pltpu.VMEM((n, 128), FULL), pltpu.VMEM((1, 128), FULL)],
        (qkv, qkv, qkv, grad_mixed, mark_keys, mark_query, summary), 20 * n * n * 128,
    )


def trade(value):
    return lax.all_to_all(
        value, ("ctx", "tensor"), 0, 0, axis_index_groups=GROUPS, tiled=True
    )


def local(
    stream, segments, w_qkv, qv_bias, w_out, norm_gains, shifts, w_in, in_bias, w_back, cotangent
):
    layers = w_qkv.shape[0]
    dp, ctx, me_x = lax.axis_index("dp"), lax.axis_index("ctx"), lax.axis_index("tensor")
    core, z_lo = ctx & 1, ctx >> 1
    me_y, me_z = dp & 3, (dp >> 2) * 2 + z_lo
    rows = stream.shape[1]
    width = stream.shape[2]

    vectors = jnp.concatenate(
        [norm_gains.reshape(-1), shifts.reshape(-1), qv_bias.reshape(-1), in_bias.reshape(-1)]
    )
    vectors = jnp.pad(vectors, (0, 512 - vectors.shape[0]))
    spread = lax.all_to_all(jnp.broadcast_to(vectors, (128, 512)), ALL, 0, 0, tiled=True)
    spread = spread.reshape(32, 4, 512)
    gains_abs = spread[:, 0, 0:128].reshape(32, 4, 32).transpose(1, 0, 2).reshape(4, width)
    shifts_abs = spread[:, 0, 128:384].reshape(32, 8, 32).transpose(1, 0, 2).reshape(8, width)
    pair = spread[:, :, 384:416].reshape(32, 4, layers, 2, 2, 2, 2).transpose(2, 3, 1, 4, 5, 0, 6)
    pair = lax.dynamic_index_in_dim(pair.reshape(layers, 2, 4, 2, 2, 64), core, 3, False)
    pair = take_relative(pair, me_x, 2).astype(FULL)
    up = spread[:, :, 416:480].reshape(32, 4, layers, 2, 2, 8).transpose(2, 1, 3, 4, 0, 5)
    up = lax.dynamic_index_in_dim(up.reshape(layers, 4, 2, 2, 256), core, 2, False)
    up = take_relative(up, me_x, 1).astype(FULL)

    place = lax.broadcasted_iota(jnp.int32, (width, width), 1)
    block = place >> 6
    far_z = me_z ^ (((block >> 2) & 1) ^ ((block >> 3) * 3))
    far_y = me_y ^ ((block & 1) ^ (((block >> 1) & 1) * 3))
    source = (((far_z >> 1) * 4 + far_y) * 2 + (far_z & 1)) * 64 + (place & 63)
    reorder = source == lax.broadcasted_iota(jnp.int32, (width, width), 0)
    reorder_low = reorder.astype(LOW)
    reorder_full = reorder.astype(FULL)

    def absolute(value):
        return lax.dot_general(
            value, reorder_full, (((1,), (1,)), ((), ())), precision=lax.Precision.HIGHEST,
            preferred_element_type=FULL,
        )

    tokens = 2 * rows
    inputs = times(
        jnp.concatenate(
            [
                stream.reshape(tokens, width), cotangent.reshape(tokens, width),
                gains_abs, shifts_abs,
            ]
        ),
        reorder_low,
    )
    state = inputs[:tokens]
    incoming = inputs[tokens : 2 * tokens]
    gains = inputs[2 * tokens : 2 * tokens + 4].reshape(layers, 2, width)
    shift = inputs[2 * tokens + 4 :].reshape(layers, 4, width)

    columns = jnp.concatenate(
        [
            w_qkv.reshape(layers, 32, 3, 2, 128).transpose(0, 1, 3, 2, 4).reshape(
                layers, 32, 2, 384
            ),
            w_out.transpose(0, 2, 1).reshape(layers, 32, 2, 128),
            w_in.reshape(layers, 32, 2, 512),
            w_back.transpose(0, 2, 1).reshape(layers, 32, 2, 512),
        ],
        3,
    )
    keep = lax.dynamic_index_in_dim(columns, core, 2, False)
    new = swap(lax.dynamic_index_in_dim(columns, 1 - core, 2, False))
    rows_two = jnp.where(
        core == 0, jnp.concatenate([keep, new], 1), jnp.concatenate([new, keep], 1)
    )
    parts = [rows_two[None, :, :, q * 256 : (q + 1) * 256] for q in range(6)]
    parts = gather_phases(parts, 0, 4)
    weights = []
    for layer in range(layers):
        mine = [value[:, layer] for value in parts]
        if layer:
            mine, weights[-1] = lax.optimization_barrier((mine, weights[-1]))
        weights.append(gather_phases(mine, 4, 6))

    marks = segments.reshape(2, 2, 2, 4, rows)
    marks = jnp.where(core == 0, marks, marks[:, :, ::-1])
    marks = marks.transpose(0, 1, 3, 2, 4).reshape(2, 16 * rows)
    marks_t = marks.T
    order = jnp.stack([relative_x(me_x, r) for r in range(4)]).astype(jnp.int32)

    saved = []
    for layer in range(layers):
        w_qk, w_vo = weights[layer][:2]
        bias = pair[layer].reshape(2, 4, 1, 128)
        gathered = both(state.astype(LOW))
        qkv = trade(project(order, gathered, w_qk, w_vo, bias[0], bias[1]).reshape(8, 2 * rows, 384))
        qkv = qkv.reshape(16 * rows, 384)
        mixed, summary = attend(qkv, marks_t, marks)
        mixed = trade(mixed.reshape(8, 2 * rows, 128)).reshape(2, 4, 2 * rows, 128)
        mixed, attended = mix(order, mixed, w_vo)
        attended = own_sum(attended) + shift[layer, 2]
        first, unit_one, inv_one = normalize(state + attended, gains[layer, 0], shift[layer, 0])
        gathered_two = both(first.astype(LOW))
        hidden, active, down = feed(gathered_two, up[layer], weights[layer][2:])
        down = own_sum(down)
        state, unit_two, inv_two = normalize(
            first + down + shift[layer, 3], gains[layer, 1], shift[layer, 1]
        )
        saved.append(
            (gathered, qkv, summary, mixed, unit_one, inv_one, gathered_two, hidden, active,
             unit_two, inv_two)
        )
    result = absolute(state)

    grads = [None] * layers
    small = [None] * layers
    for layer in reversed(range(layers)):
        w_qk, w_vo = weights[layer][:2]
        (gathered, qkv, summary, mixed, unit_one, inv_one, gathered_two, hidden, active,
         unit_two, inv_two) = saved[layer]
        grad_two, gain_two, shift_two = normalize_back(
            incoming, unit_two, inv_two, gains[layer, 1]
        )
        spread_two = both(grad_two.astype(LOW))
        *grad_feed, grad_upbias, grad_first = feed_back(
            spread_two, gathered_two, hidden, active, weights[layer][2:]
        )
        grad_first = grad_two + own_sum(grad_first)
        grad_one, gain_one, shift_one = normalize_back(
            grad_first, unit_one, inv_one, gains[layer, 0]
        )
        spread_one = both(grad_one.astype(LOW))
        grad_mixed = trade(mix_back(order, spread_one, w_vo).reshape(8, 2 * rows, 128))
        grad_mixed = grad_mixed.reshape(16 * rows, 128)
        low_packed, grad_pair = attend_back(qkv, grad_mixed, marks_t, marks, summary)
        grad_pair = grad_pair.reshape(2, 2, 64).sum(1)
        low_packed = trade(low_packed.reshape(8, 2 * rows, 384)).reshape(2, 4, 2 * rows, 384)
        grad_qk, grad_vo, grad_x = project_back(
            order, low_packed, gathered, spread_one, mixed, w_qk, w_vo
        )
        incoming = grad_one + own_sum(grad_x)
        grads[layer] = reduce_phases(
            [value.reshape(64, 64, 256) for value in [grad_qk, grad_vo] + grad_feed], 0, 2
        )
        small[layer] = (
            jnp.stack([gain_one, gain_two]),
            jnp.stack(
                [shift_one, shift_two, jnp.sum(grad_one, axis=0), jnp.sum(grad_two, axis=0)]
            ),
            grad_pair,
            grad_upbias,
        )
    grad_stream = absolute(incoming)

    parts = [jnp.stack([grads[layer][q] for layer in range(layers)], 1) for q in range(6)]
    parts = reduce_phases(parts, 2, 6)
    total = jnp.concatenate([value[0] for value in parts], 2).reshape(layers, 2, 32, 1536)
    keep = lax.dynamic_index_in_dim(total, core, 1, False)
    new = swap(lax.dynamic_index_in_dim(total, 1 - core, 1, False))
    total = jnp.stack(
        [jnp.where(core == 0, keep, new), jnp.where(core == 0, new, keep)], 2
    ).astype(FULL)
    out_qkv = total[..., :384].reshape(layers, 32, 2, 3, 128).transpose(0, 1, 3, 2, 4)
    out_qkv = out_qkv.reshape(layers, 32, 3, 256)
    out_o = total[..., 384:512].reshape(layers, 32, 256).transpose(0, 2, 1)
    out_up = total[..., 512:1024].reshape(layers, 32, 1024)
    out_down = total[..., 1024:].reshape(layers, 32, 1024).transpose(0, 2, 1)

    vec = absolute(
        jnp.concatenate([small[layer][0] for layer in range(layers)]
                        + [small[layer][1] for layer in range(layers)])
    )
    vec = vec.reshape(12, 32, 32).transpose(1, 0, 2).reshape(32, 1, 384)
    vec = jnp.broadcast_to(vec, (32, 4, 384))
    pair = jnp.stack([small[layer][2] for layer in range(layers)])
    head = me_x * 4 + core * 2 + z_lo
    pair = jnp.where((jnp.arange(16) == head)[:, None], pair[:, :, None], 0.0)
    pair = pair.reshape(layers, 2, 4, 4, 32, 2).transpose(4, 2, 0, 1, 3, 5).reshape(32, 4, 32)
    up = take_absolute(jnp.stack([small[layer][3] for layer in range(layers)]), me_x, 1)
    up = jnp.where((jnp.arange(2) == core)[:, None, None], up[:, :, None], 0.0)
    up = up.reshape(layers, 4, 4, 32, 8).transpose(3, 1, 0, 2, 4).reshape(32, 4, 64)
    vec = jnp.concatenate([vec, pair, up, jnp.zeros((32, 4, 32), FULL)], 2).reshape(128, 512)
    vec = jnp.sum(lax.all_to_all(vec, ALL, 0, 0, tiled=True), axis=0)

    return (
        result.reshape(stream.shape),
        grad_stream.reshape(stream.shape),
        out_qkv,
        vec[384:416].reshape(qv_bias.shape),
        out_o,
        vec[:128].reshape(norm_gains.shape),
        vec[128:384].reshape(shifts.shape),
        out_up,
        vec[416:480].reshape(in_bias.shape),
        out_down,
    )


def solution(mesh):
    return jax.shard_map(
        local,
        mesh=mesh,
        in_specs=(
            P("dp", ("ctx", "tensor"), None),
            P("dp", None),
            P(None, ("dp", "ctx"), None, "tensor"),
            P(None, None, "tensor", ("dp", "ctx")),
            P(None, "tensor", ("dp", "ctx")),
            P(None, None, ("dp", "ctx")),
            P(None, None, ("dp", "ctx")),
            P(None, ("dp", "ctx"), "tensor"),
            P(None, "tensor", ("dp", "ctx")),
            P(None, "tensor", ("dp", "ctx")),
            P("dp", ("ctx", "tensor"), None),
        ),
        out_specs=(
            P("dp", ("ctx", "tensor"), None),
            P("dp", ("ctx", "tensor"), None),
            P(None, ("dp", "ctx"), None, "tensor"),
            P(None, None, "tensor", ("dp", "ctx")),
            P(None, "tensor", ("dp", "ctx")),
            P(None, None, ("dp", "ctx")),
            P(None, None, ("dp", "ctx")),
            P(None, ("dp", "ctx"), "tensor"),
            P(None, "tensor", ("dp", "ctx")),
            P(None, "tensor", ("dp", "ctx")),
        ),
        check_vma=False,
    )
```

```python
import functools

import jax
import jax.numpy as jnp
from jax import lax
from jax.experimental import pallas as pl
from jax.experimental.pallas import tpu as pltpu
from jax.sharding import PartitionSpec as P

EPSILON = 1e-12
MASKED = -1000000000.0
ROOT_HALF = 0.7071067811865476
ROOT_TWOPI = 2.5066282746310002
ALL = ("dp", "ctx", "tensor")
LOW = jnp.bfloat16
FULL = jnp.float32

X1, X3, Y1, Y3, Z1, Z3 = ("x", 1), ("x", 3), ("y", 1), ("y", 3), ("z", 1), ("z", 3)
ORDERS = (
    (X1, Y3, X3, Z3, Y1, Z1),
    (Y1, X1, Z3, X3, Z1, Y3),
    (X3, Z1, X1, Y1, Y3, Z3),
    (Z1, X3, Y3, X1, Z3, Y1),
)
GROUPS = [[(zl * 2 + c) * 4 + x for zl in range(2) for x in range(4)] for c in range(2)]


def exchange_perm(axis, mask):
    pairs = []
    for device in range(128):
        dp, ctx, x = device // 16, (device // 4) % 4, device % 4
        at = {"x": x, "y": dp % 4, "z": (dp // 4) * 2 + ctx // 2, "core": ctx % 2}
        at[axis] ^= mask
        other = ((at["z"] // 2) * 4 + at["y"]) * 16
        other += ((at["z"] % 2) * 2 + at["core"]) * 4 + at["x"]
        pairs.append((device, other))
    return pairs


def swap(value, axis="core", mask=1):
    return lax.ppermute(value, ALL, exchange_perm(axis, mask))


def gather_early(parts):
    for phase in range(4):
        got = [swap(value, *ORDERS[k][phase]) for k, value in enumerate(parts)]
        parts = [jnp.concatenate([value, new], 0) for value, new in zip(parts, got)]
    return parts


def gather_late(parts):
    near = [swap(value, *ORDERS[k][4]) for k, value in enumerate(parts)]
    far = [swap(value, *ORDERS[k][5]) for k, value in enumerate(parts)]
    both_far = [swap(value, *ORDERS[k][5]) for k, value in enumerate(near)]
    return [list(four) for four in zip(parts, near, far, both_far)]


def add_low(left, right):
    return (left.astype(FULL) + right.astype(FULL)).astype(LOW)


def reduce_first(pairs, orders):
    parts = [add_low(kept, swap(sent, *ORDERS[k][5])) for k, (kept, sent) in zip(orders, pairs)]
    return reduce_phase(parts, orders, 1)


def reduce_phase(parts, orders, phase):
    half = parts[0].shape[0] // 2
    got = [swap(value[half:], *ORDERS[k][5 - phase]) for k, value in zip(orders, parts)]
    return [add_low(value[:half], new) for value, new in zip(parts, got)]


def reduce_rest(parts, orders):
    for phase in range(2, 6):
        parts = reduce_phase(parts, orders, phase)
    return [value[0] for value in parts]


def relative_x(me_x, r):
    return me_x ^ (0, 1, 3, 2)[r]


def take_relative(value, me_x, axis):
    return jnp.concatenate(
        [lax.dynamic_slice_in_dim(value, relative_x(me_x, r), 1, axis) for r in range(4)], axis
    )


def take_absolute(value, me_x, axis):
    parts = []
    for x in range(4):
        off = me_x ^ x
        parts.append(lax.dynamic_slice_in_dim(value, off ^ (off >> 1), 1, axis))
    return jnp.concatenate(parts, axis)


def both(value):
    return jnp.concatenate([value, swap(value)], 0)


def own_sum(value):
    half = value.shape[0] // 2
    value = value.astype(FULL)
    return value[:half] + swap(value[half:].astype(LOW)).astype(FULL)


def normalize(values, gain, shift):
    mean = jnp.mean(values, axis=-1, keepdims=True)
    centred = values - mean
    inverse = lax.rsqrt(jnp.mean(centred * centred, axis=-1, keepdims=True) + EPSILON)
    unit = centred * inverse
    return (unit * gain + shift, unit, inverse)


def normalize_back(incoming, unit, inverse, gain):
    scaled = incoming * gain
    inner = (
        scaled
        - jnp.mean(scaled, axis=-1, keepdims=True)
        - unit * jnp.mean(scaled * unit, axis=-1, keepdims=True)
    )
    return (inverse * inner, jnp.sum(incoming * unit, axis=0), jnp.sum(incoming, axis=0))


def dot(left, right, dims):
    return lax.dot_general(left, right, (dims, ((), ())), preferred_element_type=FULL)


def times(left, right):
    return dot(left, right, ((1,), (0,)))


def times_t(left, right):
    return dot(left, right, ((1,), (1,)))


def t_times(left, right):
    return dot(left, right, ((0,), (0,)))


VMEM_BYTES = 56 * 1024 * 1024


ZY = (Z3, Z1, Y3, Y1)


class Exchanged:
    def __init__(self, k, pieces, columns):
        self.k = k
        self.arrays = [value.reshape((2,) * 4 + value.shape[1:]) for value in pieces]
        axes = ORDERS[k][3::-1]

        def index(r, *_):
            at = {X3: r // 2, X1: r % 2}
            return tuple(at.get(dim, 0) for dim in axes) + (0, 0)

        shape = tuple(1 if dim[0] == "x" else 2 for dim in axes) + (64, columns)
        self.specs = [pl.BlockSpec(shape, index)] * 4

    def load(self, info, refs):
        rows = []
        for i in range(16):
            bits = dict(zip(ZY, (i >> 3, (i >> 2) & 1, (i >> 1) & 1, i & 1)))
            piece = 2 * bits[ORDERS[self.k][5]] + bits[ORDERS[self.k][4]]
            at = tuple(bits.get(dim, 0) for dim in ORDERS[self.k][3::-1])
            rows.append(refs[piece][at])
        return jnp.concatenate(rows, 0)


class Gathered:
    def __init__(self, array, base, columns, step):
        self.arrays = [array]

        def index(r, info):
            return (0, 0, info[r], 0, base + info[4] * step)

        self.specs = [pl.BlockSpec((16, 2, 1, 32, columns), index)]

    def load(self, info, refs):
        (ref,) = refs
        return jnp.concatenate(
            [ref[info[5 + i], half, 0] for i in range(16) for half in range(2)], 0
        )


class Grads:
    def __init__(self, k, width, at):
        self.k, self.width, self.at = k, width, at

    def store(self, refs, value):
        for i in range(16):
            bits = dict(zip(ZY, (i >> 3, (i >> 2) & 1, (i >> 1) & 1, i & 1)))
            place = tuple(bits.get(dim, 0) for dim in ORDERS[self.k][4::-1])
            place += (slice(None), slice(self.at, self.at + value.shape[1]))
            refs[bits[ORDERS[self.k][5]]][place] = value[i * 64 : (i + 1) * 64]


def grad_spec(sink):
    axes = ORDERS[sink.k][4::-1]

    def index(r, *_):
        at = {X3: r // 2, X1: r % 2}
        return tuple(at.get(dim, 0) for dim in axes) + (0, 0)

    shape = tuple(1 if dim[0] == "x" else 2 for dim in axes) + (64, sink.width)
    return [pl.BlockSpec(shape, index)] * 2


def grad_outs(sinks):
    first = [sink for sink in sinks if sink.at == 0]
    specs = [spec for sink in first for spec in grad_spec(sink)]
    shapes = [
        jax.ShapeDtypeStruct((2,) * 5 + (64, sink.width), LOW) for sink in first for _ in range(2)
    ]
    return specs, shapes


def grad_refs(sinks, refs):
    pairs, at = [], -2
    for sink in sinks:
        at += 2 if sink.at == 0 else 0
        pairs.append(refs[at : at + 2])
    return pairs


def take_refs(weights, refs):
    groups = []
    for weight in weights:
        groups.append(refs[: len(weight.arrays)])
        refs = refs[len(weight.arrays) :]
    return groups, refs


APART = [Grads(k, 128, 0) for k in range(4)]
PAIRED = [Grads(k, 256, at) for k in (0, 2) for at in (0, 128)]
FEED = [Grads(k, 512, at) for k in (0, 2) for at in (0, 256)]


def halves(refs):
    pairs = zip(refs[::2], refs[1::2])
    return [tuple(v.reshape((32,) + v.shape[-2:]) for v in pair) for pair in pairs]


def joined(weights, field):
    return [entry for weight in weights for entry in getattr(weight, field)]


def call(body, grid, in_specs, out_specs, out_shape, scratch, args, flops, scalars=()):
    size = sum(value.size * value.dtype.itemsize for value in args)
    size += sum(value.size * value.dtype.itemsize for value in out_shape)
    return pl.pallas_call(
        body,
        grid_spec=pltpu.PrefetchScalarGridSpec(
            num_scalar_prefetch=len(scalars),
            grid=grid,
            in_specs=in_specs,
            out_specs=out_specs,
            scratch_shapes=scratch,
        ),
        out_shape=out_shape,
        compiler_params=pltpu.CompilerParams(vmem_limit_bytes=VMEM_BYTES),
        cost_estimate=pl.CostEstimate(flops=flops, bytes_accessed=size, transcendentals=0),
    )(*scalars, *args)


def whole(shape):
    return pl.BlockSpec(shape, lambda *_: (0,) * len(shape))


def pick(value):
    return pl.BlockSpec(
        (1,) + value.shape[1:], lambda r, *_: (r,) + (0,) * (len(value.shape) - 1)
    )


def cross(left, right):
    lane = lax.broadcasted_iota(jnp.int32, left.shape, 1) < 64
    turned_left, turned_right = pltpu.roll(left, 64, 1), pltpu.roll(right, 64, 1)
    return jnp.where(lane, left, turned_right), jnp.where(lane, turned_left, right)


def split_rows(value):
    n = value.shape[0] // 4
    return (
        jnp.concatenate([value[:n], value[2 * n : 3 * n]], 0),
        jnp.concatenate([value[n : 2 * n], value[3 * n :]], 0),
    )


def join_rows(left, right):
    n = left.shape[0] // 2
    return jnp.concatenate([left[:n], right[:n], left[n:], right[n:]], 0)


def accumulate(ref, r, value):
    @pl.when(r == 0)
    def _():
        ref[...] = value

    @pl.when(r > 0)
    def _():
        ref[...] += value


def project_body(weights, info, x, *refs):
    groups, (bias_q, bias_v, out) = take_refs(weights, refs)
    q, k, v = [times(x[...], w.load(info, group)) for w, group in zip(weights, groups)]
    for i, value in enumerate((q + bias_q[0], k, v + bias_v[0])):
        for j, head in enumerate(cross(*split_rows(value))):
            out[j, 0, :, i * 128 : (i + 1) * 128] = head.astype(LOW)


def heads_spec(rows, lanes):
    return pl.BlockSpec((2, 1, rows, lanes), lambda r, order: (0, order[r], 0, 0))


def project(order, x, weights, bias_q, bias_v):
    m = x.shape[0]
    weights = weights[:3]
    (out,) = call(
        functools.partial(project_body, weights), (4,),
        [whole(x.shape)] + joined(weights, "specs") + [pick(bias_q), pick(bias_v)],
        [heads_spec(m // 2, 384)],
        [jax.ShapeDtypeStruct((2, 4, m // 2, 384), LOW)], [],
        [x] + joined(weights, "arrays") + [bias_q, bias_v], 2 * m * 1024 * 1536, (order,),
    )
    return out


def tokens_of(ref, lanes):
    left, right = cross(ref[0, 0, :, lanes].astype(FULL), ref[1, 0, :, lanes].astype(FULL))
    return join_rows(left, right).astype(LOW)


def mix_body(weight, info, heads, *refs):
    (group,), (mixed_out, out) = take_refs([weight], refs)
    mixed = tokens_of(heads, slice(0, 128))
    mixed_out[0] = mixed
    accumulate(out, pl.program_id(0), times_t(mixed, weight.load(info, group)))


def mix(order, heads, weight):
    m = heads.shape[2] * 2
    return call(
        functools.partial(mix_body, weight), (4,),
        [heads_spec(m // 2, 128)] + weight.specs,
        [pl.BlockSpec((1, m, 128), lambda r, *_: (r, 0, 0)), whole((m, 1024))],
        [jax.ShapeDtypeStruct((4, m, 128), LOW), jax.ShapeDtypeStruct((m, 1024), FULL)], [],
        [heads] + weight.arrays, 2 * m * 1024 * 512, (order,),
    )


def mix_back_body(weight, info, x, *refs):
    (group,), (out,) = take_refs([weight], refs)
    value = times(x[...], weight.load(info, group))
    for j, head in enumerate(cross(*split_rows(value))):
        out[j, 0] = head.astype(LOW)


def mix_back(order, x, weight):
    m = x.shape[0]
    (out,) = call(
        functools.partial(mix_back_body, weight), (4,),
        [whole(x.shape)] + weight.specs,
        [heads_spec(m // 2, 128)],
        [jax.ShapeDtypeStruct((2, 4, m // 2, 128), LOW)], [],
        [x] + weight.arrays, 2 * m * 1024 * 512, (order,),
    )
    return out


def project_back_body(weights, sinks, info, heads, x, spread, mixed, *refs):
    groups, refs = take_refs(weights, refs)
    pairs, out = grad_refs(sinks, refs[:-1]), refs[-1]
    terms = None
    for i in range(3):
        low = tokens_of(heads, slice(i * 128, (i + 1) * 128))
        sinks[i].store(pairs[i], t_times(x[...], low).astype(LOW))
        term = times_t(low, weights[i].load(info, groups[i]))
        terms = term if terms is None else terms + term
    sinks[3].store(pairs[3], t_times(spread[...], mixed[0]).astype(LOW))
    accumulate(out, pl.program_id(0), terms)


def project_back(order, heads, x, spread, mixed, weights, sinks):
    m = x.shape[0]
    weights = weights[:3]
    specs, shapes = grad_outs(sinks)
    *grads, out = call(
        functools.partial(project_back_body, weights, sinks), (4,),
        [heads_spec(m // 2, 384), whole(x.shape), whole(x.shape), pick(mixed)]
        + joined(weights, "specs"),
        specs + [whole((m, 1024))],
        shapes + [jax.ShapeDtypeStruct((m, 1024), FULL)], [],
        [heads, x, spread, mixed] + joined(weights, "arrays"), 2 * m * 1024 * 3584, (order,),
    )
    return halves(grads), out


def feed_body(weights, info, x, bias, *refs):
    groups, (hidden_out, active_out, out) = take_refs(weights, refs)
    total = None
    for j in range(2):
        hidden = times(x[...], weights[j].load(info, groups[j])) + bias[0, j : j + 1]
        hidden_out[0, j] = hidden
        active = (hidden * (0.5 * (1.0 + lax.erf(hidden * ROOT_HALF)))).astype(LOW)
        active_out[0, j] = active
        term = times_t(active, weights[2 + j].load(info, groups[2 + j]))
        total = term if total is None else total + term
    accumulate(out, pl.program_id(0), total)


def feed(order, x, bias, weights):
    m = x.shape[0]
    block = pl.BlockSpec((1, 2, m, 256), lambda r, *_: (r, 0, 0, 0))
    return call(
        functools.partial(feed_body, weights), (4,),
        [whole(x.shape), pick(bias)] + joined(weights, "specs"),
        [block, block, whole((m, 1024))],
        [
            jax.ShapeDtypeStruct((4, 2, m, 256), FULL), jax.ShapeDtypeStruct((4, 2, m, 256), LOW),
            jax.ShapeDtypeStruct((m, 1024), FULL),
        ], [],
        [x, bias] + joined(weights, "arrays"), 4 * m * 1024 * 2048, (order,),
    )


def feed_back_body(weights, info, spread, x, hidden, active, *refs):
    groups, refs = take_refs(weights, refs)
    pairs, (grad_bias, out) = grad_refs(FEED, refs[:-2]), refs[-2:]
    total = None
    for j in range(2):
        value = hidden[0, j]
        slope = 0.5 * (1.0 + lax.erf(value * ROOT_HALF))
        slope += value * jnp.exp(-0.5 * value * value) * (1.0 / ROOT_TWOPI)
        grad = times(spread[...], weights[2 + j].load(info, groups[2 + j])) * slope
        grad_bias[0, j : j + 1] = jnp.sum(grad, axis=0, keepdims=True)
        low = grad.astype(LOW)
        FEED[2 + j].store(pairs[2 + j], t_times(spread[...], active[0, j]).astype(LOW))
        FEED[j].store(pairs[j], t_times(x[...], low).astype(LOW))
        term = times_t(low, weights[j].load(info, groups[j]))
        total = term if total is None else total + term
    accumulate(out, pl.program_id(0), total)


def feed_back(order, spread, x, hidden, active, weights):
    m = x.shape[0]
    specs, shapes = grad_outs(FEED)
    *grads, grad_bias, out = call(
        functools.partial(feed_back_body, weights), (4,),
        [whole(x.shape), whole(x.shape), pick(hidden), pick(active)] + joined(weights, "specs"),
        specs + [pl.BlockSpec((1, 2, 256), lambda r, *_: (r, 0, 0)), whole((m, 1024))],
        shapes
        + [jax.ShapeDtypeStruct((4, 2, 256), FULL), jax.ShapeDtypeStruct((m, 1024), FULL)], [],
        [spread, x, hidden, active] + joined(weights, "arrays"), 8 * m * 1024 * 2048, (order,),
    )
    return halves(grads), grad_bias, out


def one_row(value, s):
    lane = lax.broadcasted_iota(jnp.int32, value.shape, 1) // 64 == s
    return jnp.where(lane, value, jnp.zeros_like(value))


def scores_of(keys, query, mark_keys, mark_query, s):
    scores = times_t(keys, one_row(query, s) * LOW(0.125))
    same = mark_keys[:, s : s + 1] == mark_query[s : s + 1, :]
    return jnp.where(same, scores, MASKED)


def attend_body(query, keys, values, mark_keys, mark_query, out, summary):
    turned = values[...].astype(FULL).T.astype(LOW)
    results = []
    for s in range(2):
        scores = scores_of(keys[...], query[...], mark_keys, mark_query, s)
        top = jnp.max(scores, axis=0, keepdims=True)
        weights = jnp.exp(scores - top)
        total = jnp.sum(weights, axis=0, keepdims=True)
        probs = (weights * (1.0 / total)).astype(LOW)
        results.append(times(turned[s * 64 : (s + 1) * 64], probs))
        summary[s : s + 1] = top + jnp.log(total)
    out[...] = jnp.concatenate(results, 0).T.astype(LOW)


def attend(qkv, mark_keys, mark_query):
    n = qkv.shape[0]
    q = 384

    return call(
        attend_body, (n // q,),
        [
            pl.BlockSpec((q, 128), lambda i: (i, 0)), pl.BlockSpec((n, 128), lambda i: (0, 1)),
            pl.BlockSpec((n, 128), lambda i: (0, 2)), whole((n, 2)),
            pl.BlockSpec((2, q), lambda i: (0, i)),
        ],
        [pl.BlockSpec((q, 128), lambda i: (i, 0)), pl.BlockSpec((2, q), lambda i: (0, i))],
        [jax.ShapeDtypeStruct((n, 128), LOW), jax.ShapeDtypeStruct((2, n), FULL)], [],
        (qkv, qkv, qkv, mark_keys, mark_query), 8 * n * n * 128,
    )


def attend_back_body(
    query, keys, values, grad_mixed, mark_keys, mark_query, summary, out, sums, sum_k, sum_v, sum_q
):
    i = pl.program_id(0)
    n, q = keys.shape[0], query.shape[0]
    turned = keys[...].astype(FULL).T.astype(LOW)
    lane = lax.broadcasted_iota(jnp.int32, (n, 128), 1) < 64
    grads_q, grads_k, grads_v = [], [], []
    for s in range(2):
        scores = scores_of(keys[...], query[...], mark_keys, mark_query, s)
        probs = jnp.exp(scores - summary[s : s + 1])
        grad_probs = times_t(values[...], one_row(grad_mixed[...], s))
        inner = jnp.sum(probs * grad_probs, axis=0, keepdims=True)
        low_probs = probs.astype(LOW)
        grad_scores = (probs * (grad_probs - inner)).astype(LOW)
        grads_v.append(times(low_probs, grad_mixed[...]))
        grads_k.append(times(grad_scores, query[...]))
        grads_q.append(times(turned[s * 64 : (s + 1) * 64], grad_scores))
    accumulate(sum_k, i, jnp.where(lane, grads_k[0], grads_k[1]) * 0.125)
    accumulate(sum_v, i, jnp.where(lane, grads_v[0], grads_v[1]))
    grad_q = jnp.concatenate(grads_q, 0).T * 0.125
    accumulate(sum_q, i, jnp.sum(grad_q, axis=0, keepdims=True))
    out[pl.ds(pl.multiple_of(i * q, q), q), :128] = grad_q.astype(LOW)

    @pl.when(i == pl.num_programs(0) - 1)
    def _():
        out[:, 128:256] = sum_k[...].astype(LOW)
        out[:, 256:] = sum_v[...].astype(LOW)
        sums[0:1] = sum_q[...]
        sums[1:2] = jnp.sum(sum_v[...], axis=0, keepdims=True)


def attend_back(qkv, grad_mixed, mark_keys, mark_query, summary):
    n = qkv.shape[0]
    q = 384
    return call(
        attend_back_body, (n // q,),
        [
            pl.BlockSpec((q, 128), lambda i: (i, 0)), pl.BlockSpec((n, 128), lambda i: (0, 1)),
            pl.BlockSpec((n, 128), lambda i: (0, 2)), pl.BlockSpec((q, 128), lambda i: (i, 0)),
            whole((n, 2)), pl.BlockSpec((2, q), lambda i: (0, i)),
            pl.BlockSpec((2, q), lambda i: (0, i)),
        ],
        [whole((n, 384)), whole((2, 128))],
        [jax.ShapeDtypeStruct((n, 384), LOW), jax.ShapeDtypeStruct((2, 128), FULL)],
        [pltpu.VMEM((n, 128), FULL), pltpu.VMEM((n, 128), FULL), pltpu.VMEM((1, 128), FULL)],
        (qkv, qkv, qkv, grad_mixed, mark_keys, mark_query, summary), 20 * n * n * 128,
    )


def trade(value):
    return lax.all_to_all(
        value, ("ctx", "tensor"), 0, 0, axis_index_groups=GROUPS, tiled=True
    )


def local(
    stream, segments, w_qkv, qv_bias, w_out, norm_gains, shifts, w_in, in_bias, w_back, cotangent
):
    layers = w_qkv.shape[0]
    dp, ctx, me_x = lax.axis_index("dp"), lax.axis_index("ctx"), lax.axis_index("tensor")
    core, z_lo = ctx & 1, ctx >> 1
    me_y, me_z = dp & 3, (dp >> 2) * 2 + z_lo
    rows = stream.shape[1]
    width = stream.shape[2]

    def both_rows(columns):
        axis = columns.ndim - 2
        keep = lax.dynamic_index_in_dim(columns, core, axis, False)
        new = swap(lax.dynamic_index_in_dim(columns, 1 - core, axis, False))
        return jnp.where(
            core == 0, jnp.concatenate([keep, new], -2), jnp.concatenate([new, keep], -2)
        )

    lead = both_rows(
        jnp.concatenate(
            [
                w_qkv[0].reshape(32, 3, 2, 128).transpose(0, 2, 1, 3).reshape(32, 2, 384),
                w_out[0].T.reshape(32, 2, 128),
            ],
            2,
        )
    )
    lead = gather_early([lead[None, :, k * 128 : (k + 1) * 128] for k in range(4)])
    lead, norm_gains = lax.optimization_barrier((lead, norm_gains))
    lead = gather_late(lead)

    later = jnp.concatenate(
        [w_in[0], w_back[0].T, w_qkv[1].reshape(32, 768), w_out[1].T, w_in[1], w_back[1].T], 1
    )
    later = lax.all_gather(later, "tensor", axis=0, tiled=True)

    def everywhere(value):
        value = lax.all_gather(value, ("dp", "ctx"), axis=0, tiled=True)
        return value.reshape(16, 2, 4, 32, value.shape[1])

    feed_zero = everywhere(later[:, :2048])
    attention_one = everywhere(later[:, 2048:3072])
    feed_one = everywhere(later[:, 3072:])
    attention_w = [
        [Exchanged(k, lead[k], 128) for k in range(4)],
        [Gathered(attention_one, 2 * k, 128, 1) for k in range(4)],
    ]
    feed_w = [
        [Gathered(value, base, 256, 2) for base in (0, 1, 4, 5)] for value in (feed_zero, feed_one)
    ]

    vectors = jnp.concatenate(
        [norm_gains.reshape(-1), shifts.reshape(-1), qv_bias.reshape(-1), in_bias.reshape(-1)]
    )
    vectors = jnp.pad(vectors, (0, 512 - vectors.shape[0]))
    spread = lax.all_to_all(jnp.broadcast_to(vectors, (128, 512)), ALL, 0, 0, tiled=True)
    spread = spread.reshape(32, 4, 512)
    gains_abs = spread[:, 0, 0:128].reshape(32, 4, 32).transpose(1, 0, 2).reshape(4, width)
    shifts_abs = spread[:, 0, 128:384].reshape(32, 8, 32).transpose(1, 0, 2).reshape(8, width)
    pair = spread[:, :, 384:416].reshape(32, 4, layers, 2, 2, 2, 2).transpose(2, 3, 1, 4, 5, 0, 6)
    pair = lax.dynamic_index_in_dim(pair.reshape(layers, 2, 4, 2, 2, 64), core, 3, False)
    pair = take_relative(pair, me_x, 2).astype(FULL)
    up = spread[:, :, 416:480].reshape(32, 4, layers, 2, 2, 8).transpose(2, 1, 3, 4, 0, 5)
    up = lax.dynamic_index_in_dim(up.reshape(layers, 4, 2, 2, 256), core, 2, False)
    up = take_relative(up, me_x, 1).astype(FULL)

    place = lax.broadcasted_iota(jnp.int32, (width, width), 1)
    block = place >> 6
    far_z = me_z ^ (((block >> 2) & 1) ^ ((block >> 3) * 3))
    far_y = me_y ^ ((block & 1) ^ (((block >> 1) & 1) * 3))
    source = (((far_z >> 1) * 4 + far_y) * 2 + (far_z & 1)) * 64 + (place & 63)
    reorder = source == lax.broadcasted_iota(jnp.int32, (width, width), 0)
    reorder_low = reorder.astype(LOW)
    reorder_full = reorder.astype(FULL)

    def absolute(value):
        return lax.dot_general(
            value, reorder_full, (((1,), (1,)), ((), ())), precision=lax.Precision.HIGHEST,
            preferred_element_type=FULL,
        )

    tokens = 2 * rows
    inputs = times(
        jnp.concatenate(
            [
                stream.reshape(tokens, width), cotangent.reshape(tokens, width),
                gains_abs, shifts_abs,
            ]
        ),
        reorder_low,
    )
    state = inputs[:tokens]
    incoming = inputs[tokens : 2 * tokens]
    gains = inputs[2 * tokens : 2 * tokens + 4].reshape(layers, 2, width)
    shift = inputs[2 * tokens + 4 :].reshape(layers, 4, width)

    marks = segments.reshape(2, 2, 2, 4, rows)
    marks = jnp.where(core == 0, marks, marks[:, :, ::-1])
    marks = marks.transpose(0, 1, 3, 2, 4).reshape(2, 16 * rows)
    marks_t = marks.T
    chips = []
    for i in range(16):
        far_z = me_z ^ (((i >> 2) & 1) ^ ((i >> 3) * 3))
        far_y = me_y ^ ((i & 1) ^ (((i >> 1) & 1) * 3))
        chips.append(((far_z >> 1) * 4 + far_y) * 2 + (far_z & 1))
    order = [relative_x(me_x, r) for r in range(4)] + [core] + chips
    order = jnp.stack(order).astype(jnp.int32)

    saved = []
    for layer in range(layers):
        bias = pair[layer].reshape(2, 4, 1, 128)
        gathered = both(state.astype(LOW))
        qkv = project(order, gathered, attention_w[layer], bias[0], bias[1])
        qkv = trade(qkv.reshape(8, 2 * rows, 384)).reshape(16 * rows, 384)
        mixed, summary = attend(qkv, marks_t, marks)
        mixed = trade(mixed.reshape(8, 2 * rows, 128)).reshape(2, 4, 2 * rows, 128)
        mixed, attended = mix(order, mixed, attention_w[layer][3])
        attended = own_sum(attended) + shift[layer, 2]
        first, unit_one, inv_one = normalize(state + attended, gains[layer, 0], shift[layer, 0])
        gathered_two = both(first.astype(LOW))
        hidden, active, down = feed(order, gathered_two, up[layer], feed_w[layer])
        down = own_sum(down)
        state, unit_two, inv_two = normalize(
            first + down + shift[layer, 3], gains[layer, 1], shift[layer, 1]
        )
        saved.append(
            (gathered, qkv, summary, mixed, unit_one, inv_one, gathered_two, hidden, active,
             unit_two, inv_two)
        )
    result = absolute(state)

    small = [None] * layers
    for layer in reversed(range(layers)):
        (gathered, qkv, summary, mixed, unit_one, inv_one, gathered_two, hidden, active,
         unit_two, inv_two) = saved[layer]
        grad_two, gain_two, shift_two = normalize_back(
            incoming, unit_two, inv_two, gains[layer, 1]
        )
        spread_two = both(grad_two.astype(LOW))
        grad_feed, grad_upbias, grad_first = feed_back(
            order, spread_two, gathered_two, hidden, active, feed_w[layer]
        )
        grad_feed = reduce_first(grad_feed, (0, 2))
        grad_first = grad_two + own_sum(grad_first)
        grad_one, gain_one, shift_one = normalize_back(
            grad_first, unit_one, inv_one, gains[layer, 0]
        )
        spread_one = both(grad_one.astype(LOW))
        grad_mixed = trade(mix_back(order, spread_one, attention_w[layer][3]).reshape(8, 2 * rows, 128))
        grad_mixed = grad_mixed.reshape(16 * rows, 128)
        low_packed, grad_pair = attend_back(qkv, grad_mixed, marks_t, marks, summary)
        grad_pair = grad_pair.reshape(2, 2, 64).sum(1)
        low_packed = trade(low_packed.reshape(8, 2 * rows, 384)).reshape(2, 4, 2 * rows, 384)
        grad_attention, grad_x = project_back(
            order, low_packed, gathered, spread_one, mixed, attention_w[layer],
            PAIRED if layer else APART,
        )
        incoming = grad_one + own_sum(grad_x)
        if layer:
            grad_attention = reduce_first(grad_attention, (0, 2))
            later = reduce_rest(
                [jnp.concatenate(pair, 2) for pair in zip(grad_feed, grad_attention)], (0, 2)
            )
        else:
            tail = reduce_rest(grad_feed, (0, 2))
            grad_attention, later, tail = lax.optimization_barrier((grad_attention, later, tail))
            lead = reduce_rest(reduce_first(grad_attention, range(4)), range(4))
        small[layer] = (
            jnp.stack([gain_one, gain_two]),
            jnp.stack(
                [shift_one, shift_two, jnp.sum(grad_one, axis=0), jnp.sum(grad_two, axis=0)]
            ),
            grad_pair,
            grad_upbias,
        )
    grad_stream = absolute(incoming)

    def own_rows(parts):
        total = jnp.stack(parts, 1)
        total = total.reshape((2, 32) + total.shape[1:])
        keep = lax.dynamic_index_in_dim(total, core, 0, False)
        new = swap(lax.dynamic_index_in_dim(total, 1 - core, 0, False))
        return jnp.stack(
            [jnp.where(core == 0, keep, new), jnp.where(core == 0, new, keep)], 1
        ).astype(FULL)

    tail = own_rows([jnp.concatenate([a, b], 1) for a, b in zip(tail, later)])
    lead = own_rows(lead)
    attention = [lead, tail[..., 1024:].reshape(32, 2, 4, 128)]
    feeds = [tail[..., i * 512 : (i + 1) * 512].reshape(32, 2, 4, 256) for i in range(2)]
    out_qkv = jnp.stack(
        [value[:, :, :3].transpose(0, 2, 1, 3).reshape(32, 3, 256) for value in attention]
    )
    out_o = jnp.stack([value[:, :, 3].reshape(32, 256).T for value in attention])
    out_up = jnp.stack([value[:, :, :2].reshape(32, 1024) for value in feeds])
    out_down = jnp.stack([value[:, :, 2:].reshape(32, 1024).T for value in feeds])

    vec = absolute(
        jnp.concatenate([small[layer][0] for layer in range(layers)]
                        + [small[layer][1] for layer in range(layers)])
    )
    vec = vec.reshape(12, 32, 32).transpose(1, 0, 2).reshape(32, 1, 384)
    vec = jnp.broadcast_to(vec, (32, 4, 384))
    pair = jnp.stack([small[layer][2] for layer in range(layers)])
    head = me_x * 4 + core * 2 + z_lo
    pair = jnp.where((jnp.arange(16) == head)[:, None], pair[:, :, None], 0.0)
    pair = pair.reshape(layers, 2, 4, 4, 32, 2).transpose(4, 2, 0, 1, 3, 5).reshape(32, 4, 32)
    up = take_absolute(jnp.stack([small[layer][3] for layer in range(layers)]), me_x, 1)
    up = jnp.where((jnp.arange(2) == core)[:, None, None], up[:, :, None], 0.0)
    up = up.reshape(layers, 4, 4, 32, 8).transpose(3, 1, 0, 2, 4).reshape(32, 4, 64)
    vec = jnp.concatenate([vec, pair, up, jnp.zeros((32, 4, 32), FULL)], 2).reshape(128, 512)
    vec = jnp.sum(lax.all_to_all(vec, ALL, 0, 0, tiled=True), axis=0)

    return (
        result.reshape(stream.shape),
        grad_stream.reshape(stream.shape),
        out_qkv,
        vec[384:416].reshape(qv_bias.shape),
        out_o,
        vec[:128].reshape(norm_gains.shape),
        vec[128:384].reshape(shifts.shape),
        out_up,
        vec[416:480].reshape(in_bias.shape),
        out_down,
    )


def solution(mesh):
    return jax.shard_map(
        local,
        mesh=mesh,
        in_specs=(
            P("dp", ("ctx", "tensor"), None),
            P("dp", None),
            P(None, ("dp", "ctx"), None, "tensor"),
            P(None, None, "tensor", ("dp", "ctx")),
            P(None, "tensor", ("dp", "ctx")),
            P(None, None, ("dp", "ctx")),
            P(None, None, ("dp", "ctx")),
            P(None, ("dp", "ctx"), "tensor"),
            P(None, "tensor", ("dp", "ctx")),
            P(None, "tensor", ("dp", "ctx")),
            P("dp", ("ctx", "tensor"), None),
        ),
        out_specs=(
            P("dp", ("ctx", "tensor"), None),
            P("dp", ("ctx", "tensor"), None),
            P(None, ("dp", "ctx"), None, "tensor"),
            P(None, None, "tensor", ("dp", "ctx")),
            P(None, "tensor", ("dp", "ctx")),
            P(None, None, ("dp", "ctx")),
            P(None, None, ("dp", "ctx")),
            P(None, ("dp", "ctx"), "tensor"),
            P(None, "tensor", ("dp", "ctx")),
            P(None, "tensor", ("dp", "ctx")),
        ),
        check_vma=False,
    )
```

```python
import functools

import jax
import jax.numpy as jnp
from jax import lax
from jax.experimental import pallas as pl
from jax.experimental.pallas import tpu as pltpu
from jax.sharding import PartitionSpec as P

EPSILON = 1e-12
MASKED = -1000000000.0
ROOT_HALF = 0.7071067811865476
ROOT_TWOPI = 2.5066282746310002
ALL = ("dp", "ctx", "tensor")
LOW = jnp.bfloat16
FULL = jnp.float32

X1, X3, Y1, Y3, Z1, Z3 = ("x", 1), ("x", 3), ("y", 1), ("y", 3), ("z", 1), ("z", 3)
ORDERS = (
    (X1, Y3, X3, Z3, Y1, Z1),
    (Y1, X1, Z3, X3, Z1, Y3),
    (X3, Z1, X1, Y1, Y3, Z3),
    (Z1, X3, Y3, X1, Z3, Y1),
)
GROUPS = [[(zl * 2 + c) * 4 + x for zl in range(2) for x in range(4)] for c in range(2)]


def exchange_perm(axis, mask):
    pairs = []
    for device in range(128):
        dp, ctx, x = device // 16, (device // 4) % 4, device % 4
        at = {"x": x, "y": dp % 4, "z": (dp // 4) * 2 + ctx // 2, "core": ctx % 2}
        at[axis] ^= mask
        other = ((at["z"] // 2) * 4 + at["y"]) * 16
        other += ((at["z"] % 2) * 2 + at["core"]) * 4 + at["x"]
        pairs.append((device, other))
    return pairs


def swap(value, axis="core", mask=1):
    return lax.ppermute(value, ALL, exchange_perm(axis, mask))


def gather_early(parts):
    for phase in range(4):
        got = [swap(value, *ORDERS[k][phase]) for k, value in enumerate(parts)]
        parts = [jnp.concatenate([value, new], 0) for value, new in zip(parts, got)]
    return parts


def gather_late(parts):
    near = [swap(value, *ORDERS[k][4]) for k, value in enumerate(parts)]
    far = [swap(value, *ORDERS[k][5]) for k, value in enumerate(parts)]
    both_far = [swap(value, *ORDERS[k][5]) for k, value in enumerate(near)]
    return [list(four) for four in zip(parts, near, far, both_far)]


def add_low(left, right):
    return (left.astype(FULL) + right.astype(FULL)).astype(LOW)


def reduce_first(pairs, orders):
    parts = [add_low(kept, swap(sent, *ORDERS[k][5])) for k, (kept, sent) in zip(orders, pairs)]
    return reduce_phase(parts, orders, 1)


def reduce_phase(parts, orders, phase):
    half = parts[0].shape[0] // 2
    got = [swap(value[half:], *ORDERS[k][5 - phase]) for k, value in zip(orders, parts)]
    return [add_low(value[:half], new) for value, new in zip(parts, got)]


def reduce_phases(parts, orders, first):
    for phase in range(first, 6):
        parts = reduce_phase(parts, orders, phase)
    return [value[0] for value in parts]


def relative_x(me_x, r):
    return me_x ^ (0, 1, 3, 2)[r]


def take_relative(value, me_x, axis):
    return jnp.concatenate(
        [lax.dynamic_slice_in_dim(value, relative_x(me_x, r), 1, axis) for r in range(4)], axis
    )


def take_absolute(value, me_x, axis):
    parts = []
    for x in range(4):
        off = me_x ^ x
        parts.append(lax.dynamic_slice_in_dim(value, off ^ (off >> 1), 1, axis))
    return jnp.concatenate(parts, axis)


def both(value):
    return jnp.concatenate([value, swap(value)], 0)


def own_sum(value):
    half = value.shape[0] // 2
    value = value.astype(FULL)
    return value[:half] + swap(value[half:].astype(LOW)).astype(FULL)


def normalize(values, gain, shift):
    mean = jnp.mean(values, axis=-1, keepdims=True)
    centred = values - mean
    inverse = lax.rsqrt(jnp.mean(centred * centred, axis=-1, keepdims=True) + EPSILON)
    unit = centred * inverse
    return (unit * gain + shift, unit, inverse)


def normalize_back(incoming, unit, inverse, gain):
    scaled = incoming * gain
    inner = (
        scaled
        - jnp.mean(scaled, axis=-1, keepdims=True)
        - unit * jnp.mean(scaled * unit, axis=-1, keepdims=True)
    )
    return (inverse * inner, jnp.sum(incoming * unit, axis=0), jnp.sum(incoming, axis=0))


def dot(left, right, dims):
    return lax.dot_general(left, right, (dims, ((), ())), preferred_element_type=FULL)


def times(left, right):
    return dot(left, right, ((1,), (0,)))


def times_t(left, right):
    return dot(left, right, ((1,), (1,)))


def t_times(left, right):
    return dot(left, right, ((0,), (0,)))


VMEM_BYTES = 56 * 1024 * 1024


ZY = (Z3, Z1, Y3, Y1)


class Exchanged:
    def __init__(self, k, pieces, columns):
        self.k = k
        self.arrays = [value.reshape((2,) * 4 + value.shape[1:]) for value in pieces]
        axes = ORDERS[k][3::-1]

        def index(r, *_):
            at = {X3: r // 2, X1: r % 2}
            return tuple(at.get(dim, 0) for dim in axes) + (0, 0)

        shape = tuple(1 if dim[0] == "x" else 2 for dim in axes) + (64, columns)
        self.specs = [pl.BlockSpec(shape, index)] * 4

    def load(self, info, refs):
        rows = []
        for i in range(16):
            bits = dict(zip(ZY, (i >> 3, (i >> 2) & 1, (i >> 1) & 1, i & 1)))
            piece = 2 * bits[ORDERS[self.k][5]] + bits[ORDERS[self.k][4]]
            at = tuple(bits.get(dim, 0) for dim in ORDERS[self.k][3::-1])
            rows.append(refs[piece][at])
        return jnp.concatenate(rows, 0)


class Gathered:
    def __init__(self, array, base, columns, step):
        self.arrays = [array]

        def index(r, info):
            return (0, 0, info[r], 0, base + info[4] * step)

        self.specs = [pl.BlockSpec((16, 2, 1, 32, columns), index)]

    def load(self, info, refs):
        (ref,) = refs
        return jnp.concatenate(
            [ref[info[5 + i], half, 0] for i in range(16) for half in range(2)], 0
        )


class Grads:
    def __init__(self, k, width, at):
        self.k, self.width, self.at = k, width, at

    def store(self, refs, value):
        for i in range(16):
            bits = dict(zip(ZY, (i >> 3, (i >> 2) & 1, (i >> 1) & 1, i & 1)))
            place = tuple(bits.get(dim, 0) for dim in ORDERS[self.k][4::-1])
            place += (slice(None), slice(self.at, self.at + value.shape[1]))
            refs[bits[ORDERS[self.k][5]]][place] = value[i * 64 : (i + 1) * 64]


def grad_spec(sink):
    axes = ORDERS[sink.k][4::-1]

    def index(r, *_):
        at = {X3: r // 2, X1: r % 2}
        return tuple(at.get(dim, 0) for dim in axes) + (0, 0)

    shape = tuple(1 if dim[0] == "x" else 2 for dim in axes) + (64, sink.width)
    return [pl.BlockSpec(shape, index)] * 2


def grad_outs(sinks):
    first = [sink for sink in sinks if sink.at == 0]
    specs = [spec for sink in first for spec in grad_spec(sink)]
    shapes = [
        jax.ShapeDtypeStruct((2,) * 5 + (64, sink.width), LOW) for sink in first for _ in range(2)
    ]
    return specs, shapes


def grad_refs(sinks, refs):
    pairs, at = [], -2
    for sink in sinks:
        at += 2 if sink.at == 0 else 0
        pairs.append(refs[at : at + 2])
    return pairs


def take_refs(weights, refs):
    groups = []
    for weight in weights:
        groups.append(refs[: len(weight.arrays)])
        refs = refs[len(weight.arrays) :]
    return groups, refs


APART = [Grads(k, 128, 0) for k in range(4)]
FEED = [Grads(k, 256, 0) for k in range(4)]


def halves(refs):
    pairs = zip(refs[::2], refs[1::2])
    return [tuple(v.reshape((32,) + v.shape[-2:]) for v in pair) for pair in pairs]


def joined(weights, field):
    return [entry for weight in weights for entry in getattr(weight, field)]


def call(body, grid, in_specs, out_specs, out_shape, scratch, args, flops, scalars=()):
    size = sum(value.size * value.dtype.itemsize for value in args)
    size += sum(value.size * value.dtype.itemsize for value in out_shape)
    return pl.pallas_call(
        body,
        grid_spec=pltpu.PrefetchScalarGridSpec(
            num_scalar_prefetch=len(scalars),
            grid=grid,
            in_specs=in_specs,
            out_specs=out_specs,
            scratch_shapes=scratch,
        ),
        out_shape=out_shape,
        compiler_params=pltpu.CompilerParams(vmem_limit_bytes=VMEM_BYTES),
        cost_estimate=pl.CostEstimate(flops=flops, bytes_accessed=size, transcendentals=0),
    )(*scalars, *args)


def whole(shape):
    return pl.BlockSpec(shape, lambda *_: (0,) * len(shape))


def pick(value):
    return pl.BlockSpec(
        (1,) + value.shape[1:], lambda r, *_: (r,) + (0,) * (len(value.shape) - 1)
    )


def cross(left, right):
    lane = lax.broadcasted_iota(jnp.int32, left.shape, 1) < 64
    turned_left, turned_right = pltpu.roll(left, 64, 1), pltpu.roll(right, 64, 1)
    return jnp.where(lane, left, turned_right), jnp.where(lane, turned_left, right)


def split_rows(value):
    n = value.shape[0] // 4
    return (
        jnp.concatenate([value[:n], value[2 * n : 3 * n]], 0),
        jnp.concatenate([value[n : 2 * n], value[3 * n :]], 0),
    )


def join_rows(left, right):
    n = left.shape[0] // 2
    return jnp.concatenate([left[:n], right[:n], left[n:], right[n:]], 0)


def accumulate(ref, r, value):
    @pl.when(r == 0)
    def _():
        ref[...] = value

    @pl.when(r > 0)
    def _():
        ref[...] += value


def project_body(weights, info, x, *refs):
    groups, (bias_q, bias_v, out) = take_refs(weights, refs)
    q, k, v = [times(x[...], w.load(info, group)) for w, group in zip(weights, groups)]
    for i, value in enumerate((q + bias_q[0], k, v + bias_v[0])):
        for j, head in enumerate(cross(*split_rows(value))):
            out[j, 0, :, i * 128 : (i + 1) * 128] = head.astype(LOW)


def heads_spec(rows, lanes):
    return pl.BlockSpec((2, 1, rows, lanes), lambda r, order: (0, order[r], 0, 0))


def project(order, x, weights, bias_q, bias_v):
    m = x.shape[0]
    weights = weights[:3]
    (out,) = call(
        functools.partial(project_body, weights), (4,),
        [whole(x.shape)] + joined(weights, "specs") + [pick(bias_q), pick(bias_v)],
        [heads_spec(m // 2, 384)],
        [jax.ShapeDtypeStruct((2, 4, m // 2, 384), LOW)], [],
        [x] + joined(weights, "arrays") + [bias_q, bias_v], 2 * m * 1024 * 1536, (order,),
    )
    return out


def tokens_of(ref, lanes):
    left, right = cross(ref[0, 0, :, lanes].astype(FULL), ref[1, 0, :, lanes].astype(FULL))
    return join_rows(left, right).astype(LOW)


def mix_body(weight, info, heads, *refs):
    (group,), (mixed_out, out) = take_refs([weight], refs)
    mixed = tokens_of(heads, slice(0, 128))
    mixed_out[0] = mixed
    accumulate(out, pl.program_id(0), times_t(mixed, weight.load(info, group)))


def mix(order, heads, weight):
    m = heads.shape[2] * 2
    return call(
        functools.partial(mix_body, weight), (4,),
        [heads_spec(m // 2, 128)] + weight.specs,
        [pl.BlockSpec((1, m, 128), lambda r, *_: (r, 0, 0)), whole((m, 1024))],
        [jax.ShapeDtypeStruct((4, m, 128), LOW), jax.ShapeDtypeStruct((m, 1024), FULL)], [],
        [heads] + weight.arrays, 2 * m * 1024 * 512, (order,),
    )


def mix_back_body(weight, info, x, *refs):
    (group,), (out,) = take_refs([weight], refs)
    value = times(x[...], weight.load(info, group))
    for j, head in enumerate(cross(*split_rows(value))):
        out[j, 0] = head.astype(LOW)


def mix_back(order, x, weight):
    m = x.shape[0]
    (out,) = call(
        functools.partial(mix_back_body, weight), (4,),
        [whole(x.shape)] + weight.specs,
        [heads_spec(m // 2, 128)],
        [jax.ShapeDtypeStruct((2, 4, m // 2, 128), LOW)], [],
        [x] + weight.arrays, 2 * m * 1024 * 512, (order,),
    )
    return out


def project_back_body(weights, sinks, info, heads, x, spread, mixed, *refs):
    groups, refs = take_refs(weights, refs)
    pairs, out = grad_refs(sinks, refs[:-1]), refs[-1]
    terms = None
    for i in range(3):
        low = tokens_of(heads, slice(i * 128, (i + 1) * 128))
        sinks[i].store(pairs[i], t_times(x[...], low).astype(LOW))
        term = times_t(low, weights[i].load(info, groups[i]))
        terms = term if terms is None else terms + term
    sinks[3].store(pairs[3], t_times(spread[...], mixed[0]).astype(LOW))
    accumulate(out, pl.program_id(0), terms)


def project_back(order, heads, x, spread, mixed, weights, sinks):
    m = x.shape[0]
    weights = weights[:3]
    specs, shapes = grad_outs(sinks)
    *grads, out = call(
        functools.partial(project_back_body, weights, sinks), (4,),
        [heads_spec(m // 2, 384), whole(x.shape), whole(x.shape), pick(mixed)]
        + joined(weights, "specs"),
        specs + [whole((m, 1024))],
        shapes + [jax.ShapeDtypeStruct((m, 1024), FULL)], [],
        [heads, x, spread, mixed] + joined(weights, "arrays"), 2 * m * 1024 * 3584, (order,),
    )
    return halves(grads), out


def feed_body(weights, info, x, bias, *refs):
    groups, (hidden_out, active_out, out) = take_refs(weights, refs)
    total = None
    for j in range(2):
        hidden = times(x[...], weights[j].load(info, groups[j])) + bias[0, j : j + 1]
        hidden_out[0, j] = hidden
        active = (hidden * (0.5 * (1.0 + lax.erf(hidden * ROOT_HALF)))).astype(LOW)
        active_out[0, j] = active
        term = times_t(active, weights[2 + j].load(info, groups[2 + j]))
        total = term if total is None else total + term
    accumulate(out, pl.program_id(0), total)


def feed(order, x, bias, weights):
    m = x.shape[0]
    block = pl.BlockSpec((1, 2, m, 256), lambda r, *_: (r, 0, 0, 0))
    return call(
        functools.partial(feed_body, weights), (4,),
        [whole(x.shape), pick(bias)] + joined(weights, "specs"),
        [block, block, whole((m, 1024))],
        [
            jax.ShapeDtypeStruct((4, 2, m, 256), FULL), jax.ShapeDtypeStruct((4, 2, m, 256), LOW),
            jax.ShapeDtypeStruct((m, 1024), FULL),
        ], [],
        [x, bias] + joined(weights, "arrays"), 4 * m * 1024 * 2048, (order,),
    )


def feed_back_body(weights, info, spread, x, hidden, active, *refs):
    groups, refs = take_refs(weights, refs)
    pairs, (grad_bias, out) = grad_refs(FEED, refs[:-2]), refs[-2:]
    total = None
    for j in range(2):
        value = hidden[0, j]
        slope = 0.5 * (1.0 + lax.erf(value * ROOT_HALF))
        slope += value * jnp.exp(-0.5 * value * value) * (1.0 / ROOT_TWOPI)
        grad = times(spread[...], weights[2 + j].load(info, groups[2 + j])) * slope
        grad_bias[0, j : j + 1] = jnp.sum(grad, axis=0, keepdims=True)
        low = grad.astype(LOW)
        FEED[2 + j].store(pairs[2 + j], t_times(spread[...], active[0, j]).astype(LOW))
        FEED[j].store(pairs[j], t_times(x[...], low).astype(LOW))
        term = times_t(low, weights[j].load(info, groups[j]))
        total = term if total is None else total + term
    accumulate(out, pl.program_id(0), total)


def feed_back(order, spread, x, hidden, active, weights):
    m = x.shape[0]
    specs, shapes = grad_outs(FEED)
    *grads, grad_bias, out = call(
        functools.partial(feed_back_body, weights), (4,),
        [whole(x.shape), whole(x.shape), pick(hidden), pick(active)] + joined(weights, "specs"),
        specs + [pl.BlockSpec((1, 2, 256), lambda r, *_: (r, 0, 0)), whole((m, 1024))],
        shapes
        + [jax.ShapeDtypeStruct((4, 2, 256), FULL), jax.ShapeDtypeStruct((m, 1024), FULL)], [],
        [spread, x, hidden, active] + joined(weights, "arrays"), 8 * m * 1024 * 2048, (order,),
    )
    return halves(grads), grad_bias, out


def one_row(value, s):
    lane = lax.broadcasted_iota(jnp.int32, value.shape, 1) // 64 == s
    return jnp.where(lane, value, jnp.zeros_like(value))


def scores_of(keys, query, mark_keys, mark_query, s):
    scores = times_t(keys, one_row(query, s) * LOW(0.125))
    same = mark_keys[:, s : s + 1] == mark_query[s : s + 1, :]
    return jnp.where(same, scores, MASKED)


def attend_body(query, keys, values, mark_keys, mark_query, out, summary):
    turned = values[...].astype(FULL).T.astype(LOW)
    results = []
    for s in range(2):
        scores = scores_of(keys[...], query[...], mark_keys, mark_query, s)
        top = jnp.max(scores, axis=0, keepdims=True)
        weights = jnp.exp(scores - top)
        total = jnp.sum(weights, axis=0, keepdims=True)
        probs = (weights * (1.0 / total)).astype(LOW)
        results.append(times(turned[s * 64 : (s + 1) * 64], probs))
        summary[s : s + 1] = top + jnp.log(total)
    out[...] = jnp.concatenate(results, 0).T.astype(LOW)


def attend(qkv, mark_keys, mark_query):
    n = qkv.shape[0]
    q = 384

    return call(
        attend_body, (n // q,),
        [
            pl.BlockSpec((q, 128), lambda i: (i, 0)), pl.BlockSpec((n, 128), lambda i: (0, 1)),
            pl.BlockSpec((n, 128), lambda i: (0, 2)), whole((n, 2)),
            pl.BlockSpec((2, q), lambda i: (0, i)),
        ],
        [pl.BlockSpec((q, 128), lambda i: (i, 0)), pl.BlockSpec((2, q), lambda i: (0, i))],
        [jax.ShapeDtypeStruct((n, 128), LOW), jax.ShapeDtypeStruct((2, n), FULL)], [],
        (qkv, qkv, qkv, mark_keys, mark_query), 8 * n * n * 128,
    )


def attend_back_body(
    query, keys, values, grad_mixed, mark_keys, mark_query, summary, out, sums, sum_k, sum_v, sum_q
):
    i = pl.program_id(0)
    n, q = keys.shape[0], query.shape[0]
    turned = keys[...].astype(FULL).T.astype(LOW)
    lane = lax.broadcasted_iota(jnp.int32, (n, 128), 1) < 64
    grads_q, grads_k, grads_v = [], [], []
    for s in range(2):
        scores = scores_of(keys[...], query[...], mark_keys, mark_query, s)
        probs = jnp.exp(scores - summary[s : s + 1])
        grad_probs = times_t(values[...], one_row(grad_mixed[...], s))
        inner = jnp.sum(probs * grad_probs, axis=0, keepdims=True)
        low_probs = probs.astype(LOW)
        grad_scores = (probs * (grad_probs - inner)).astype(LOW)
        grads_v.append(times(low_probs, grad_mixed[...]))
        grads_k.append(times(grad_scores, query[...]))
        grads_q.append(times(turned[s * 64 : (s + 1) * 64], grad_scores))
    accumulate(sum_k, i, jnp.where(lane, grads_k[0], grads_k[1]) * 0.125)
    accumulate(sum_v, i, jnp.where(lane, grads_v[0], grads_v[1]))
    grad_q = jnp.concatenate(grads_q, 0).T * 0.125
    accumulate(sum_q, i, jnp.sum(grad_q, axis=0, keepdims=True))
    out[pl.ds(pl.multiple_of(i * q, q), q), :128] = grad_q.astype(LOW)

    @pl.when(i == pl.num_programs(0) - 1)
    def _():
        out[:, 128:256] = sum_k[...].astype(LOW)
        out[:, 256:] = sum_v[...].astype(LOW)
        sums[0:1] = sum_q[...]
        sums[1:2] = jnp.sum(sum_v[...], axis=0, keepdims=True)


def attend_back(qkv, grad_mixed, mark_keys, mark_query, summary):
    n = qkv.shape[0]
    q = 384
    return call(
        attend_back_body, (n // q,),
        [
            pl.BlockSpec((q, 128), lambda i: (i, 0)), pl.BlockSpec((n, 128), lambda i: (0, 1)),
            pl.BlockSpec((n, 128), lambda i: (0, 2)), pl.BlockSpec((q, 128), lambda i: (i, 0)),
            whole((n, 2)), pl.BlockSpec((2, q), lambda i: (0, i)),
            pl.BlockSpec((2, q), lambda i: (0, i)),
        ],
        [whole((n, 384)), whole((2, 128))],
        [jax.ShapeDtypeStruct((n, 384), LOW), jax.ShapeDtypeStruct((2, 128), FULL)],
        [pltpu.VMEM((n, 128), FULL), pltpu.VMEM((n, 128), FULL), pltpu.VMEM((1, 128), FULL)],
        (qkv, qkv, qkv, grad_mixed, mark_keys, mark_query, summary), 20 * n * n * 128,
    )


def trade(value):
    return lax.all_to_all(
        value, ("ctx", "tensor"), 0, 0, axis_index_groups=GROUPS, tiled=True
    )


def local(
    stream, segments, w_qkv, qv_bias, w_out, norm_gains, shifts, w_in, in_bias, w_back, cotangent
):
    layers = w_qkv.shape[0]
    dp, ctx, me_x = lax.axis_index("dp"), lax.axis_index("ctx"), lax.axis_index("tensor")
    core, z_lo = ctx & 1, ctx >> 1
    me_y, me_z = dp & 3, (dp >> 2) * 2 + z_lo
    rows = stream.shape[1]
    width = stream.shape[2]

    def both_rows(columns):
        axis = columns.ndim - 2
        keep = lax.dynamic_index_in_dim(columns, core, axis, False)
        new = swap(lax.dynamic_index_in_dim(columns, 1 - core, axis, False))
        return jnp.where(
            core == 0, jnp.concatenate([keep, new], -2), jnp.concatenate([new, keep], -2)
        )

    lead = both_rows(
        jnp.concatenate(
            [
                jnp.concatenate(
                    [
                        w_qkv[layer].reshape(32, 3, 2, 128).transpose(0, 2, 1, 3).reshape(
                            32, 2, 384
                        ),
                        w_out[layer].T.reshape(32, 2, 128),
                    ],
                    2,
                )
                for layer in range(2)
            ],
            2,
        )
    ).reshape(1, 64, 2, 4, 128)
    lead = gather_early([lead[:, :, :, k].reshape(1, 64, 256) for k in range(4)])
    later = jnp.concatenate([w_in[0], w_back[0].T, w_in[1], w_back[1].T], 1)
    later = lax.all_gather(later, "tensor", axis=0, tiled=True)
    lead, norm_gains, later = lax.optimization_barrier((lead, norm_gains, later))
    lead_one = [value[:, :, 128:] for value in lead]
    lead = gather_late([value[:, :, :128] for value in lead])
    lead, lead_one = lax.optimization_barrier((lead, lead_one))
    near_one = [swap(value, *ORDERS[k][4]) for k, value in enumerate(lead_one)]
    far_one = [swap(value, *ORDERS[k][5]) for k, value in enumerate(lead_one)]

    def everywhere(value):
        value = lax.all_gather(value, ("dp", "ctx"), axis=0, tiled=True)
        return value.reshape(16, 2, 4, 32, value.shape[1])

    feed_zero = everywhere(later[:, :2048])
    feed_one = everywhere(later[:, 2048:])
    attention_w = [[Exchanged(k, lead[k], 128) for k in range(4)]]
    feed_w = [
        [Gathered(value, base, 256, 2) for base in (0, 1, 4, 5)] for value in (feed_zero, feed_one)
    ]

    vectors = jnp.concatenate(
        [norm_gains.reshape(-1), shifts.reshape(-1), qv_bias.reshape(-1), in_bias.reshape(-1)]
    )
    vectors = jnp.pad(vectors, (0, 512 - vectors.shape[0]))
    spread = lax.all_to_all(jnp.broadcast_to(vectors, (128, 512)), ALL, 0, 0, tiled=True)
    spread = spread.reshape(32, 4, 512)
    gains_abs = spread[:, 0, 0:128].reshape(32, 4, 32).transpose(1, 0, 2).reshape(4, width)
    shifts_abs = spread[:, 0, 128:384].reshape(32, 8, 32).transpose(1, 0, 2).reshape(8, width)
    pair = spread[:, :, 384:416].reshape(32, 4, layers, 2, 2, 2, 2).transpose(2, 3, 1, 4, 5, 0, 6)
    pair = lax.dynamic_index_in_dim(pair.reshape(layers, 2, 4, 2, 2, 64), core, 3, False)
    pair = take_relative(pair, me_x, 2).astype(FULL)
    up = spread[:, :, 416:480].reshape(32, 4, layers, 2, 2, 8).transpose(2, 1, 3, 4, 0, 5)
    up = lax.dynamic_index_in_dim(up.reshape(layers, 4, 2, 2, 256), core, 2, False)
    up = take_relative(up, me_x, 1).astype(FULL)

    place = lax.broadcasted_iota(jnp.int32, (width, width), 1)
    block = place >> 6
    far_z = me_z ^ (((block >> 2) & 1) ^ ((block >> 3) * 3))
    far_y = me_y ^ ((block & 1) ^ (((block >> 1) & 1) * 3))
    source = (((far_z >> 1) * 4 + far_y) * 2 + (far_z & 1)) * 64 + (place & 63)
    reorder = source == lax.broadcasted_iota(jnp.int32, (width, width), 0)
    reorder_low = reorder.astype(LOW)
    reorder_full = reorder.astype(FULL)

    def absolute(value):
        return lax.dot_general(
            value, reorder_full, (((1,), (1,)), ((), ())), precision=lax.Precision.HIGHEST,
            preferred_element_type=FULL,
        )

    tokens = 2 * rows
    inputs = times(
        jnp.concatenate(
            [
                stream.reshape(tokens, width), cotangent.reshape(tokens, width),
                gains_abs, shifts_abs,
            ]
        ),
        reorder_low,
    )
    state = inputs[:tokens]
    incoming = inputs[tokens : 2 * tokens]
    gains = inputs[2 * tokens : 2 * tokens + 4].reshape(layers, 2, width)
    shift = inputs[2 * tokens + 4 :].reshape(layers, 4, width)

    marks = segments.reshape(2, 2, 2, 4, rows)
    marks = jnp.where(core == 0, marks, marks[:, :, ::-1])
    marks = marks.transpose(0, 1, 3, 2, 4).reshape(2, 16 * rows)
    marks_t = marks.T
    chips = []
    for i in range(16):
        far_z = me_z ^ (((i >> 2) & 1) ^ ((i >> 3) * 3))
        far_y = me_y ^ ((i & 1) ^ (((i >> 1) & 1) * 3))
        chips.append(((far_z >> 1) * 4 + far_y) * 2 + (far_z & 1))
    order = [relative_x(me_x, r) for r in range(4)] + [core] + chips
    order = jnp.stack(order).astype(jnp.int32)

    saved = []
    for layer in range(layers):
        bias = pair[layer].reshape(2, 4, 1, 128)
        gathered = both(state.astype(LOW))
        qkv = project(order, gathered, attention_w[layer], bias[0], bias[1])
        qkv = trade(qkv.reshape(8, 2 * rows, 384)).reshape(16 * rows, 384)
        if layer == 0:
            qkv, near_one, far_one = lax.optimization_barrier((qkv, near_one, far_one))
            last_one = [swap(value, *ORDERS[k][5]) for k, value in enumerate(near_one)]
        mixed, summary = attend(qkv, marks_t, marks)
        mixed = trade(mixed.reshape(8, 2 * rows, 128)).reshape(2, 4, 2 * rows, 128)
        if layer == 0:
            mixed, last_one = lax.optimization_barrier((mixed, last_one))
            pieces = zip(lead_one, near_one, far_one, last_one)
            attention_w.append([Exchanged(k, four, 128) for k, four in enumerate(pieces)])
        mixed, attended = mix(order, mixed, attention_w[layer][3])
        attended = own_sum(attended) + shift[layer, 2]
        first, unit_one, inv_one = normalize(state + attended, gains[layer, 0], shift[layer, 0])
        gathered_two = both(first.astype(LOW))
        hidden, active, down = feed(order, gathered_two, up[layer], feed_w[layer])
        down = own_sum(down)
        state, unit_two, inv_two = normalize(
            first + down + shift[layer, 3], gains[layer, 1], shift[layer, 1]
        )
        saved.append(
            (gathered, qkv, summary, mixed, unit_one, inv_one, gathered_two, hidden, active,
             unit_two, inv_two)
        )
    result = absolute(state)

    small = [None] * layers
    for layer in reversed(range(layers)):
        (gathered, qkv, summary, mixed, unit_one, inv_one, gathered_two, hidden, active,
         unit_two, inv_two) = saved[layer]
        grad_two, gain_two, shift_two = normalize_back(
            incoming, unit_two, inv_two, gains[layer, 1]
        )
        spread_two = both(grad_two.astype(LOW))
        grad_feed, grad_upbias, grad_first = feed_back(
            order, spread_two, gathered_two, hidden, active, feed_w[layer]
        )
        grad_feed = reduce_first(grad_feed, range(4))
        grad_first = grad_two + own_sum(grad_first)
        grad_one, gain_one, shift_one = normalize_back(
            grad_first, unit_one, inv_one, gains[layer, 0]
        )
        spread_one = both(grad_one.astype(LOW))
        if layer == 0:
            spread_one, later = lax.optimization_barrier((spread_one, later))
        grad_mixed = trade(mix_back(order, spread_one, attention_w[layer][3]).reshape(8, 2 * rows, 128))
        grad_mixed = grad_mixed.reshape(16 * rows, 128)
        if layer == 0:
            grad_mixed, grad_feed = lax.optimization_barrier((grad_mixed, grad_feed))
            tail = [jnp.concatenate([a, b], 2) for a, b in zip(grad_feed, later)]
            tail = reduce_phase(reduce_phase(tail, range(4), 2), range(4), 3)
        low_packed, grad_pair = attend_back(qkv, grad_mixed, marks_t, marks, summary)
        grad_pair = grad_pair.reshape(2, 2, 64).sum(1)
        low_packed = trade(low_packed.reshape(8, 2 * rows, 384)).reshape(2, 4, 2 * rows, 384)
        if layer:
            low_packed, grad_feed = lax.optimization_barrier((low_packed, grad_feed))
        else:
            low_packed, tail = lax.optimization_barrier((low_packed, tail))
        grad_attention, grad_x = project_back(
            order, low_packed, gathered, spread_one, mixed, attention_w[layer],
            APART,
        )
        incoming = grad_one + own_sum(grad_x)
        if layer:
            grad_attention = reduce_first(grad_attention, range(4))
            later = [jnp.concatenate(pair, 2) for pair in zip(grad_feed, grad_attention)]
        else:
            lead = reduce_first(grad_attention, range(4))
            lead = reduce_phase(reduce_phase(lead, range(4), 2), range(4), 3)
            tail = [jnp.concatenate(pair, 2) for pair in zip(tail, lead)]
            tail = reduce_phases(tail, range(4), 4)
        small[layer] = (
            jnp.stack([gain_one, gain_two]),
            jnp.stack(
                [shift_one, shift_two, jnp.sum(grad_one, axis=0), jnp.sum(grad_two, axis=0)]
            ),
            grad_pair,
            grad_upbias,
        )
    grad_stream = absolute(incoming)

    def own_rows(parts):
        total = jnp.stack(parts, 1)
        total = total.reshape((2, 32) + total.shape[1:])
        keep = lax.dynamic_index_in_dim(total, core, 0, False)
        new = swap(lax.dynamic_index_in_dim(total, 1 - core, 0, False))
        return jnp.stack(
            [jnp.where(core == 0, keep, new), jnp.where(core == 0, new, keep)], 1
        ).astype(FULL)

    tail = own_rows(tail)
    attention = [tail[..., 640:], tail[..., 512:640]]
    feeds = [tail[..., :256], tail[..., 256:512]]
    out_qkv = jnp.stack(
        [value[:, :, :3].transpose(0, 2, 1, 3).reshape(32, 3, 256) for value in attention]
    )
    out_o = jnp.stack([value[:, :, 3].reshape(32, 256).T for value in attention])
    out_up = jnp.stack([value[:, :, :2].reshape(32, 1024) for value in feeds])
    out_down = jnp.stack([value[:, :, 2:].reshape(32, 1024).T for value in feeds])

    vec = absolute(
        jnp.concatenate([small[layer][0] for layer in range(layers)]
                        + [small[layer][1] for layer in range(layers)])
    )
    vec = vec.reshape(12, 32, 32).transpose(1, 0, 2).reshape(32, 1, 384)
    vec = jnp.broadcast_to(vec, (32, 4, 384))
    pair = jnp.stack([small[layer][2] for layer in range(layers)])
    head = me_x * 4 + core * 2 + z_lo
    pair = jnp.where((jnp.arange(16) == head)[:, None], pair[:, :, None], 0.0)
    pair = pair.reshape(layers, 2, 4, 4, 32, 2).transpose(4, 2, 0, 1, 3, 5).reshape(32, 4, 32)
    up = take_absolute(jnp.stack([small[layer][3] for layer in range(layers)]), me_x, 1)
    up = jnp.where((jnp.arange(2) == core)[:, None, None], up[:, :, None], 0.0)
    up = up.reshape(layers, 4, 4, 32, 8).transpose(3, 1, 0, 2, 4).reshape(32, 4, 64)
    vec = jnp.concatenate([vec, pair, up, jnp.zeros((32, 4, 32), FULL)], 2).reshape(128, 512)
    vec = jnp.sum(lax.all_to_all(vec, ALL, 0, 0, tiled=True), axis=0)

    return (
        result.reshape(stream.shape),
        grad_stream.reshape(stream.shape),
        out_qkv,
        vec[384:416].reshape(qv_bias.shape),
        out_o,
        vec[:128].reshape(norm_gains.shape),
        vec[128:384].reshape(shifts.shape),
        out_up,
        vec[416:480].reshape(in_bias.shape),
        out_down,
    )


def solution(mesh):
    return jax.shard_map(
        local,
        mesh=mesh,
        in_specs=(
            P("dp", ("ctx", "tensor"), None),
            P("dp", None),
            P(None, ("dp", "ctx"), None, "tensor"),
            P(None, None, "tensor", ("dp", "ctx")),
            P(None, "tensor", ("dp", "ctx")),
            P(None, None, ("dp", "ctx")),
            P(None, None, ("dp", "ctx")),
            P(None, ("dp", "ctx"), "tensor"),
            P(None, "tensor", ("dp", "ctx")),
            P(None, "tensor", ("dp", "ctx")),
            P("dp", ("ctx", "tensor"), None),
        ),
        out_specs=(
            P("dp", ("ctx", "tensor"), None),
            P("dp", ("ctx", "tensor"), None),
            P(None, ("dp", "ctx"), None, "tensor"),
            P(None, None, "tensor", ("dp", "ctx")),
            P(None, "tensor", ("dp", "ctx")),
            P(None, None, ("dp", "ctx")),
            P(None, None, ("dp", "ctx")),
            P(None, ("dp", "ctx"), "tensor"),
            P(None, "tensor", ("dp", "ctx")),
            P(None, "tensor", ("dp", "ctx")),
        ),
        check_vma=False,
    )
```

```python
import functools

import jax
import jax.numpy as jnp
from jax import lax
from jax.experimental import pallas as pl
from jax.experimental.pallas import tpu as pltpu
from jax.sharding import PartitionSpec as P

EPSILON = 1e-12
MASKED = -1000000000.0
ROOT_HALF = 0.7071067811865476
ROOT_TWOPI = 2.5066282746310002
ALL = ("dp", "ctx", "tensor")
LOW = jnp.bfloat16
FULL = jnp.float32

X1, X3, Y1, Y3, Z1, Z3 = ("x", 1), ("x", 3), ("y", 1), ("y", 3), ("z", 1), ("z", 3)
ORDERS = (
    (X1, Y3, X3, Z3, Y1, Z1),
    (Y1, X1, Z3, X3, Z1, Y3),
    (X3, Z1, X1, Y1, Y3, Z3),
    (Z1, X3, Y3, X1, Z3, Y1),
)
GROUPS = [[(zl * 2 + c) * 4 + x for zl in range(2) for x in range(4)] for c in range(2)]


def exchange_perm(axis, mask):
    pairs = []
    for device in range(128):
        dp, ctx, x = device // 16, (device // 4) % 4, device % 4
        at = {"x": x, "y": dp % 4, "z": (dp // 4) * 2 + ctx // 2, "core": ctx % 2}
        at[axis] ^= mask
        other = ((at["z"] // 2) * 4 + at["y"]) * 16
        other += ((at["z"] % 2) * 2 + at["core"]) * 4 + at["x"]
        pairs.append((device, other))
    return pairs


def swap(value, axis="core", mask=1):
    return lax.ppermute(value, ALL, exchange_perm(axis, mask))


def gather_early(parts):
    for phase in range(4):
        got = [swap(value, *ORDERS[k][phase]) for k, value in enumerate(parts)]
        parts = [jnp.concatenate([value, new], 0) for value, new in zip(parts, got)]
    return parts


def gather_late(parts):
    near = [swap(value, *ORDERS[k][4]) for k, value in enumerate(parts)]
    far = [swap(value, *ORDERS[k][5]) for k, value in enumerate(parts)]
    both_far = [swap(value, *ORDERS[k][5]) for k, value in enumerate(near)]
    return [list(four) for four in zip(parts, near, far, both_far)]


def add_low(left, right):
    return (left.astype(FULL) + right.astype(FULL)).astype(LOW)


def reduce_first(pairs, orders):
    return [add_low(kept, swap(sent, *ORDERS[k][5])) for k, (kept, sent) in zip(orders, pairs)]


def reduce_phase(parts, orders, phase):
    half = parts[0].shape[0] // 2
    got = [swap(value[half:], *ORDERS[k][5 - phase]) for k, value in zip(orders, parts)]
    return [add_low(value[:half], new) for value, new in zip(parts, got)]


def reduce_phases(parts, orders, first):
    for phase in range(first, 6):
        parts = reduce_phase(parts, orders, phase)
    return [value[0] for value in parts]


def relative_x(me_x, r):
    return me_x ^ (0, 1, 3, 2)[r]


def take_relative(value, me_x, axis):
    return jnp.concatenate(
        [lax.dynamic_slice_in_dim(value, relative_x(me_x, r), 1, axis) for r in range(4)], axis
    )


def take_absolute(value, me_x, axis):
    parts = []
    for x in range(4):
        off = me_x ^ x
        parts.append(lax.dynamic_slice_in_dim(value, off ^ (off >> 1), 1, axis))
    return jnp.concatenate(parts, axis)


def both(value):
    return jnp.concatenate([value, swap(value)], 0)


def own_sum(value):
    half = value.shape[0] // 2
    value = value.astype(FULL)
    return value[:half] + swap(value[half:].astype(LOW)).astype(FULL)


def normalize(values, gain, shift):
    mean = jnp.mean(values, axis=-1, keepdims=True)
    centred = values - mean
    inverse = lax.rsqrt(jnp.mean(centred * centred, axis=-1, keepdims=True) + EPSILON)
    unit = centred * inverse
    return (unit * gain + shift, unit, inverse)


def normalize_back(incoming, unit, inverse, gain):
    scaled = incoming * gain
    inner = (
        scaled
        - jnp.mean(scaled, axis=-1, keepdims=True)
        - unit * jnp.mean(scaled * unit, axis=-1, keepdims=True)
    )
    return (inverse * inner, jnp.sum(incoming * unit, axis=0), jnp.sum(incoming, axis=0))


def dot(left, right, dims):
    return lax.dot_general(left, right, (dims, ((), ())), preferred_element_type=FULL)


def times(left, right):
    return dot(left, right, ((1,), (0,)))


def times_t(left, right):
    return dot(left, right, ((1,), (1,)))


def t_times(left, right):
    return dot(left, right, ((0,), (0,)))


VMEM_BYTES = 56 * 1024 * 1024


ZY = (Z3, Z1, Y3, Y1)


class Exchanged:
    def __init__(self, k, pieces, columns):
        self.k = k
        self.arrays = [value.reshape((2,) * 4 + value.shape[1:]) for value in pieces]
        axes = ORDERS[k][3::-1]

        def index(r, *_):
            at = {X3: r // 2, X1: r % 2}
            return tuple(at.get(dim, 0) for dim in axes) + (0, 0)

        shape = tuple(1 if dim[0] == "x" else 2 for dim in axes) + (64, columns)
        self.specs = [pl.BlockSpec(shape, index)] * 4

    def load(self, info, refs):
        rows = []
        for i in range(16):
            bits = dict(zip(ZY, (i >> 3, (i >> 2) & 1, (i >> 1) & 1, i & 1)))
            piece = 2 * bits[ORDERS[self.k][5]] + bits[ORDERS[self.k][4]]
            at = tuple(bits.get(dim, 0) for dim in ORDERS[self.k][3::-1])
            rows.append(refs[piece][at])
        return jnp.concatenate(rows, 0)


class Gathered:
    def __init__(self, array, base, columns, step):
        self.arrays = [array]

        def index(r, info):
            return (0, 0, info[r], 0, base + info[4] * step)

        self.specs = [pl.BlockSpec((16, 2, 1, 32, columns), index)]

    def load(self, info, refs):
        (ref,) = refs
        return jnp.concatenate(
            [ref[info[5 + i], half, 0] for i in range(16) for half in range(2)], 0
        )


class Grads:
    def __init__(self, k, width, at):
        self.k, self.width, self.at = k, width, at

    def store(self, refs, value):
        for i in range(16):
            bits = dict(zip(ZY, (i >> 3, (i >> 2) & 1, (i >> 1) & 1, i & 1)))
            place = tuple(bits.get(dim, 0) for dim in ORDERS[self.k][4::-1])
            place += (slice(None), slice(self.at, self.at + value.shape[1]))
            refs[bits[ORDERS[self.k][5]]][place] = value[i * 64 : (i + 1) * 64]


def grad_spec(sink):
    axes = ORDERS[sink.k][4::-1]

    def index(r, *_):
        at = {X3: r // 2, X1: r % 2}
        return tuple(at.get(dim, 0) for dim in axes) + (0, 0)

    shape = tuple(1 if dim[0] == "x" else 2 for dim in axes) + (64, sink.width)
    return [pl.BlockSpec(shape, index)] * 2


def grad_outs(sinks):
    first = [sink for sink in sinks if sink.at == 0]
    specs = [spec for sink in first for spec in grad_spec(sink)]
    shapes = [
        jax.ShapeDtypeStruct((2,) * 5 + (64, sink.width), LOW) for sink in first for _ in range(2)
    ]
    return specs, shapes


def grad_refs(sinks, refs):
    pairs, at = [], -2
    for sink in sinks:
        at += 2 if sink.at == 0 else 0
        pairs.append(refs[at : at + 2])
    return pairs


def take_refs(weights, refs):
    groups = []
    for weight in weights:
        groups.append(refs[: len(weight.arrays)])
        refs = refs[len(weight.arrays) :]
    return groups, refs


APART = [Grads(k, 128, 0) for k in range(4)]
FEED = [Grads(k, 256, 0) for k in range(4)]


def halves(refs):
    pairs = zip(refs[::2], refs[1::2])
    return [tuple(v.reshape((32,) + v.shape[-2:]) for v in pair) for pair in pairs]


def joined(weights, field):
    return [entry for weight in weights for entry in getattr(weight, field)]


def call(body, grid, in_specs, out_specs, out_shape, scratch, args, flops, scalars=()):
    size = sum(value.size * value.dtype.itemsize for value in args)
    size += sum(value.size * value.dtype.itemsize for value in out_shape)
    return pl.pallas_call(
        body,
        grid_spec=pltpu.PrefetchScalarGridSpec(
            num_scalar_prefetch=len(scalars),
            grid=grid,
            in_specs=in_specs,
            out_specs=out_specs,
            scratch_shapes=scratch,
        ),
        out_shape=out_shape,
        compiler_params=pltpu.CompilerParams(vmem_limit_bytes=VMEM_BYTES),
        cost_estimate=pl.CostEstimate(flops=flops, bytes_accessed=size, transcendentals=0),
    )(*scalars, *args)


def whole(shape):
    return pl.BlockSpec(shape, lambda *_: (0,) * len(shape))


def pick(value):
    return pl.BlockSpec(
        (1,) + value.shape[1:], lambda r, *_: (r,) + (0,) * (len(value.shape) - 1)
    )


def cross(left, right):
    lane = lax.broadcasted_iota(jnp.int32, left.shape, 1) < 64
    turned_left, turned_right = pltpu.roll(left, 64, 1), pltpu.roll(right, 64, 1)
    return jnp.where(lane, left, turned_right), jnp.where(lane, turned_left, right)


def split_rows(value):
    n = value.shape[0] // 4
    return (
        jnp.concatenate([value[:n], value[2 * n : 3 * n]], 0),
        jnp.concatenate([value[n : 2 * n], value[3 * n :]], 0),
    )


def join_rows(left, right):
    n = left.shape[0] // 2
    return jnp.concatenate([left[:n], right[:n], left[n:], right[n:]], 0)


def accumulate(ref, r, value):
    @pl.when(r == 0)
    def _():
        ref[...] = value

    @pl.when(r > 0)
    def _():
        ref[...] += value


def project_body(weights, info, x, *refs):
    groups, (bias_q, bias_v, out) = take_refs(weights, refs)
    q, k, v = [times(x[...], w.load(info, group)) for w, group in zip(weights, groups)]
    for i, value in enumerate((q + bias_q[0], k, v + bias_v[0])):
        for j, head in enumerate(cross(*split_rows(value))):
            out[j, 0, :, i * 128 : (i + 1) * 128] = head.astype(LOW)


def heads_spec(rows, lanes):
    return pl.BlockSpec((2, 1, rows, lanes), lambda r, order: (0, order[r], 0, 0))


def project(order, x, weights, bias_q, bias_v):
    m = x.shape[0]
    weights = weights[:3]
    (out,) = call(
        functools.partial(project_body, weights), (4,),
        [whole(x.shape)] + joined(weights, "specs") + [pick(bias_q), pick(bias_v)],
        [heads_spec(m // 2, 384)],
        [jax.ShapeDtypeStruct((2, 4, m // 2, 384), LOW)], [],
        [x] + joined(weights, "arrays") + [bias_q, bias_v], 2 * m * 1024 * 1536, (order,),
    )
    return out


def tokens_of(ref, lanes):
    left, right = cross(ref[0, 0, :, lanes].astype(FULL), ref[1, 0, :, lanes].astype(FULL))
    return join_rows(left, right).astype(LOW)


def mix_body(weight, info, heads, *refs):
    (group,), (mixed_out, out) = take_refs([weight], refs)
    mixed = tokens_of(heads, slice(0, 128))
    mixed_out[0] = mixed
    accumulate(out, pl.program_id(0), times_t(mixed, weight.load(info, group)))


def mix(order, heads, weight):
    m = heads.shape[2] * 2
    return call(
        functools.partial(mix_body, weight), (4,),
        [heads_spec(m // 2, 128)] + weight.specs,
        [pl.BlockSpec((1, m, 128), lambda r, *_: (r, 0, 0)), whole((m, 1024))],
        [jax.ShapeDtypeStruct((4, m, 128), LOW), jax.ShapeDtypeStruct((m, 1024), FULL)], [],
        [heads] + weight.arrays, 2 * m * 1024 * 512, (order,),
    )


def mix_back_body(weight, info, x, *refs):
    (group,), (out,) = take_refs([weight], refs)
    value = times(x[...], weight.load(info, group))
    for j, head in enumerate(cross(*split_rows(value))):
        out[j, 0] = head.astype(LOW)


def mix_back(order, x, weight):
    m = x.shape[0]
    (out,) = call(
        functools.partial(mix_back_body, weight), (4,),
        [whole(x.shape)] + weight.specs,
        [heads_spec(m // 2, 128)],
        [jax.ShapeDtypeStruct((2, 4, m // 2, 128), LOW)], [],
        [x] + weight.arrays, 2 * m * 1024 * 512, (order,),
    )
    return out


def project_back_body(weights, sinks, info, heads, x, spread, mixed, *refs):
    groups, refs = take_refs(weights, refs)
    pairs, out = grad_refs(sinks, refs[:-1]), refs[-1]
    terms = None
    for i in range(3):
        low = tokens_of(heads, slice(i * 128, (i + 1) * 128))
        sinks[i].store(pairs[i], t_times(x[...], low).astype(LOW))
        term = times_t(low, weights[i].load(info, groups[i]))
        terms = term if terms is None else terms + term
    sinks[3].store(pairs[3], t_times(spread[...], mixed[0]).astype(LOW))
    accumulate(out, pl.program_id(0), terms)


def project_back(order, heads, x, spread, mixed, weights, sinks):
    m = x.shape[0]
    weights = weights[:3]
    specs, shapes = grad_outs(sinks)
    *grads, out = call(
        functools.partial(project_back_body, weights, sinks), (4,),
        [heads_spec(m // 2, 384), whole(x.shape), whole(x.shape), pick(mixed)]
        + joined(weights, "specs"),
        specs + [whole((m, 1024))],
        shapes + [jax.ShapeDtypeStruct((m, 1024), FULL)], [],
        [heads, x, spread, mixed] + joined(weights, "arrays"), 2 * m * 1024 * 3584, (order,),
    )
    return halves(grads), out


def feed_body(weights, info, x, bias, *refs):
    groups, (hidden_out, active_out, out) = take_refs(weights, refs)
    total = None
    for j in range(2):
        hidden = times(x[...], weights[j].load(info, groups[j])) + bias[0, j : j + 1]
        hidden_out[0, j] = hidden
        active = (hidden * (0.5 * (1.0 + lax.erf(hidden * ROOT_HALF)))).astype(LOW)
        active_out[0, j] = active
        term = times_t(active, weights[2 + j].load(info, groups[2 + j]))
        total = term if total is None else total + term
    accumulate(out, pl.program_id(0), total)


def feed(order, x, bias, weights):
    m = x.shape[0]
    block = pl.BlockSpec((1, 2, m, 256), lambda r, *_: (r, 0, 0, 0))
    return call(
        functools.partial(feed_body, weights), (4,),
        [whole(x.shape), pick(bias)] + joined(weights, "specs"),
        [block, block, whole((m, 1024))],
        [
            jax.ShapeDtypeStruct((4, 2, m, 256), FULL), jax.ShapeDtypeStruct((4, 2, m, 256), LOW),
            jax.ShapeDtypeStruct((m, 1024), FULL),
        ], [],
        [x, bias] + joined(weights, "arrays"), 4 * m * 1024 * 2048, (order,),
    )


def feed_back_body(weights, info, spread, x, hidden, active, *refs):
    groups, refs = take_refs(weights, refs)
    pairs, (grad_bias, out) = grad_refs(FEED, refs[:-2]), refs[-2:]
    total = None
    for j in range(2):
        value = hidden[0, j]
        slope = 0.5 * (1.0 + lax.erf(value * ROOT_HALF))
        slope += value * jnp.exp(-0.5 * value * value) * (1.0 / ROOT_TWOPI)
        grad = times(spread[...], weights[2 + j].load(info, groups[2 + j])) * slope
        grad_bias[0, j : j + 1] = jnp.sum(grad, axis=0, keepdims=True)
        low = grad.astype(LOW)
        FEED[2 + j].store(pairs[2 + j], t_times(spread[...], active[0, j]).astype(LOW))
        FEED[j].store(pairs[j], t_times(x[...], low).astype(LOW))
        term = times_t(low, weights[j].load(info, groups[j]))
        total = term if total is None else total + term
    accumulate(out, pl.program_id(0), total)


def feed_back(order, spread, x, hidden, active, weights):
    m = x.shape[0]
    specs, shapes = grad_outs(FEED)
    *grads, grad_bias, out = call(
        functools.partial(feed_back_body, weights), (4,),
        [whole(x.shape), whole(x.shape), pick(hidden), pick(active)] + joined(weights, "specs"),
        specs + [pl.BlockSpec((1, 2, 256), lambda r, *_: (r, 0, 0)), whole((m, 1024))],
        shapes
        + [jax.ShapeDtypeStruct((4, 2, 256), FULL), jax.ShapeDtypeStruct((m, 1024), FULL)], [],
        [spread, x, hidden, active] + joined(weights, "arrays"), 8 * m * 1024 * 2048, (order,),
    )
    return halves(grads), grad_bias, out


def one_row(value, s):
    lane = lax.broadcasted_iota(jnp.int32, value.shape, 1) // 64 == s
    return jnp.where(lane, value, jnp.zeros_like(value))


def scores_of(keys, query, mark_keys, mark_query, s):
    scores = times_t(keys, one_row(query, s) * LOW(0.125))
    same = mark_keys[:, s : s + 1] == mark_query[s : s + 1, :]
    return jnp.where(same, scores, MASKED)


def attend_body(query, keys, values, mark_keys, mark_query, out, summary):
    turned = values[...].astype(FULL).T.astype(LOW)
    results = []
    for s in range(2):
        scores = scores_of(keys[...], query[...], mark_keys, mark_query, s)
        top = jnp.max(scores, axis=0, keepdims=True)
        weights = jnp.exp(scores - top)
        total = jnp.sum(weights, axis=0, keepdims=True)
        probs = (weights * (1.0 / total)).astype(LOW)
        results.append(times(turned[s * 64 : (s + 1) * 64], probs))
        summary[s : s + 1] = top + jnp.log(total)
    out[...] = jnp.concatenate(results, 0).T.astype(LOW)


def attend(qkv, mark_keys, mark_query):
    n = qkv.shape[0]
    q = 384

    return call(
        attend_body, (n // q,),
        [
            pl.BlockSpec((q, 128), lambda i: (i, 0)), pl.BlockSpec((n, 128), lambda i: (0, 1)),
            pl.BlockSpec((n, 128), lambda i: (0, 2)), whole((n, 2)),
            pl.BlockSpec((2, q), lambda i: (0, i)),
        ],
        [pl.BlockSpec((q, 128), lambda i: (i, 0)), pl.BlockSpec((2, q), lambda i: (0, i))],
        [jax.ShapeDtypeStruct((n, 128), LOW), jax.ShapeDtypeStruct((2, n), FULL)], [],
        (qkv, qkv, qkv, mark_keys, mark_query), 8 * n * n * 128,
    )


def attend_back_body(
    query, keys, values, grad_mixed, mark_keys, mark_query, summary, out, sums, sum_k, sum_v, sum_q
):
    i = pl.program_id(0)
    n, q = keys.shape[0], query.shape[0]
    turned = keys[...].astype(FULL).T.astype(LOW)
    lane = lax.broadcasted_iota(jnp.int32, (n, 128), 1) < 64
    grads_q, grads_k, grads_v = [], [], []
    for s in range(2):
        scores = scores_of(keys[...], query[...], mark_keys, mark_query, s)
        probs = jnp.exp(scores - summary[s : s + 1])
        grad_probs = times_t(values[...], one_row(grad_mixed[...], s))
        inner = jnp.sum(probs * grad_probs, axis=0, keepdims=True)
        low_probs = probs.astype(LOW)
        grad_scores = (probs * (grad_probs - inner)).astype(LOW)
        grads_v.append(times(low_probs, grad_mixed[...]))
        grads_k.append(times(grad_scores, query[...]))
        grads_q.append(times(turned[s * 64 : (s + 1) * 64], grad_scores))
    accumulate(sum_k, i, jnp.where(lane, grads_k[0], grads_k[1]) * 0.125)
    accumulate(sum_v, i, jnp.where(lane, grads_v[0], grads_v[1]))
    grad_q = jnp.concatenate(grads_q, 0).T * 0.125
    accumulate(sum_q, i, jnp.sum(grad_q, axis=0, keepdims=True))
    out[pl.ds(pl.multiple_of(i * q, q), q), :128] = grad_q.astype(LOW)

    @pl.when(i == pl.num_programs(0) - 1)
    def _():
        out[:, 128:256] = sum_k[...].astype(LOW)
        out[:, 256:] = sum_v[...].astype(LOW)
        sums[0:1] = sum_q[...]
        sums[1:2] = jnp.sum(sum_v[...], axis=0, keepdims=True)


def attend_back(qkv, grad_mixed, mark_keys, mark_query, summary):
    n = qkv.shape[0]
    q = 384
    return call(
        attend_back_body, (n // q,),
        [
            pl.BlockSpec((q, 128), lambda i: (i, 0)), pl.BlockSpec((n, 128), lambda i: (0, 1)),
            pl.BlockSpec((n, 128), lambda i: (0, 2)), pl.BlockSpec((q, 128), lambda i: (i, 0)),
            whole((n, 2)), pl.BlockSpec((2, q), lambda i: (0, i)),
            pl.BlockSpec((2, q), lambda i: (0, i)),
        ],
        [whole((n, 384)), whole((2, 128))],
        [jax.ShapeDtypeStruct((n, 384), LOW), jax.ShapeDtypeStruct((2, 128), FULL)],
        [pltpu.VMEM((n, 128), FULL), pltpu.VMEM((n, 128), FULL), pltpu.VMEM((1, 128), FULL)],
        (qkv, qkv, qkv, grad_mixed, mark_keys, mark_query, summary), 20 * n * n * 128,
    )


def trade(value):
    return lax.all_to_all(
        value, ("ctx", "tensor"), 0, 0, axis_index_groups=GROUPS, tiled=True
    )


def local(
    stream, segments, w_qkv, qv_bias, w_out, norm_gains, shifts, w_in, in_bias, w_back, cotangent
):
    layers = w_qkv.shape[0]
    dp, ctx, me_x = lax.axis_index("dp"), lax.axis_index("ctx"), lax.axis_index("tensor")
    core, z_lo = ctx & 1, ctx >> 1
    me_y, me_z = dp & 3, (dp >> 2) * 2 + z_lo
    rows = stream.shape[1]
    width = stream.shape[2]

    def both_rows(columns):
        axis = columns.ndim - 2
        keep = lax.dynamic_index_in_dim(columns, core, axis, False)
        new = swap(lax.dynamic_index_in_dim(columns, 1 - core, axis, False))
        return jnp.where(
            core == 0, jnp.concatenate([keep, new], -2), jnp.concatenate([new, keep], -2)
        )

    lead = both_rows(
        jnp.concatenate(
            [
                jnp.concatenate(
                    [
                        w_qkv[layer].reshape(32, 3, 2, 128).transpose(0, 2, 1, 3).reshape(
                            32, 2, 384
                        ),
                        w_out[layer].T.reshape(32, 2, 128),
                    ],
                    2,
                )
                for layer in range(2)
            ],
            2,
        )
    ).reshape(1, 64, 2, 4, 128)
    lead = gather_early([lead[:, :, :, k].reshape(1, 64, 256) for k in range(4)])
    later = jnp.concatenate([w_in[0], w_back[0].T, w_in[1], w_back[1].T], 1)
    later = lax.all_gather(later, "tensor", axis=0, tiled=True)
    lead, norm_gains, later = lax.optimization_barrier((lead, norm_gains, later))
    lead_one = [value[:, :, 128:] for value in lead]
    lead = gather_late([value[:, :, :128] for value in lead])
    lead, lead_one = lax.optimization_barrier((lead, lead_one))
    near_one = [swap(value, *ORDERS[k][4]) for k, value in enumerate(lead_one)]

    def everywhere(value):
        value = lax.all_gather(value, ("dp", "ctx"), axis=0, tiled=True)
        return value.reshape(16, 2, 4, 32, value.shape[1])

    feed_zero = everywhere(later[:, :2048])
    feed_one = everywhere(later[:, 2048:])
    attention_w = [[Exchanged(k, lead[k], 128) for k in range(4)]]
    feed_w = [
        [Gathered(value, base, 256, 2) for base in (0, 1, 4, 5)] for value in (feed_zero, feed_one)
    ]

    vectors = jnp.concatenate(
        [norm_gains.reshape(-1), shifts.reshape(-1), qv_bias.reshape(-1), in_bias.reshape(-1)]
    )
    vectors = jnp.pad(vectors, (0, 512 - vectors.shape[0]))
    spread = lax.all_to_all(jnp.broadcast_to(vectors, (128, 512)), ALL, 0, 0, tiled=True)
    spread = spread.reshape(32, 4, 512)
    gains_abs = spread[:, 0, 0:128].reshape(32, 4, 32).transpose(1, 0, 2).reshape(4, width)
    shifts_abs = spread[:, 0, 128:384].reshape(32, 8, 32).transpose(1, 0, 2).reshape(8, width)
    pair = spread[:, :, 384:416].reshape(32, 4, layers, 2, 2, 2, 2).transpose(2, 3, 1, 4, 5, 0, 6)
    pair = lax.dynamic_index_in_dim(pair.reshape(layers, 2, 4, 2, 2, 64), core, 3, False)
    pair = take_relative(pair, me_x, 2).astype(FULL)
    up = spread[:, :, 416:480].reshape(32, 4, layers, 2, 2, 8).transpose(2, 1, 3, 4, 0, 5)
    up = lax.dynamic_index_in_dim(up.reshape(layers, 4, 2, 2, 256), core, 2, False)
    up = take_relative(up, me_x, 1).astype(FULL)

    place = lax.broadcasted_iota(jnp.int32, (width, width), 1)
    block = place >> 6
    far_z = me_z ^ (((block >> 2) & 1) ^ ((block >> 3) * 3))
    far_y = me_y ^ ((block & 1) ^ (((block >> 1) & 1) * 3))
    source = (((far_z >> 1) * 4 + far_y) * 2 + (far_z & 1)) * 64 + (place & 63)
    reorder = source == lax.broadcasted_iota(jnp.int32, (width, width), 0)
    reorder_low = reorder.astype(LOW)
    reorder_full = reorder.astype(FULL)

    def absolute(value):
        return lax.dot_general(
            value, reorder_full, (((1,), (1,)), ((), ())), precision=lax.Precision.HIGHEST,
            preferred_element_type=FULL,
        )

    tokens = 2 * rows
    inputs = times(
        jnp.concatenate(
            [
                stream.reshape(tokens, width), cotangent.reshape(tokens, width),
                gains_abs, shifts_abs,
            ]
        ),
        reorder_low,
    )
    state = inputs[:tokens]
    incoming = inputs[tokens : 2 * tokens]
    gains = inputs[2 * tokens : 2 * tokens + 4].reshape(layers, 2, width)
    shift = inputs[2 * tokens + 4 :].reshape(layers, 4, width)

    marks = segments.reshape(2, 2, 2, 4, rows)
    marks = jnp.where(core == 0, marks, marks[:, :, ::-1])
    marks = marks.transpose(0, 1, 3, 2, 4).reshape(2, 16 * rows)
    marks_t = marks.T
    chips = []
    for i in range(16):
        far_z = me_z ^ (((i >> 2) & 1) ^ ((i >> 3) * 3))
        far_y = me_y ^ ((i & 1) ^ (((i >> 1) & 1) * 3))
        chips.append(((far_z >> 1) * 4 + far_y) * 2 + (far_z & 1))
    order = [relative_x(me_x, r) for r in range(4)] + [core] + chips
    order = jnp.stack(order).astype(jnp.int32)

    saved = []
    for layer in range(layers):
        bias = pair[layer].reshape(2, 4, 1, 128)
        gathered = both(state.astype(LOW))
        qkv = project(order, gathered, attention_w[layer], bias[0], bias[1])
        qkv = trade(qkv.reshape(8, 2 * rows, 384)).reshape(16 * rows, 384)
        if layer == 0:
            qkv, near_one = lax.optimization_barrier((qkv, near_one))
            far_one = [swap(value, *ORDERS[k][5]) for k, value in enumerate(lead_one)]
            last_one = [swap(value, *ORDERS[k][5]) for k, value in enumerate(near_one)]
        mixed, summary = attend(qkv, marks_t, marks)
        mixed = trade(mixed.reshape(8, 2 * rows, 128)).reshape(2, 4, 2 * rows, 128)
        if layer == 0:
            mixed, far_one = lax.optimization_barrier((mixed, far_one))
        mixed, attended = mix(order, mixed, attention_w[layer][3])
        attended = own_sum(attended) + shift[layer, 2]
        first, unit_one, inv_one = normalize(state + attended, gains[layer, 0], shift[layer, 0])
        gathered_two = both(first.astype(LOW))
        if layer == 0:
            gathered_two, last_one = lax.optimization_barrier((gathered_two, last_one))
            pieces = zip(lead_one, near_one, far_one, last_one)
            attention_w.append([Exchanged(k, four, 128) for k, four in enumerate(pieces)])
        hidden, active, down = feed(order, gathered_two, up[layer], feed_w[layer])
        down = own_sum(down)
        state, unit_two, inv_two = normalize(
            first + down + shift[layer, 3], gains[layer, 1], shift[layer, 1]
        )
        saved.append(
            (gathered, qkv, summary, mixed, unit_one, inv_one, gathered_two, hidden, active,
             unit_two, inv_two)
        )
    result = absolute(state)

    small = [None] * layers

    def vector_sums():
        vec = absolute(
            jnp.concatenate([small[layer][0] for layer in range(layers)]
                            + [small[layer][1] for layer in range(layers)])
        )
        vec = vec.reshape(12, 32, 32).transpose(1, 0, 2).reshape(32, 1, 384)
        vec = jnp.broadcast_to(vec, (32, 4, 384))
        pair = jnp.stack([small[layer][2] for layer in range(layers)])
        head = me_x * 4 + core * 2 + z_lo
        pair = jnp.where((jnp.arange(16) == head)[:, None], pair[:, :, None], 0.0)
        pair = pair.reshape(layers, 2, 4, 4, 32, 2).transpose(4, 2, 0, 1, 3, 5).reshape(32, 4, 32)
        up = take_absolute(jnp.stack([small[layer][3] for layer in range(layers)]), me_x, 1)
        up = jnp.where((jnp.arange(2) == core)[:, None, None], up[:, :, None], 0.0)
        up = up.reshape(layers, 4, 4, 32, 8).transpose(3, 1, 0, 2, 4).reshape(32, 4, 64)
        vec = jnp.concatenate([vec, pair, up, jnp.zeros((32, 4, 32), FULL)], 2).reshape(128, 512)
        return jnp.sum(lax.all_to_all(vec, ALL, 0, 0, tiled=True), axis=0)

    for layer in reversed(range(layers)):
        (gathered, qkv, summary, mixed, unit_one, inv_one, gathered_two, hidden, active,
         unit_two, inv_two) = saved[layer]
        grad_two, gain_two, shift_two = normalize_back(
            incoming, unit_two, inv_two, gains[layer, 1]
        )
        spread_two = both(grad_two.astype(LOW))
        grad_feed, grad_upbias, grad_first = feed_back(
            order, spread_two, gathered_two, hidden, active, feed_w[layer]
        )
        if layer == 0:
            grad_feed = reduce_first(grad_feed, range(4))
        grad_first = grad_two + own_sum(grad_first)
        grad_one, gain_one, shift_one = normalize_back(
            grad_first, unit_one, inv_one, gains[layer, 0]
        )
        spread_one = both(grad_one.astype(LOW))
        if layer == 0:
            spread_one, later = lax.optimization_barrier((spread_one, later))
            later = reduce_phase(later, range(4), 1)
        grad_mixed = trade(mix_back(order, spread_one, attention_w[layer][3]).reshape(8, 2 * rows, 128))
        grad_mixed = grad_mixed.reshape(16 * rows, 128)
        if layer == 0:
            grad_mixed, grad_feed, later = lax.optimization_barrier((grad_mixed, grad_feed, later))
            grad_feed = reduce_phase(grad_feed, range(4), 1)
        low_packed, grad_pair = attend_back(qkv, grad_mixed, marks_t, marks, summary)
        grad_pair = grad_pair.reshape(2, 2, 64).sum(1)
        if layer == 0:
            low_packed, grad_feed = lax.optimization_barrier((low_packed, grad_feed))
            tail = [jnp.concatenate([a, b], 2) for a, b in zip(grad_feed, later)]
            tail = reduce_phase(reduce_phase(tail, range(4), 2), range(4), 3)
        small[layer] = (
            jnp.stack([gain_one, gain_two]),
            jnp.stack(
                [shift_one, shift_two, jnp.sum(grad_one, axis=0), jnp.sum(grad_two, axis=0)]
            ),
            grad_pair,
            grad_upbias,
        )
        low_packed = trade(low_packed.reshape(8, 2 * rows, 384)).reshape(2, 4, 2 * rows, 384)
        if layer == 0:
            low_packed, tail, vec = lax.optimization_barrier((low_packed, tail, vector_sums()))
        grad_attention, grad_x = project_back(
            order, low_packed, gathered, spread_one, mixed, attention_w[layer],
            APART,
        )
        incoming = grad_one + own_sum(grad_x)
        if layer:
            later = [
                [jnp.concatenate(half, 2) for half in zip(*pairs)]
                for pairs in zip(grad_feed, grad_attention)
            ]
            later = reduce_first(later, range(4))
        else:
            lead = reduce_phase(reduce_first(grad_attention, range(4)), range(4), 1)
            lead = reduce_phase(reduce_phase(lead, range(4), 2), range(4), 3)
            tail = [jnp.concatenate(pair, 2) for pair in zip(tail, lead)]
            tail = reduce_phases(tail, range(4), 4)
    grad_stream = absolute(incoming)

    def own_rows(parts):
        total = jnp.stack(parts, 1)
        total = total.reshape((2, 32) + total.shape[1:])
        keep = lax.dynamic_index_in_dim(total, core, 0, False)
        new = swap(lax.dynamic_index_in_dim(total, 1 - core, 0, False))
        return jnp.stack(
            [jnp.where(core == 0, keep, new), jnp.where(core == 0, new, keep)], 1
        ).astype(FULL)

    tail = own_rows(tail)
    attention = [tail[..., 640:], tail[..., 512:640]]
    feeds = [tail[..., :256], tail[..., 256:512]]
    out_qkv = jnp.stack(
        [value[:, :, :3].transpose(0, 2, 1, 3).reshape(32, 3, 256) for value in attention]
    )
    out_o = jnp.stack([value[:, :, 3].reshape(32, 256).T for value in attention])
    out_up = jnp.stack([value[:, :, :2].reshape(32, 1024) for value in feeds])
    out_down = jnp.stack([value[:, :, 2:].reshape(32, 1024).T for value in feeds])

    return (
        result.reshape(stream.shape),
        grad_stream.reshape(stream.shape),
        out_qkv,
        vec[384:416].reshape(qv_bias.shape),
        out_o,
        vec[:128].reshape(norm_gains.shape),
        vec[128:384].reshape(shifts.shape),
        out_up,
        vec[416:480].reshape(in_bias.shape),
        out_down,
    )


def solution(mesh):
    return jax.shard_map(
        local,
        mesh=mesh,
        in_specs=(
            P("dp", ("ctx", "tensor"), None),
            P("dp", None),
            P(None, ("dp", "ctx"), None, "tensor"),
            P(None, None, "tensor", ("dp", "ctx")),
            P(None, "tensor", ("dp", "ctx")),
            P(None, None, ("dp", "ctx")),
            P(None, None, ("dp", "ctx")),
            P(None, ("dp", "ctx"), "tensor"),
            P(None, "tensor", ("dp", "ctx")),
            P(None, "tensor", ("dp", "ctx")),
            P("dp", ("ctx", "tensor"), None),
        ),
        out_specs=(
            P("dp", ("ctx", "tensor"), None),
            P("dp", ("ctx", "tensor"), None),
            P(None, ("dp", "ctx"), None, "tensor"),
            P(None, None, "tensor", ("dp", "ctx")),
            P(None, "tensor", ("dp", "ctx")),
            P(None, None, ("dp", "ctx")),
            P(None, None, ("dp", "ctx")),
            P(None, ("dp", "ctx"), "tensor"),
            P(None, "tensor", ("dp", "ctx")),
            P(None, "tensor", ("dp", "ctx")),
        ),
        check_vma=False,
    )
```

```python
import functools

import jax
import jax.numpy as jnp
from jax import lax
from jax.experimental import pallas as pl
from jax.experimental.pallas import tpu as pltpu
from jax.sharding import PartitionSpec as P

EPSILON = 1e-12
MASKED = -1000000000.0
ROOT_HALF = 0.7071067811865476
ROOT_TWOPI = 2.5066282746310002
ALL = ("dp", "ctx", "tensor")
LOW = jnp.bfloat16
FULL = jnp.float32

X1, X3, Y1, Y3, Z1, Z3 = ("x", 1), ("x", 3), ("y", 1), ("y", 3), ("z", 1), ("z", 3)
ORDERS = (
    (X1, Y3, X3, Z3, Y1, Z1),
    (Y1, X1, Z3, X3, Z1, Y3),
    (X3, Z1, X1, Y1, Y3, Z3),
    (Z1, X3, Y3, X1, Z3, Y1),
)
GROUPS = [[(zl * 2 + c) * 4 + x for zl in range(2) for x in range(4)] for c in range(2)]


def exchange_perm(axis, mask):
    pairs = []
    for device in range(128):
        dp, ctx, x = device // 16, (device // 4) % 4, device % 4
        at = {"x": x, "y": dp % 4, "z": (dp // 4) * 2 + ctx // 2, "core": ctx % 2}
        at[axis] ^= mask
        other = ((at["z"] // 2) * 4 + at["y"]) * 16
        other += ((at["z"] % 2) * 2 + at["core"]) * 4 + at["x"]
        pairs.append((device, other))
    return pairs


def swap(value, axis="core", mask=1):
    return lax.ppermute(value, ALL, exchange_perm(axis, mask))


def gather_early(parts):
    for phase in range(4):
        got = [swap(value, *ORDERS[k][phase]) for k, value in enumerate(parts)]
        parts = [jnp.concatenate([value, new], 0) for value, new in zip(parts, got)]
    return parts


def gather_late(parts):
    near = [swap(value, *ORDERS[k][4]) for k, value in enumerate(parts)]
    far = [swap(value, *ORDERS[k][5]) for k, value in enumerate(parts)]
    both_far = [swap(value, *ORDERS[k][5]) for k, value in enumerate(near)]
    return [list(four) for four in zip(parts, near, far, both_far)]


def add_low(left, right):
    return (left.astype(FULL) + right.astype(FULL)).astype(LOW)


def reduce_first(pairs, orders):
    parts = [add_low(kept, swap(sent, *ORDERS[k][5])) for k, (kept, sent) in zip(orders, pairs)]
    return reduce_phase(parts, orders, 1)


def reduce_phase(parts, orders, phase):
    half = parts[0].shape[0] // 2
    got = [swap(value[half:], *ORDERS[k][5 - phase]) for k, value in zip(orders, parts)]
    return [add_low(value[:half], new) for value, new in zip(parts, got)]


def reduce_phases(parts, orders, first):
    for phase in range(first, 6):
        parts = reduce_phase(parts, orders, phase)
    return [value[0] for value in parts]


def relative_x(me_x, r):
    return me_x ^ (0, 1, 3, 2)[r]


def take_relative(value, me_x, axis):
    return jnp.concatenate(
        [lax.dynamic_slice_in_dim(value, relative_x(me_x, r), 1, axis) for r in range(4)], axis
    )


def take_absolute(value, me_x, axis):
    parts = []
    for x in range(4):
        off = me_x ^ x
        parts.append(lax.dynamic_slice_in_dim(value, off ^ (off >> 1), 1, axis))
    return jnp.concatenate(parts, axis)


def both(value):
    return jnp.concatenate([value, swap(value)], 0)


def own_sum(value):
    half = value.shape[0] // 2
    value = value.astype(FULL)
    return value[:half] + swap(value[half:].astype(LOW)).astype(FULL)


def normalize(values, gain, shift):
    mean = jnp.mean(values, axis=-1, keepdims=True)
    centred = values - mean
    inverse = lax.rsqrt(jnp.mean(centred * centred, axis=-1, keepdims=True) + EPSILON)
    unit = centred * inverse
    return (unit * gain + shift, unit, inverse)


def normalize_back(incoming, unit, inverse, gain):
    scaled = incoming * gain
    inner = (
        scaled
        - jnp.mean(scaled, axis=-1, keepdims=True)
        - unit * jnp.mean(scaled * unit, axis=-1, keepdims=True)
    )
    return (inverse * inner, jnp.sum(incoming * unit, axis=0), jnp.sum(incoming, axis=0))


def dot(left, right, dims):
    return lax.dot_general(left, right, (dims, ((), ())), preferred_element_type=FULL)


def times(left, right):
    return dot(left, right, ((1,), (0,)))


def times_t(left, right):
    return dot(left, right, ((1,), (1,)))


def t_times(left, right):
    return dot(left, right, ((0,), (0,)))


VMEM_BYTES = 56 * 1024 * 1024


ZY = (Z3, Z1, Y3, Y1)


class Exchanged:
    def __init__(self, k, pieces, columns):
        self.k = k
        self.arrays = [value.reshape((2,) * 4 + value.shape[1:]) for value in pieces]
        axes = ORDERS[k][3::-1]

        def index(r, *_):
            at = {X3: r // 2, X1: r % 2}
            return tuple(at.get(dim, 0) for dim in axes) + (0, 0)

        shape = tuple(1 if dim[0] == "x" else 2 for dim in axes) + (64, columns)
        self.specs = [pl.BlockSpec(shape, index)] * 4

    def load(self, info, refs):
        rows = []
        for i in range(16):
            bits = dict(zip(ZY, (i >> 3, (i >> 2) & 1, (i >> 1) & 1, i & 1)))
            piece = 2 * bits[ORDERS[self.k][5]] + bits[ORDERS[self.k][4]]
            at = tuple(bits.get(dim, 0) for dim in ORDERS[self.k][3::-1])
            rows.append(refs[piece][at])
        return jnp.concatenate(rows, 0)


class Gathered:
    def __init__(self, array, base, columns, step):
        self.arrays = [array]

        def index(r, info):
            return (0, 0, info[r], 0, base + info[4] * step)

        self.specs = [pl.BlockSpec((16, 2, 1, 32, columns), index)]

    def load(self, info, refs):
        (ref,) = refs
        return jnp.concatenate(
            [ref[info[5 + i], half, 0] for i in range(16) for half in range(2)], 0
        )


class Grads:
    def __init__(self, k, width, at):
        self.k, self.width, self.at = k, width, at

    def store(self, refs, value):
        for i in range(16):
            bits = dict(zip(ZY, (i >> 3, (i >> 2) & 1, (i >> 1) & 1, i & 1)))
            place = tuple(bits.get(dim, 0) for dim in ORDERS[self.k][4::-1])
            place += (slice(None), slice(self.at, self.at + value.shape[1]))
            refs[bits[ORDERS[self.k][5]]][place] = value[i * 64 : (i + 1) * 64]


def grad_spec(sink):
    axes = ORDERS[sink.k][4::-1]

    def index(r, *_):
        at = {X3: r // 2, X1: r % 2}
        return tuple(at.get(dim, 0) for dim in axes) + (0, 0)

    shape = tuple(1 if dim[0] == "x" else 2 for dim in axes) + (64, sink.width)
    return [pl.BlockSpec(shape, index)] * 2


def grad_outs(sinks):
    first = [sink for sink in sinks if sink.at == 0]
    specs = [spec for sink in first for spec in grad_spec(sink)]
    shapes = [
        jax.ShapeDtypeStruct((2,) * 5 + (64, sink.width), LOW) for sink in first for _ in range(2)
    ]
    return specs, shapes


def grad_refs(sinks, refs):
    pairs, at = [], -2
    for sink in sinks:
        at += 2 if sink.at == 0 else 0
        pairs.append(refs[at : at + 2])
    return pairs


def take_refs(weights, refs):
    groups = []
    for weight in weights:
        groups.append(refs[: len(weight.arrays)])
        refs = refs[len(weight.arrays) :]
    return groups, refs


APART = [Grads(k, 128, 0) for k in range(4)]
FEED = [Grads(k, 256, 0) for k in range(4)]


def halves(refs):
    pairs = zip(refs[::2], refs[1::2])
    return [tuple(v.reshape((32,) + v.shape[-2:]) for v in pair) for pair in pairs]


def joined(weights, field):
    return [entry for weight in weights for entry in getattr(weight, field)]


def call(body, grid, in_specs, out_specs, out_shape, scratch, args, flops, scalars=()):
    size = sum(value.size * value.dtype.itemsize for value in args)
    size += sum(value.size * value.dtype.itemsize for value in out_shape)
    return pl.pallas_call(
        body,
        grid_spec=pltpu.PrefetchScalarGridSpec(
            num_scalar_prefetch=len(scalars),
            grid=grid,
            in_specs=in_specs,
            out_specs=out_specs,
            scratch_shapes=scratch,
        ),
        out_shape=out_shape,
        compiler_params=pltpu.CompilerParams(vmem_limit_bytes=VMEM_BYTES),
        cost_estimate=pl.CostEstimate(flops=flops, bytes_accessed=size, transcendentals=0),
    )(*scalars, *args)


def whole(shape):
    return pl.BlockSpec(shape, lambda *_: (0,) * len(shape))


def pick(value):
    return pl.BlockSpec(
        (1,) + value.shape[1:], lambda r, *_: (r,) + (0,) * (len(value.shape) - 1)
    )


def cross(left, right):
    lane = lax.broadcasted_iota(jnp.int32, left.shape, 1) < 64
    turned_left, turned_right = pltpu.roll(left, 64, 1), pltpu.roll(right, 64, 1)
    return jnp.where(lane, left, turned_right), jnp.where(lane, turned_left, right)


def split_rows(value):
    n = value.shape[0] // 4
    return (
        jnp.concatenate([value[:n], value[2 * n : 3 * n]], 0),
        jnp.concatenate([value[n : 2 * n], value[3 * n :]], 0),
    )


def join_rows(left, right):
    n = left.shape[0] // 2
    return jnp.concatenate([left[:n], right[:n], left[n:], right[n:]], 0)


def accumulate(ref, r, value):
    @pl.when(r == 0)
    def _():
        ref[...] = value

    @pl.when(r > 0)
    def _():
        ref[...] += value


def project_body(weights, info, x, *refs):
    groups, (bias_q, bias_v, out) = take_refs(weights, refs)
    q, k, v = [times(x[...], w.load(info, group)) for w, group in zip(weights, groups)]
    for i, value in enumerate((q + bias_q[0], k, v + bias_v[0])):
        for j, head in enumerate(cross(*split_rows(value))):
            out[j, 0, :, i * 128 : (i + 1) * 128] = head.astype(LOW)


def heads_spec(rows, lanes):
    return pl.BlockSpec((2, 1, rows, lanes), lambda r, order: (0, order[r], 0, 0))


def project(order, x, weights, bias_q, bias_v):
    m = x.shape[0]
    weights = weights[:3]
    (out,) = call(
        functools.partial(project_body, weights), (4,),
        [whole(x.shape)] + joined(weights, "specs") + [pick(bias_q), pick(bias_v)],
        [heads_spec(m // 2, 384)],
        [jax.ShapeDtypeStruct((2, 4, m // 2, 384), LOW)], [],
        [x] + joined(weights, "arrays") + [bias_q, bias_v], 2 * m * 1024 * 1536, (order,),
    )
    return out


def tokens_of(ref, lanes):
    left, right = cross(ref[0, 0, :, lanes].astype(FULL), ref[1, 0, :, lanes].astype(FULL))
    return join_rows(left, right).astype(LOW)


def mix_body(weight, info, heads, *refs):
    (group,), (mixed_out, out) = take_refs([weight], refs)
    mixed = tokens_of(heads, slice(0, 128))
    mixed_out[0] = mixed
    accumulate(out, pl.program_id(0), times_t(mixed, weight.load(info, group)))


def mix(order, heads, weight):
    m = heads.shape[2] * 2
    return call(
        functools.partial(mix_body, weight), (4,),
        [heads_spec(m // 2, 128)] + weight.specs,
        [pl.BlockSpec((1, m, 128), lambda r, *_: (r, 0, 0)), whole((m, 1024))],
        [jax.ShapeDtypeStruct((4, m, 128), LOW), jax.ShapeDtypeStruct((m, 1024), FULL)], [],
        [heads] + weight.arrays, 2 * m * 1024 * 512, (order,),
    )


def mix_back_body(weight, info, x, *refs):
    (group,), (out,) = take_refs([weight], refs)
    value = times(x[...], weight.load(info, group))
    for j, head in enumerate(cross(*split_rows(value))):
        out[j, 0] = head.astype(LOW)


def mix_back(order, x, weight):
    m = x.shape[0]
    (out,) = call(
        functools.partial(mix_back_body, weight), (4,),
        [whole(x.shape)] + weight.specs,
        [heads_spec(m // 2, 128)],
        [jax.ShapeDtypeStruct((2, 4, m // 2, 128), LOW)], [],
        [x] + weight.arrays, 2 * m * 1024 * 512, (order,),
    )
    return out


def project_back_body(weights, sinks, info, heads, x, spread, mixed, *refs):
    groups, refs = take_refs(weights, refs)
    pairs, out = grad_refs(sinks, refs[:-1]), refs[-1]
    terms = None
    for i in range(3):
        low = tokens_of(heads, slice(i * 128, (i + 1) * 128))
        sinks[i].store(pairs[i], t_times(x[...], low).astype(LOW))
        term = times_t(low, weights[i].load(info, groups[i]))
        terms = term if terms is None else terms + term
    sinks[3].store(pairs[3], t_times(spread[...], mixed[0]).astype(LOW))
    accumulate(out, pl.program_id(0), terms)


def project_back(order, heads, x, spread, mixed, weights, sinks):
    m = x.shape[0]
    weights = weights[:3]
    specs, shapes = grad_outs(sinks)
    *grads, out = call(
        functools.partial(project_back_body, weights, sinks), (4,),
        [heads_spec(m // 2, 384), whole(x.shape), whole(x.shape), pick(mixed)]
        + joined(weights, "specs"),
        specs + [whole((m, 1024))],
        shapes + [jax.ShapeDtypeStruct((m, 1024), FULL)], [],
        [heads, x, spread, mixed] + joined(weights, "arrays"), 2 * m * 1024 * 3584, (order,),
    )
    return halves(grads), out


def feed_body(weights, info, x, bias, *refs):
    groups, (hidden_out, active_out, out) = take_refs(weights, refs)
    total = None
    for j in range(2):
        hidden = times(x[...], weights[j].load(info, groups[j])) + bias[0, j : j + 1]
        hidden_out[0, j] = hidden
        active = (hidden * (0.5 * (1.0 + lax.erf(hidden * ROOT_HALF)))).astype(LOW)
        active_out[0, j] = active
        term = times_t(active, weights[2 + j].load(info, groups[2 + j]))
        total = term if total is None else total + term
    accumulate(out, pl.program_id(0), total)


def feed(order, x, bias, weights):
    m = x.shape[0]
    block = pl.BlockSpec((1, 2, m, 256), lambda r, *_: (r, 0, 0, 0))
    return call(
        functools.partial(feed_body, weights), (4,),
        [whole(x.shape), pick(bias)] + joined(weights, "specs"),
        [block, block, whole((m, 1024))],
        [
            jax.ShapeDtypeStruct((4, 2, m, 256), FULL), jax.ShapeDtypeStruct((4, 2, m, 256), LOW),
            jax.ShapeDtypeStruct((m, 1024), FULL),
        ], [],
        [x, bias] + joined(weights, "arrays"), 4 * m * 1024 * 2048, (order,),
    )


def feed_back_body(weights, info, spread, x, hidden, active, *refs):
    groups, refs = take_refs(weights, refs)
    pairs, (grad_bias, out) = grad_refs(FEED, refs[:-2]), refs[-2:]
    total = None
    for j in range(2):
        value = hidden[0, j]
        slope = 0.5 * (1.0 + lax.erf(value * ROOT_HALF))
        slope += value * jnp.exp(-0.5 * value * value) * (1.0 / ROOT_TWOPI)
        grad = times(spread[...], weights[2 + j].load(info, groups[2 + j])) * slope
        grad_bias[0, j : j + 1] = jnp.sum(grad, axis=0, keepdims=True)
        low = grad.astype(LOW)
        FEED[2 + j].store(pairs[2 + j], t_times(spread[...], active[0, j]).astype(LOW))
        FEED[j].store(pairs[j], t_times(x[...], low).astype(LOW))
        term = times_t(low, weights[j].load(info, groups[j]))
        total = term if total is None else total + term
    accumulate(out, pl.program_id(0), total)


def feed_back(order, spread, x, hidden, active, weights):
    m = x.shape[0]
    specs, shapes = grad_outs(FEED)
    *grads, grad_bias, out = call(
        functools.partial(feed_back_body, weights), (4,),
        [whole(x.shape), whole(x.shape), pick(hidden), pick(active)] + joined(weights, "specs"),
        specs + [pl.BlockSpec((1, 2, 256), lambda r, *_: (r, 0, 0)), whole((m, 1024))],
        shapes
        + [jax.ShapeDtypeStruct((4, 2, 256), FULL), jax.ShapeDtypeStruct((m, 1024), FULL)], [],
        [spread, x, hidden, active] + joined(weights, "arrays"), 8 * m * 1024 * 2048, (order,),
    )
    return halves(grads), grad_bias, out


def one_row(value, s):
    lane = lax.broadcasted_iota(jnp.int32, value.shape, 1) // 64 == s
    return jnp.where(lane, value, jnp.zeros_like(value))


def scores_of(keys, query, mark_keys, mark_query, s):
    scores = times_t(keys, one_row(query, s) * LOW(0.125))
    same = mark_keys[:, s : s + 1] == mark_query[s : s + 1, :]
    return jnp.where(same, scores, MASKED)


def attend_body(query, keys, values, mark_keys, mark_query, out, summary):
    turned = values[...].astype(FULL).T.astype(LOW)
    results = []
    for s in range(2):
        scores = scores_of(keys[...], query[...], mark_keys, mark_query, s)
        top = jnp.max(scores, axis=0, keepdims=True)
        weights = jnp.exp(scores - top)
        total = jnp.sum(weights, axis=0, keepdims=True)
        probs = (weights * (1.0 / total)).astype(LOW)
        results.append(times(turned[s * 64 : (s + 1) * 64], probs))
        summary[s : s + 1] = top + jnp.log(total)
    out[...] = jnp.concatenate(results, 0).T.astype(LOW)


def attend(qkv, mark_keys, mark_query):
    n = qkv.shape[0]
    q = 384

    return call(
        attend_body, (n // q,),
        [
            pl.BlockSpec((q, 128), lambda i: (i, 0)), pl.BlockSpec((n, 128), lambda i: (0, 1)),
            pl.BlockSpec((n, 128), lambda i: (0, 2)), whole((n, 2)),
            pl.BlockSpec((2, q), lambda i: (0, i)),
        ],
        [pl.BlockSpec((q, 128), lambda i: (i, 0)), pl.BlockSpec((2, q), lambda i: (0, i))],
        [jax.ShapeDtypeStruct((n, 128), LOW), jax.ShapeDtypeStruct((2, n), FULL)], [],
        (qkv, qkv, qkv, mark_keys, mark_query), 8 * n * n * 128,
    )


def attend_back_body(
    query, keys, values, grad_mixed, mark_keys, mark_query, summary, out, sums, sum_k, sum_v, sum_q
):
    i = pl.program_id(0)
    n, q = keys.shape[0], query.shape[0]
    turned = keys[...].astype(FULL).T.astype(LOW)
    lane = lax.broadcasted_iota(jnp.int32, (n, 128), 1) < 64
    grads_q, grads_k, grads_v = [], [], []
    for s in range(2):
        scores = scores_of(keys[...], query[...], mark_keys, mark_query, s)
        probs = jnp.exp(scores - summary[s : s + 1])
        grad_probs = times_t(values[...], one_row(grad_mixed[...], s))
        inner = jnp.sum(probs * grad_probs, axis=0, keepdims=True)
        low_probs = probs.astype(LOW)
        grad_scores = (probs * (grad_probs - inner)).astype(LOW)
        grads_v.append(times(low_probs, grad_mixed[...]))
        grads_k.append(times(grad_scores, query[...]))
        grads_q.append(times(turned[s * 64 : (s + 1) * 64], grad_scores))
    accumulate(sum_k, i, jnp.where(lane, grads_k[0], grads_k[1]) * 0.125)
    accumulate(sum_v, i, jnp.where(lane, grads_v[0], grads_v[1]))
    grad_q = jnp.concatenate(grads_q, 0).T * 0.125
    accumulate(sum_q, i, jnp.sum(grad_q, axis=0, keepdims=True))
    out[pl.ds(pl.multiple_of(i * q, q), q), :128] = grad_q.astype(LOW)

    @pl.when(i == pl.num_programs(0) - 1)
    def _():
        out[:, 128:256] = sum_k[...].astype(LOW)
        out[:, 256:] = sum_v[...].astype(LOW)
        sums[0:1] = sum_q[...]
        sums[1:2] = jnp.sum(sum_v[...], axis=0, keepdims=True)


def attend_back(qkv, grad_mixed, mark_keys, mark_query, summary):
    n = qkv.shape[0]
    q = 384
    return call(
        attend_back_body, (n // q,),
        [
            pl.BlockSpec((q, 128), lambda i: (i, 0)), pl.BlockSpec((n, 128), lambda i: (0, 1)),
            pl.BlockSpec((n, 128), lambda i: (0, 2)), pl.BlockSpec((q, 128), lambda i: (i, 0)),
            whole((n, 2)), pl.BlockSpec((2, q), lambda i: (0, i)),
            pl.BlockSpec((2, q), lambda i: (0, i)),
        ],
        [whole((n, 384)), whole((2, 128))],
        [jax.ShapeDtypeStruct((n, 384), LOW), jax.ShapeDtypeStruct((2, 128), FULL)],
        [pltpu.VMEM((n, 128), FULL), pltpu.VMEM((n, 128), FULL), pltpu.VMEM((1, 128), FULL)],
        (qkv, qkv, qkv, grad_mixed, mark_keys, mark_query, summary), 20 * n * n * 128,
    )


def trade(value):
    return lax.all_to_all(
        value, ("ctx", "tensor"), 0, 0, axis_index_groups=GROUPS, tiled=True
    )


def local(
    stream, segments, w_qkv, qv_bias, w_out, norm_gains, shifts, w_in, in_bias, w_back, cotangent
):
    layers = w_qkv.shape[0]
    dp, ctx, me_x = lax.axis_index("dp"), lax.axis_index("ctx"), lax.axis_index("tensor")
    core, z_lo = ctx & 1, ctx >> 1
    me_y, me_z = dp & 3, (dp >> 2) * 2 + z_lo
    rows = stream.shape[1]
    width = stream.shape[2]

    def both_rows(columns):
        axis = columns.ndim - 2
        keep = lax.dynamic_index_in_dim(columns, core, axis, False)
        new = swap(lax.dynamic_index_in_dim(columns, 1 - core, axis, False))
        return jnp.where(
            core == 0, jnp.concatenate([keep, new], -2), jnp.concatenate([new, keep], -2)
        )

    lead = both_rows(
        jnp.concatenate(
            [
                jnp.concatenate(
                    [
                        w_qkv[layer].reshape(32, 3, 2, 128).transpose(0, 2, 1, 3).reshape(
                            32, 2, 384
                        ),
                        w_out[layer].T.reshape(32, 2, 128),
                    ],
                    2,
                )
                for layer in range(2)
            ],
            2,
        )
    ).reshape(1, 64, 2, 4, 128)
    lead = gather_early([lead[:, :, :, k].reshape(1, 64, 256) for k in range(4)])
    later = jnp.concatenate([w_in[0], w_back[0].T, w_in[1], w_back[1].T], 1)
    later = lax.all_gather(later, "tensor", axis=0, tiled=True)
    lead, norm_gains, later = lax.optimization_barrier((lead, norm_gains, later))
    lead_one = [value[:, :, 128:] for value in lead]
    lead = gather_late([value[:, :, :128] for value in lead])
    lead, lead_one = lax.optimization_barrier((lead, lead_one))
    near_one = [swap(value, *ORDERS[k][4]) for k, value in enumerate(lead_one)]
    far_one = [swap(value, *ORDERS[k][5]) for k, value in enumerate(lead_one)]

    def everywhere(value):
        value = lax.all_gather(value, ("dp", "ctx"), axis=0, tiled=True)
        return value.reshape(16, 2, 4, 32, value.shape[1])

    feed_zero = everywhere(later[:, :2048])
    feed_one = everywhere(later[:, 2048:])
    attention_w = [[Exchanged(k, lead[k], 128) for k in range(4)]]
    feed_w = [
        [Gathered(value, base, 256, 2) for base in (0, 1, 4, 5)] for value in (feed_zero, feed_one)
    ]

    vectors = jnp.concatenate(
        [norm_gains.reshape(-1), shifts.reshape(-1), qv_bias.reshape(-1), in_bias.reshape(-1)]
    )
    vectors = jnp.pad(vectors, (0, 512 - vectors.shape[0]))
    spread = lax.all_to_all(jnp.broadcast_to(vectors, (128, 512)), ALL, 0, 0, tiled=True)
    spread = spread.reshape(32, 4, 512)
    gains_abs = spread[:, 0, 0:128].reshape(32, 4, 32).transpose(1, 0, 2).reshape(4, width)
    shifts_abs = spread[:, 0, 128:384].reshape(32, 8, 32).transpose(1, 0, 2).reshape(8, width)
    pair = spread[:, :, 384:416].reshape(32, 4, layers, 2, 2, 2, 2).transpose(2, 3, 1, 4, 5, 0, 6)
    pair = lax.dynamic_index_in_dim(pair.reshape(layers, 2, 4, 2, 2, 64), core, 3, False)
    pair = take_relative(pair, me_x, 2).astype(FULL)
    up = spread[:, :, 416:480].reshape(32, 4, layers, 2, 2, 8).transpose(2, 1, 3, 4, 0, 5)
    up = lax.dynamic_index_in_dim(up.reshape(layers, 4, 2, 2, 256), core, 2, False)
    up = take_relative(up, me_x, 1).astype(FULL)

    place = lax.broadcasted_iota(jnp.int32, (width, width), 1)
    block = place >> 6
    far_z = me_z ^ (((block >> 2) & 1) ^ ((block >> 3) * 3))
    far_y = me_y ^ ((block & 1) ^ (((block >> 1) & 1) * 3))
    source = (((far_z >> 1) * 4 + far_y) * 2 + (far_z & 1)) * 64 + (place & 63)
    reorder = source == lax.broadcasted_iota(jnp.int32, (width, width), 0)
    reorder_low = reorder.astype(LOW)
    reorder_full = reorder.astype(FULL)

    def absolute(value):
        return lax.dot_general(
            value, reorder_full, (((1,), (1,)), ((), ())), precision=lax.Precision.HIGHEST,
            preferred_element_type=FULL,
        )

    tokens = 2 * rows
    inputs = times(
        jnp.concatenate(
            [
                stream.reshape(tokens, width), cotangent.reshape(tokens, width),
                gains_abs, shifts_abs,
            ]
        ),
        reorder_low,
    )
    state = inputs[:tokens]
    incoming = inputs[tokens : 2 * tokens]
    gains = inputs[2 * tokens : 2 * tokens + 4].reshape(layers, 2, width)
    shift = inputs[2 * tokens + 4 :].reshape(layers, 4, width)

    marks = segments.reshape(2, 2, 2, 4, rows)
    marks = jnp.where(core == 0, marks, marks[:, :, ::-1])
    marks = marks.transpose(0, 1, 3, 2, 4).reshape(2, 16 * rows)
    marks_t = marks.T
    chips = []
    for i in range(16):
        far_z = me_z ^ (((i >> 2) & 1) ^ ((i >> 3) * 3))
        far_y = me_y ^ ((i & 1) ^ (((i >> 1) & 1) * 3))
        chips.append(((far_z >> 1) * 4 + far_y) * 2 + (far_z & 1))
    order = [relative_x(me_x, r) for r in range(4)] + [core] + chips
    order = jnp.stack(order).astype(jnp.int32)

    saved = []
    for layer in range(layers):
        bias = pair[layer].reshape(2, 4, 1, 128)
        gathered = both(state.astype(LOW))
        qkv = project(order, gathered, attention_w[layer], bias[0], bias[1])
        qkv = trade(qkv.reshape(8, 2 * rows, 384)).reshape(16 * rows, 384)
        if layer == 0:
            qkv, near_one, far_one = lax.optimization_barrier((qkv, near_one, far_one))
            last_one = [swap(value, *ORDERS[k][5]) for k, value in enumerate(near_one)]
        mixed, summary = attend(qkv, marks_t, marks)
        mixed = trade(mixed.reshape(8, 2 * rows, 128)).reshape(2, 4, 2 * rows, 128)
        if layer == 0:
            mixed, last_one = lax.optimization_barrier((mixed, last_one))
            pieces = zip(lead_one, near_one, far_one, last_one)
            attention_w.append([Exchanged(k, four, 128) for k, four in enumerate(pieces)])
        mixed, attended = mix(order, mixed, attention_w[layer][3])
        attended = own_sum(attended) + shift[layer, 2]
        first, unit_one, inv_one = normalize(state + attended, gains[layer, 0], shift[layer, 0])
        gathered_two = both(first.astype(LOW))
        hidden, active, down = feed(order, gathered_two, up[layer], feed_w[layer])
        down = own_sum(down)
        state, unit_two, inv_two = normalize(
            first + down + shift[layer, 3], gains[layer, 1], shift[layer, 1]
        )
        saved.append(
            (gathered, qkv, summary, mixed, unit_one, inv_one, gathered_two, hidden, active,
             unit_two, inv_two)
        )
    result = absolute(state)

    small = [None] * layers
    for layer in reversed(range(layers)):
        (gathered, qkv, summary, mixed, unit_one, inv_one, gathered_two, hidden, active,
         unit_two, inv_two) = saved[layer]
        grad_two, gain_two, shift_two = normalize_back(
            incoming, unit_two, inv_two, gains[layer, 1]
        )
        spread_two = both(grad_two.astype(LOW))
        grad_feed, grad_upbias, grad_first = feed_back(
            order, spread_two, gathered_two, hidden, active, feed_w[layer]
        )
        grad_feed = reduce_first(grad_feed, range(4))
        grad_first = grad_two + own_sum(grad_first)
        grad_one, gain_one, shift_one = normalize_back(
            grad_first, unit_one, inv_one, gains[layer, 0]
        )
        spread_one = both(grad_one.astype(LOW))
        if layer == 0:
            spread_one, later = lax.optimization_barrier((spread_one, later))
        grad_mixed = trade(mix_back(order, spread_one, attention_w[layer][3]).reshape(8, 2 * rows, 128))
        grad_mixed = grad_mixed.reshape(16 * rows, 128)
        if layer == 0:
            grad_mixed, grad_feed = lax.optimization_barrier((grad_mixed, grad_feed))
            tail = [jnp.concatenate([a, b], 2) for a, b in zip(grad_feed, later)]
            tail = reduce_phase(reduce_phase(tail, range(4), 2), range(4), 3)
        low_packed, grad_pair = attend_back(qkv, grad_mixed, marks_t, marks, summary)
        grad_pair = grad_pair.reshape(2, 2, 64).sum(1)
        low_packed = trade(low_packed.reshape(8, 2 * rows, 384)).reshape(2, 4, 2 * rows, 384)
        if layer:
            low_packed, grad_feed = lax.optimization_barrier((low_packed, grad_feed))
        else:
            low_packed, tail = lax.optimization_barrier((low_packed, tail))
        grad_attention, grad_x = project_back(
            order, low_packed, gathered, spread_one, mixed, attention_w[layer],
            APART,
        )
        incoming = grad_one + own_sum(grad_x)
        if layer:
            grad_attention = reduce_first(grad_attention, range(4))
            later = [jnp.concatenate(pair, 2) for pair in zip(grad_feed, grad_attention)]
        else:
            lead = reduce_first(grad_attention, range(4))
            lead, small_zero = lax.optimization_barrier((lead, (gain_one, gain_two)))
            gain_one, gain_two = small_zero
            lead = reduce_phase(reduce_phase(lead, range(4), 2), range(4), 3)
            tail = [jnp.concatenate(pair, 2) for pair in zip(tail, lead)]
            tail = reduce_phases(tail, range(4), 4)
        small[layer] = (
            jnp.stack([gain_one, gain_two]),
            jnp.stack(
                [shift_one, shift_two, jnp.sum(grad_one, axis=0), jnp.sum(grad_two, axis=0)]
            ),
            grad_pair,
            grad_upbias,
        )
    grad_stream = absolute(incoming)

    def own_rows(parts):
        total = jnp.stack(parts, 1)
        total = total.reshape((2, 32) + total.shape[1:])
        keep = lax.dynamic_index_in_dim(total, core, 0, False)
        new = swap(lax.dynamic_index_in_dim(total, 1 - core, 0, False))
        return jnp.stack(
            [jnp.where(core == 0, keep, new), jnp.where(core == 0, new, keep)], 1
        ).astype(FULL)

    tail = own_rows(tail)
    attention = [tail[..., 640:], tail[..., 512:640]]
    feeds = [tail[..., :256], tail[..., 256:512]]
    out_qkv = jnp.stack(
        [value[:, :, :3].transpose(0, 2, 1, 3).reshape(32, 3, 256) for value in attention]
    )
    out_o = jnp.stack([value[:, :, 3].reshape(32, 256).T for value in attention])
    out_up = jnp.stack([value[:, :, :2].reshape(32, 1024) for value in feeds])
    out_down = jnp.stack([value[:, :, 2:].reshape(32, 1024).T for value in feeds])

    vec = absolute(
        jnp.concatenate([small[layer][0] for layer in range(layers)]
                        + [small[layer][1] for layer in range(layers)])
    )
    vec = vec.reshape(12, 32, 32).transpose(1, 0, 2).reshape(32, 1, 384)
    vec = jnp.broadcast_to(vec, (32, 4, 384))
    pair = jnp.stack([small[layer][2] for layer in range(layers)])
    head = me_x * 4 + core * 2 + z_lo
    pair = jnp.where((jnp.arange(16) == head)[:, None], pair[:, :, None], 0.0)
    pair = pair.reshape(layers, 2, 4, 4, 32, 2).transpose(4, 2, 0, 1, 3, 5).reshape(32, 4, 32)
    up = take_absolute(jnp.stack([small[layer][3] for layer in range(layers)]), me_x, 1)
    up = jnp.where((jnp.arange(2) == core)[:, None, None], up[:, :, None], 0.0)
    up = up.reshape(layers, 4, 4, 32, 8).transpose(3, 1, 0, 2, 4).reshape(32, 4, 64)
    vec = jnp.concatenate([vec, pair, up, jnp.zeros((32, 4, 32), FULL)], 2).reshape(128, 512)
    vec = jnp.sum(lax.all_to_all(vec, ALL, 0, 0, tiled=True), axis=0)

    return (
        result.reshape(stream.shape),
        grad_stream.reshape(stream.shape),
        out_qkv,
        vec[384:416].reshape(qv_bias.shape),
        out_o,
        vec[:128].reshape(norm_gains.shape),
        vec[128:384].reshape(shifts.shape),
        out_up,
        vec[416:480].reshape(in_bias.shape),
        out_down,
    )


def solution(mesh):
    return jax.shard_map(
        local,
        mesh=mesh,
        in_specs=(
            P("dp", ("ctx", "tensor"), None),
            P("dp", None),
            P(None, ("dp", "ctx"), None, "tensor"),
            P(None, None, "tensor", ("dp", "ctx")),
            P(None, "tensor", ("dp", "ctx")),
            P(None, None, ("dp", "ctx")),
            P(None, None, ("dp", "ctx")),
            P(None, ("dp", "ctx"), "tensor"),
            P(None, "tensor", ("dp", "ctx")),
            P(None, "tensor", ("dp", "ctx")),
            P("dp", ("ctx", "tensor"), None),
        ),
        out_specs=(
            P("dp", ("ctx", "tensor"), None),
            P("dp", ("ctx", "tensor"), None),
            P(None, ("dp", "ctx"), None, "tensor"),
            P(None, None, "tensor", ("dp", "ctx")),
            P(None, "tensor", ("dp", "ctx")),
            P(None, None, ("dp", "ctx")),
            P(None, None, ("dp", "ctx")),
            P(None, ("dp", "ctx"), "tensor"),
            P(None, "tensor", ("dp", "ctx")),
            P(None, "tensor", ("dp", "ctx")),
        ),
        check_vma=False,
    )
```
